32 devices in a mesh: lon: 4 (over y, core), lat: 8 (over z, x).
Axes of the slice: x: 2, y: 2, z: 4, core: 2. Of those that a mesh axis runs over, the one named last changes fastest.
Arguments:
- state_pert: bfloat16 [32, 16, 6, 128, 256], P('lon', 'lat'), may hold values from -6 to 6
- state_mean: float32 [32, 16, 6, 256], P('lon', 'lat'), may hold values from -6 to 6
- obs_anom: bfloat16 [6144, 128, 128], P(('lon', 'lat')), may hold values from -6 to 6
- innov: float32 [6144, 128], P(('lon', 'lat')), may hold values from -12 to 12
- obs_rinv: float32 [6144, 128], P(('lon', 'lat')), may hold values from 0.25 to 4
- obs_lon: int32 [6144, 128], P(('lon', 'lat')), may hold values from 0 to 511, as said below
- obs_lat: int32 [6144, 128], P(('lon', 'lat')), may hold values from 40 to 215, as said below
- block_list: int32 [32, 16, 48], P('lon', 'lat'), may hold values from 0 to 6143, as said below
- block_count: int32 [32, 16], P('lon', 'lat'), may hold values from 24 to 48
Outputs:
- analysis: float32 [32, 16, 6, 128, 256], P('lon', 'lat')
The draws below stay inside these ranges and needn't reach their ends.
Inputs may be any that keep to these rules, and one draw needn't show every extreme that they name: `block_list`: block b is held by the device of flat index b // 192 over lon+lat. The first 48 entries of a patch's list name distinct blocks. Over all list entries of the patches of one device, each holder holds exactly 24 of the named blocks (counting repeats over patches). Only the first block_count entries of a patch's list are used. `obs_lon`: the longitude indices of one block's observations lie within 32 consecutive columns, counted around the periodic grid. `obs_lat`: the latitude indices of one block's observations lie within 32 consecutive columns.
All inputs are finite; a program needn't handle non-finite values.
Results may differ from the reference program's by a relative error of at most 0.0023.
Values may be sent and summed in bfloat16 or wider, within the bound.
No kernel may reach another device: no remote copies, remote signals or barrier semaphores. Data moves between devices by JAX's collectives and lax.ppermute only.
A program may use at most 192 MiB of HBM per device.

```python
import math
import jax
import jax.numpy as jnp
from jax import lax

K = 128
PSIDE = 16
PLON = 8
PLAT = 2
LMAX = 48
OB = 128
SHARE = 4
NS_ITERS = 5
OBLK = 192
NPLON = 32
NPLAT = 16
NBLK = 6144
FIELDS = 6
COLS = 256
CAP = 24


def draw_innov(key, part):
    ramp = 1.0 + 2.0 * jnp.arange(NBLK, dtype=jnp.float32)[:, None] / (NBLK - 1)
    return jax.random.truncated_normal(key, -4.0, 4.0, (NBLK, OB), jnp.float32) * ramp


def block_layout(key):
    lon_devices = NPLON // PLON
    lat_devices = NPLAT // PLAT
    groups_lat = lat_devices // SHARE
    group_total = lon_devices * groups_lat
    slot_total = PLON * PLAT * LMAX
    scores = jax.random.randint(jax.random.fold_in(key, 7), (group_total, slot_total), 0, 1 << 20) * slot_total + jnp.arange(slot_total)[None, :]
    placed = jnp.argsort(scores, axis=1).astype(jnp.int32)
    holder = placed // CAP
    within = placed % CAP
    group_ids = jnp.arange(group_total, dtype=jnp.int32)[:, None]
    blocks = holder * OBLK + group_ids * CAP + within
    slot_ids = jnp.arange(slot_total, dtype=jnp.int32)[None, :]
    patch = slot_ids // LMAX
    patch_lon = patch // PLAT
    patch_lat = patch % PLAT
    group_lon = group_ids // groups_lat
    group_lat = group_ids % groups_lat
    centre_lon = (group_lon * PLON + patch_lon) * PSIDE + PSIDE // 2 + 0 * blocks
    centre_lat = group_lat * SHARE * PLAT * PSIDE + (SHARE - 1) * PLAT * PSIDE // 2 + patch_lat * PSIDE + PSIDE // 2 + 0 * blocks
    flat_blocks = blocks.reshape(-1)
    lon_of_block = jnp.zeros((NBLK,), jnp.int32).at[flat_blocks].set(centre_lon.reshape(-1))
    lat_of_block = jnp.zeros((NBLK,), jnp.int32).at[flat_blocks].set(centre_lat.reshape(-1))
    device_lon = jnp.arange(lon_devices, dtype=jnp.int32)[:, None]
    device_lat = jnp.arange(lat_devices, dtype=jnp.int32)[None, :]
    device_group = device_lon * groups_lat + device_lat // SHARE
    lists = blocks[device_group]
    lists = lists.reshape(lon_devices, lat_devices, PLON, PLAT, LMAX).transpose(0, 2, 1, 3, 4)
    return (lists.reshape(NPLON, NPLAT, LMAX).astype(jnp.int32), lon_of_block, lat_of_block)


def draw_block_list(key, part):
    lists, lon_of_block, lat_of_block = block_layout(key)
    return lists


def draw_obs_lon(key, part):
    lists, lon_of_block, lat_of_block = block_layout(key)
    offsets = jax.random.randint(jax.random.fold_in(key, 11), (NBLK, OB), 0, 32) - 16
    return ((lon_of_block[:, None] + offsets) % (NPLON * PSIDE)).astype(jnp.int32)


def draw_obs_lat(key, part):
    lists, lon_of_block, lat_of_block = block_layout(key)
    offsets = jax.random.randint(jax.random.fold_in(key, 13), (NBLK, OB), 0, 32) - 16
    column = jnp.arange(OB, dtype=jnp.int32)[None, :]
    offsets = jnp.where(column == 0, 15, jnp.where(column == 1, -16, offsets))
    return jnp.clip(lat_of_block[:, None] + offsets, 0, NPLAT * PSIDE - 1).astype(jnp.int32)


def touch_ends(entries, rng, smallest, high):
    longest = entries.shape.index(max(entries.shape))
    spots = []
    for shift in (0, 1):
        where = [jax.random.randint(jax.random.fold_in(rng, axis), (), 0, length) for axis, length in enumerate(entries.shape)]
        where[longest] = (where[longest] + shift) % entries.shape[longest]
        spots.append(tuple(where))
    return entries.at[spots[0]].set(smallest).at[spots[1]].set(high)


def block_scale(rng, extent, split, smallest, largest):
    def one(position, parts):
        steps = jax.random.uniform(jax.random.fold_in(jax.random.fold_in(rng, 6), position), (parts,), jnp.float32, smallest / len(split), largest / len(split))
        return jnp.repeat(jnp.exp(steps), extent[position] // parts).reshape((-1,) + (1,) * (len(extent) - position - 1))

    gain = one(*split[0])
    for cut in split[1:]:
        gain = gain * one(*cut)
    return gain


def centred(key, dims, scale, bound, pieces=(), held_as=jnp.bfloat16):
    loudness = block_scale(key, dims, pieces, -0.22, 0.18) if pieces else 1.0
    entries = jax.random.normal(key, dims, jnp.float32) * scale * loudness
    return jnp.minimum(jnp.maximum(entries, -bound), bound).astype(held_as)


def setup_inputs(seed: int = 0) -> dict:
    arg_keys = jax.random.split(jax.random.key(seed), 10)
    state_pert = centred(arg_keys[0], (NPLON, NPLAT, FIELDS, K, COLS), 1.0, 6.0, ((0, 4), (1, 8)))
    state_mean = centred(arg_keys[1], (NPLON, NPLAT, FIELDS, COLS), 1.0, 6.0, ((0, 4), (1, 8)), jnp.float32)
    obs_anom = centred(arg_keys[2], (NBLK, K, OB), 1.0, 6.0, ((0, 32),))
    innov = draw_innov(jax.random.fold_in(arg_keys[9], 71), 0)
    obs_rinv = jnp.clip(jnp.exp(math.log(4.0) - 2.7725887 * jax.random.uniform(arg_keys[4], (NBLK, OB), jnp.float32) ** block_scale(arg_keys[4], (NBLK, OB), ((0, 32),), -0.2, 0.2)), 0.25, 4.0)
    obs_lon = draw_obs_lon(jax.random.fold_in(arg_keys[9], 71), 0)
    obs_lat = draw_obs_lat(jax.random.fold_in(arg_keys[9], 71), 0)
    block_list = draw_block_list(jax.random.fold_in(arg_keys[9], 71), 0)
    block_count = touch_ends(jax.random.randint(arg_keys[8], (NPLON, NPLAT), CAP, LMAX + 1), jax.random.fold_in(arg_keys[8], 1), CAP, LMAX).astype(jnp.int32)
    return {"state_pert": state_pert, "state_mean": state_mean, "obs_anom": obs_anom, "innov": innov, "obs_rinv": obs_rinv, "obs_lon": obs_lon, "obs_lat": obs_lat, "block_list": block_list, "block_count": block_count}


loc_scale = 48.0

def product(left, right):
    return jnp.dot(left, right, precision=lax.Precision.HIGHEST)

def analyse(deviations, centre_state, anomalies, obs_fields, used_count, centre_lon, centre_lat, inflation, grid_lon):
    members = anomalies.shape[1]
    in_list = (jnp.arange(anomalies.shape[0]) < used_count).astype(jnp.float32)
    lon_gap = jnp.abs(obs_fields[:, 2] - centre_lon)
    lon_gap = jnp.minimum(lon_gap, grid_lon - lon_gap)
    lat_gap = obs_fields[:, 3] - centre_lat
    weight = obs_fields[:, 1] * jnp.exp(-(lon_gap * lon_gap + lat_gap * lat_gap) / (2.0 * loc_scale * loc_scale)) * in_list[:, None]
    scaled = (anomalies.astype(jnp.float32) * weight[:, None, :]).astype(jnp.bfloat16)
    gram_matrix = jnp.einsum('lko,lmo->km', scaled.astype(jnp.float32), anomalies.astype(jnp.float32))
    projected = jnp.einsum('lko,lo->k', scaled.astype(jnp.float32), obs_fields[:, 0], precision=lax.Precision.HIGHEST)
    identity = jnp.eye(members, dtype=jnp.float32)
    system = (members - 1) / inflation * identity + gram_matrix
    scaling = jnp.sqrt(jnp.sum(system * system))
    root = system / scaling
    inverse_root = identity
    for _ in range(NS_ITERS):
        factor = 1.5 * identity - 0.5 * product(inverse_root, root)
        root = product(root, factor)
        inverse_root = product(factor, inverse_root)
    inverse_sqrt = inverse_root / jnp.sqrt(scaling)
    mean_weights = product(inverse_sqrt, product(inverse_sqrt, projected[:, None]))
    weights = (jnp.sqrt(jnp.float32(members - 1)) * inverse_sqrt + mean_weights).astype(jnp.bfloat16)
    change = jnp.einsum('fjc,jk->fkc', deviations.astype(jnp.float32), weights.astype(jnp.float32))
    return centre_state[:, None, :] + change

def reference(state_pert, state_mean, obs_anom, innov, obs_rinv, obs_lon, obs_lat, block_list, block_count):
    members = obs_anom.shape[1]
    spread = lax.optimization_barrier(jnp.sum(jnp.square(obs_anom.astype(jnp.float32)), axis=1)) / (members - 1)
    inflation = jnp.sum(obs_rinv * innov * innov) / (jnp.sum(obs_rinv * spread) + NBLK * OB)
    obs_fields = jnp.stack([innov, obs_rinv, obs_lon.astype(jnp.float32), obs_lat.astype(jnp.float32)], axis=1)
    patch_total = NPLON * NPLAT
    patch_index = jnp.arange(patch_total)
    centre_lon = (patch_index // NPLAT * PSIDE).astype(jnp.float32) + (PSIDE - 1) / 2.0
    centre_lat = (patch_index % NPLAT * PSIDE).astype(jnp.float32) + (PSIDE - 1) / 2.0
    grid_lon = jnp.float32(NPLON * PSIDE)

    def patch_update(inputs):
        deviations, centre_state, block_ids, used_count, lon_centre, lat_centre = inputs
        return analyse(deviations, centre_state, obs_anom[block_ids], obs_fields[block_ids], used_count, lon_centre, lat_centre, inflation, grid_lon)
    inputs = (state_pert.reshape(patch_total, FIELDS, K, COLS), state_mean.reshape(patch_total, FIELDS, COLS), block_list.reshape(patch_total, LMAX).astype(jnp.int32), block_count.reshape(patch_total), centre_lon, centre_lat)
    updated = lax.map(patch_update, inputs)
    return updated.reshape(NPLON, NPLAT, FIELDS, K, COLS)
```

```python
import functools

import jax
import jax.numpy as jnp
from jax import lax
from jax.experimental import pallas as pl
from jax.experimental.pallas import tpu as pltpu
from jax.sharding import PartitionSpec as P

PSIDE = 16
NS_ITERS = 5
LOC_SCALE = 48.0
GROUP = 4
EXT = 16
F32 = jnp.float32
BF16 = jnp.bfloat16
NT = (((1,), (1,)), ((), ()))


def halves(value):
    high = value.astype(BF16)
    return high, (value - high.astype(F32)).astype(BF16)


def request_table(block_list, block_count, holders, held_blocks):
    patches, length = block_list.shape
    slots = patches * length
    per_owner = slots // holders
    wanted = block_list.reshape(slots)
    used = (lax.broadcasted_iota(jnp.int32, (patches, length), 1) < block_count[:, None]).reshape(
        slots
    )
    holder = jnp.where(used, wanted // held_blocks, holders)
    order = jnp.arange(slots)
    before = (holder[:, None] == holder[None, :]) & (order[None, :] < order[:, None])
    rank = jnp.sum(before.astype(jnp.int32), axis=1)
    code = (order // length) * held_blocks + wanted % held_blocks
    place = holder * per_owner + rank
    hit = (place[None, :] == jnp.arange(holders * per_owner)[:, None]) & used[None, :]
    table = jnp.sum(jnp.where(hit, code[None, :], 0), axis=1).reshape(holders, per_owner)
    number = jnp.sum((holder[None, :] == jnp.arange(holders)[:, None]).astype(jnp.int32), axis=1)
    return jnp.concatenate([table, number[:, None]], axis=1)


def gram_kernel(
    sizes,
    targets_ref,
    requests_ref,
    anom_ref,
    ext_ref,
    lon_ref,
    lat_ref,
    rinv_ref,
    totals_ref,
    send_ref,
    keep_ref,
    acc_ref,
):
    patches, lat_patches, lon_patches, lat_devices, held, per_owner, grid_lon, sent = sizes
    step = pl.program_id(0)
    target = targets_ref[step]
    lon_first = (target // lat_devices) * lon_patches
    lat_first = (target % lat_devices) * lat_patches
    members = anom_ref.shape[1]
    acc_ref[...] = jnp.zeros_like(acc_ref)
    number = requests_ref[target, per_owner]

    def group(start, _):
        products = []
        for i in range(GROUP):
            entry = start * GROUP + i
            code = requests_ref[target, jnp.minimum(entry, per_owner - 1)]
            patch = code // held
            block = code % held
            centre_lon = (lon_first + patch // lat_patches) * (2 * PSIDE) + (PSIDE - 1)
            centre_lat = (lat_first + patch % lat_patches) * (2 * PSIDE) + (PSIDE - 1)
            lon_gap = jnp.abs(2 * lon_ref[pl.ds(block, 1), :] - centre_lon)
            lon_gap = jnp.minimum(lon_gap, 2 * grid_lon - lon_gap)
            lat_gap = 2 * lat_ref[pl.ds(block, 1), :] - centre_lat
            square = (lon_gap * lon_gap + lat_gap * lat_gap).astype(F32)
            rinv = jnp.where(entry < number, rinv_ref[pl.ds(block, 1), :], 0.0)
            weight = rinv * jnp.exp(square * (-1.0 / (8.0 * LOC_SCALE * LOC_SCALE)))
            anom = anom_ref[block]
            scaled = (anom.astype(F32) * weight).astype(BF16)
            left = jnp.concatenate([anom, ext_ref[block]], axis=0)
            product = lax.dot_general(left, scaled, NT, preferred_element_type=F32)
            products.append((patch, product[: members + 8]))
        for patch, product in products:
            acc_ref[patch] += product
        return 0

    lax.fori_loop(0, (number + GROUP - 1) // GROUP, group, 0)

    row = lax.broadcasted_iota(jnp.int32, (members, members), 0)
    column = lax.broadcasted_iota(jnp.int32, (members, members), 1)
    line = lax.broadcasted_iota(jnp.int32, (8, members), 0)

    def emit(out_ref):
        for pair in range(patches // 2):
            first = acc_ref[2 * pair]
            second = acc_ref[2 * pair + 1]
            packed = jnp.where(row < column, first[:members], second[:members])
            out_ref[0, pair, :members, :] = packed.astype(BF16)
            rows = totals_ref[...]
            for place, values in ((0, first), (2, second)):
                diagonal = jnp.sum(
                    jnp.where(row == column, values[:members], 0.0), axis=0, keepdims=True
                )
                projected = values[members : members + 1] + values[members + 1 : members + 2]
                rows = jnp.where(line == place, diagonal, rows)
                rows = jnp.where(line == place + 1, projected, rows)
            high = rows.astype(BF16).astype(F32)
            out_ref[0, pair, members:, :] = jnp.concatenate([high, rows - high], axis=0).astype(
                BF16
            )

    @pl.when(step < sent)
    def _():
        emit(send_ref)

    @pl.when(step >= sent)
    def _():
        emit(keep_ref)


def partial_grams(sizes, targets, requests, anom, ext, lon, lat, rinv, totals):
    patches, per_owner = sizes[0], sizes[5]
    sent = targets.shape[0] // 2
    members = anom.shape[1]
    rows = members + EXT
    block = (1, patches // 2, rows, members)
    whole = pl.BlockSpec(memory_space=pltpu.VMEM)
    half = jax.ShapeDtypeStruct((sent, patches // 2, rows, members), BF16)
    entries = 2 * sent * per_owner
    return pl.pallas_call(
        functools.partial(gram_kernel, (*sizes, sent)),
        out_shape=[half, half],
        grid_spec=pltpu.PrefetchScalarGridSpec(
            num_scalar_prefetch=2,
            grid=(2 * sent,),
            in_specs=[whole] * 6,
            out_specs=[
                pl.BlockSpec(block, lambda i, *_: (jnp.minimum(i, sent - 1), 0, 0, 0)),
                pl.BlockSpec(block, lambda i, *_: (jnp.maximum(i - sent, 0), 0, 0, 0)),
            ],
            scratch_shapes=[pltpu.VMEM((patches, members + 8, members), F32)],
        ),
        compiler_params=pltpu.CompilerParams(vmem_limit_bytes=32 * 2**20),
        cost_estimate=pl.CostEstimate(
            flops=entries * 8 * members**3, bytes_accessed=anom.size * 2, transcendentals=0
        ),
        name="partial_grams",
    )(targets, requests, anom, ext, lon, lat, rinv, totals)


def added(left, right):
    members = left.shape[-1]
    total = left.astype(F32) + right.astype(F32)
    rows = total[:, members : members + 8] + total[:, members + 8 :]
    high = rows.astype(BF16).astype(F32)
    rows = jnp.concatenate([high, rows - high], axis=1)
    return total[:, :members].astype(BF16), rows.astype(BF16)


def add_kernel(count, *refs):
    keep, got, outs = refs[:count], refs[count : 2 * count], refs[2 * count :]
    for i in range(count):
        members = keep[i].shape[-1]
        body, rows = added(keep[i][0], got[i][0])
        outs[i][0, :, :members, :] = body
        outs[i][0, :, members:, :] = rows


def add_all(keep, got):
    count = len(keep)
    shape = keep[0].shape
    spec = pl.BlockSpec((1, *shape[1:]), lambda i: (i, 0, 0, 0))
    size = keep[0].size * count
    return pl.pallas_call(
        functools.partial(add_kernel, count),
        out_shape=[jax.ShapeDtypeStruct(shape, BF16)] * count,
        grid=(shape[0],),
        in_specs=[spec] * (2 * count),
        out_specs=[spec] * count,
        compiler_params=pltpu.CompilerParams(vmem_limit_bytes=16 * 2**20),
        cost_estimate=pl.CostEstimate(flops=size * 4, bytes_accessed=size * 6, transcendentals=0),
        name="add_partials",
    )(*keep, *got)


def product(left, right):
    left_high, left_low = left
    right_high, right_low = right
    return jnp.dot(
        jnp.concatenate([left_high, left_low, left_high], axis=1),
        jnp.concatenate([right_high, right_high, right_low], axis=0),
        preferred_element_type=F32,
    )


def solve_kernel(count, total_obs, *refs):
    parts, (out_ref,) = refs[:count], refs[count:]
    pairs, rows, members = parts[0].shape
    row = lax.broadcasted_iota(jnp.int32, (members, members), 0)
    column = lax.broadcasted_iota(jnp.int32, (members, members), 1)
    identity = (row == column).astype(F32)

    def gathered(pair):
        total = parts[0][pair].astype(F32)
        for part in parts[1:]:
            total = total + part[pair].astype(F32)
        return total[:members], total[members : members + 8] + total[members + 8 :]

    def some(step, _):
        systems, projected = [], []
        for pair in (2 * step, 2 * step + 1):
            packed, values = gathered(pair)
            flipped = packed.T
            innovation = jnp.sum(values[4:5], axis=1, keepdims=True)
            spread = jnp.sum(values[5:6], axis=1, keepdims=True)
            ridge = (members - 1) * (spread + total_obs) / innovation
            for place, full in (
                (0, jnp.where(row < column, packed, flipped)),
                (2, jnp.where(row > column, packed, flipped)),
            ):
                full = jnp.where(row == column, values[place : place + 1], full)
                systems.append(full + ridge * identity)
                projected.append(values[place + 1 : place + 2])
        scalings, roots, inverses = [], [], []
        for system in systems:
            squares = jnp.sum(system * system, axis=0, keepdims=True)
            scaling = jnp.sqrt(jnp.sum(squares, axis=1, keepdims=True))
            scalings.append(scaling)
            roots.append(system / scaling)
        factors = [1.5 * identity - 0.5 * root for root in roots]
        roots = [product(halves(f), halves(r)) for f, r in zip(factors, roots)]
        inverses = factors
        for iteration in range(1, NS_ITERS):
            split_roots = [halves(r) for r in roots]
            split_inverses = [halves(z) for z in inverses]
            factors = [
                halves(1.5 * identity - 0.5 * product(z, r))
                for z, r in zip(split_inverses, split_roots)
            ]
            if iteration < NS_ITERS - 1:
                both = [
                    product(f, [jnp.concatenate([a, b], axis=1) for a, b in zip(r, z)])
                    for f, r, z in zip(factors, split_roots, split_inverses)
                ]
                roots = [b[:, :members] for b in both]
                inverses = [b[:, members:] for b in both]
            else:
                inverses = [product(f, z) for f, z in zip(factors, split_inverses)]
        for i in range(4):
            inverse_sqrt = inverses[i] * lax.rsqrt(scalings[i])
            inner = jnp.sum(inverse_sqrt * projected[i], axis=1, keepdims=True)
            mean = jnp.sum(inverse_sqrt * inner, axis=0, keepdims=True)
            out_ref[4 * step + i] = (
                jnp.sqrt(F32(members - 1)) * inverse_sqrt + mean
            ).astype(BF16)
        return 0

    lax.fori_loop(0, pairs // 2, some, 0)


def solve(parts, total_obs):
    pairs, rows, members = parts[0].shape
    whole = pl.BlockSpec(memory_space=pltpu.VMEM)
    return pl.pallas_call(
        functools.partial(solve_kernel, len(parts), total_obs),
        out_shape=jax.ShapeDtypeStruct((2 * pairs, members, members), BF16),
        in_specs=[whole] * len(parts),
        out_specs=whole,
        compiler_params=pltpu.CompilerParams(vmem_limit_bytes=32 * 2**20),
        name="solve",
    )(*parts)


def analysis_kernel(weights_ref, pert_ref, mean_ref, out_ref):
    for field in range(pert_ref.shape[1]):
        change = jnp.dot(weights_ref[0], pert_ref[0, field], preferred_element_type=F32)
        out_ref[0, field] = change + mean_ref[0, field : field + 1]


def analysis(weights, pert, mean):
    patches, fields, members, columns = pert.shape
    return pl.pallas_call(
        analysis_kernel,
        out_shape=jax.ShapeDtypeStruct(pert.shape, F32),
        grid=(patches,),
        in_specs=[
            pl.BlockSpec((1, members, members), lambda i: (i, 0, 0)),
            pl.BlockSpec((1, fields, members, columns), lambda i: (i, 0, 0, 0)),
            pl.BlockSpec((1, fields, columns), lambda i: (i, 0, 0)),
        ],
        out_specs=pl.BlockSpec((1, fields, members, columns), lambda i: (i, 0, 0, 0)),
        compiler_params=pltpu.CompilerParams(vmem_limit_bytes=16 * 2**20),
        name="analysis",
    )(weights, pert, mean)


def swap(value, axis, flip):
    size = lax.axis_size(axis)
    return lax.ppermute(value, axis, [(i, i ^ flip) for i in range(size)])


def on_device(
    state_pert, state_mean, obs_anom, innov, obs_rinv, obs_lon, obs_lat, block_list, block_count
):
    lon_devices, lat_devices = lax.axis_size("lon"), lax.axis_size("lat")
    holders = lon_devices * lat_devices
    lon_patches, lat_patches, fields, members, columns = state_pert.shape
    patches = lon_patches * lat_patches
    length = block_list.shape[2]
    held, _, block_obs = obs_anom.shape
    per_owner = patches * length // holders
    table = request_table(
        block_list.reshape(patches, length), block_count.reshape(patches), holders, held
    )
    requests = lax.all_to_all(table, ("lon", "lat"), split_axis=0, concat_axis=0, tiled=True)

    squares = jnp.sum(jnp.square(obs_anom.astype(F32)), axis=1) / (members - 1)
    zero = jnp.zeros((block_obs,), F32)
    totals = jnp.stack(
        [zero] * 4
        + [jnp.sum(obs_rinv * innov * innov, axis=0), jnp.sum(obs_rinv * squares, axis=0)]
        + [zero] * 2
    )
    innov_high = innov.astype(BF16).astype(F32)
    line = lax.broadcasted_iota(jnp.int32, (held, EXT, block_obs), 1)
    ext = jnp.where(
        line == 0,
        innov_high[:, None, :],
        jnp.where(line == 1, (innov - innov_high)[:, None, :], 0.0),
    ).astype(BF16)

    me_lon, me_lat = lax.axis_index("lon"), lax.axis_index("lat")
    sizes = (
        patches,
        lat_patches,
        lon_patches,
        lat_devices,
        held,
        per_owner,
        lon_devices * lon_patches * PSIDE,
    )

    def chunk(far):
        others = [(lon, near) for lon in range(0, lon_devices, 2) for near in range(2)]
        order = [(lon + core, near) for core in (1, 0) for lon, near in others]
        targets = jnp.stack(
            [(me_lon ^ lon) * lat_devices + (me_lat ^ (2 * far + near)) for lon, near in order]
        ).astype(jnp.int32)
        send, keep = partial_grams(
            sizes, targets, requests, obs_anom, ext, obs_lon, obs_lat, obs_rinv, totals
        )
        got = swap(send, "lon", 1)
        [total] = add_all([keep], [got])
        total = total.reshape(lon_devices // 2, 2, *total.shape[1:])
        cut = patches // 4
        first, second = total[:, :, :cut], total[:, :, cut:]
        shape = (-1, *first.shape[2:])
        far_lon = lon_devices // 4
        keeps = [first[:, 0], second[:far_lon].reshape(shape)]
        gots = [swap(first[:, 1], "lat", 1), swap(second[far_lon:].reshape(shape), "lon", lon_devices // 2)]
        first, second = add_all(keeps, gots)
        second = second.reshape(far_lon, 2, *second.shape[1:])
        keeps = [first[:far_lon], second[:, 0]]
        gots = [swap(first[far_lon:], "lon", lon_devices // 2), swap(second[:, 1], "lat", 1)]
        left = far_lon
        first, second = add_all(keeps, gots)
        while left > 1:
            left //= 2
            keeps = [first[:left], second[:left]]
            gots = [swap(v[left:], "lon", 2 * left) for v in (first, second)]
            first, second = add_all(keeps, gots)
        return jnp.concatenate([first[0], second[0]], axis=0)

    parts = []
    for far in reversed(range(lat_devices // 2)):
        total = chunk(far)
        parts.append(swap(total, "lat", 2 * far) if far else total)
    weights = solve(parts, holders * held * block_obs)
    updated = analysis(
        weights,
        state_pert.reshape(patches, fields, members, columns),
        state_mean.reshape(patches, fields, columns),
    )
    return updated.reshape(lon_patches, lat_patches, fields, members, columns)


def solution(mesh):
    in_specs = (
        P("lon", "lat", None, None, None),
        P("lon", "lat", None, None),
        P(("lon", "lat"), None, None),
        P(("lon", "lat"), None),
        P(("lon", "lat"), None),
        P(("lon", "lat"), None),
        P(("lon", "lat"), None),
        P("lon", "lat", None),
        P("lon", "lat"),
    )
    out_specs = P("lon", "lat", None, None, None)
    return jax.shard_map(
        on_device, mesh=mesh, in_specs=in_specs, out_specs=out_specs, check_vma=False
    )
```

```python
import functools

import jax
import jax.numpy as jnp
from jax import lax
from jax.experimental import pallas as pl
from jax.experimental.pallas import tpu as pltpu
from jax.sharding import PartitionSpec as P

PSIDE = 16
NS_ITERS = 5
LOC_SCALE = 48.0
GROUP = 4
EXT = 16
F32 = jnp.float32
BF16 = jnp.bfloat16
NT = (((1,), (1,)), ((), ()))


def halves(value):
    high = value.astype(BF16)
    return high, (value - high.astype(F32)).astype(BF16)


def request_table(block_list, block_count, holders, held_blocks):
    patches, length = block_list.shape
    slots = patches * length
    per_owner = slots // holders
    wanted = block_list.reshape(slots)
    used = (lax.broadcasted_iota(jnp.int32, (patches, length), 1) < block_count[:, None]).reshape(
        slots
    )
    holder = jnp.where(used, wanted // held_blocks, holders)
    order = jnp.arange(slots)
    before = (holder[:, None] == holder[None, :]) & (order[None, :] < order[:, None])
    rank = jnp.sum(before.astype(jnp.int32), axis=1)
    code = (order // length) * held_blocks + wanted % held_blocks
    place = holder * per_owner + rank
    hit = (place[None, :] == jnp.arange(holders * per_owner)[:, None]) & used[None, :]
    table = jnp.sum(jnp.where(hit, code[None, :], 0), axis=1).reshape(holders, per_owner)
    number = jnp.sum((holder[None, :] == jnp.arange(holders)[:, None]).astype(jnp.int32), axis=1)
    return jnp.concatenate([table, number[:, None]], axis=1)


def stage_kernel(
    chunk, anom_hbm, innov_ref, rinv_ref, lon_ref, lat_ref, left_ref, fields_ref, totals_ref, sems
):
    held, members, block_obs = anom_hbm.shape
    copies = []
    for i in range(held // chunk):
        span = pl.ds(i * chunk, chunk)
        copy = pltpu.make_async_copy(
            anom_hbm.at[span], left_ref.at[span, pl.ds(0, members), :], sems.at[i]
        )
        copy.start()
        copies.append(copy)
    fields_ref[0] = (2 * lon_ref[...]).astype(F32)
    fields_ref[1] = (2 * lat_ref[...]).astype(F32)
    fields_ref[2] = rinv_ref[...]
    line = lax.broadcasted_iota(jnp.int32, (EXT, block_obs), 0)
    sums = jnp.zeros((8, block_obs), F32)
    for i, copy in enumerate(copies):
        copy.wait()

        def block(j, total, first=i * chunk):
            at = first + j
            values = left_ref[at, :members, :].astype(F32)
            squares = jnp.sum((values * values).reshape(members // 8, 8, block_obs), axis=0)
            innov = innov_ref[pl.ds(at, 1), :]
            high = innov.astype(BF16).astype(F32)
            rows = jnp.where(line == 0, high, jnp.where(line == 1, innov - high, 0.0))
            left_ref[at, members:, :] = rows.astype(BF16)
            return total + squares * rinv_ref[pl.ds(at, 1), :]

        sums = lax.fori_loop(0, chunk, block, sums, unroll=4)
    innovation = jnp.sum(rinv_ref[...] * innov_ref[...] * innov_ref[...], axis=0, keepdims=True)
    spread = jnp.sum(sums, axis=0, keepdims=True) / (members - 1)
    line = lax.broadcasted_iota(jnp.int32, (8, block_obs), 0)
    totals_ref[...] = jnp.where(line == 4, innovation, jnp.where(line == 5, spread, 0.0))


def stage(anom, innov, rinv, lon, lat):
    held, members, block_obs = anom.shape
    chunk = 16 if held % 16 == 0 else held
    whole = pl.BlockSpec(memory_space=pltpu.VMEM)
    return pl.pallas_call(
        functools.partial(stage_kernel, chunk),
        out_shape=[
            pltpu.VMEM((held, members + EXT, block_obs), BF16),
            pltpu.VMEM((3, held, block_obs), F32),
            pltpu.VMEM((8, block_obs), F32),
        ],
        in_specs=[pl.BlockSpec(memory_space=pltpu.HBM)] + [whole] * 4,
        out_specs=[whole] * 3,
        scratch_shapes=[pltpu.SemaphoreType.DMA((held // chunk,))],
        compiler_params=pltpu.CompilerParams(vmem_limit_bytes=4 * 2**20),
        cost_estimate=pl.CostEstimate(flops=0, bytes_accessed=anom.size * 4, transcendentals=0),
        name="stage",
    )(anom, innov, rinv, lon, lat)


def gram_kernel(
    sizes, targets_ref, requests_ref, left_ref, fields_ref, totals_ref, out_ref, acc_ref
):
    patches, lat_patches, lon_patches, lat_devices, held, per_owner, grid_lon = sizes
    target = targets_ref[pl.program_id(0)]
    lon_first = (target // lat_devices) * lon_patches
    lat_first = (target % lat_devices) * lat_patches
    members = left_ref.shape[2]
    acc_ref[...] = jnp.zeros_like(acc_ref)
    number = requests_ref[target, per_owner]

    def group(start, _):
        products = []
        for i in range(GROUP):
            entry = start * GROUP + i
            code = requests_ref[target, jnp.minimum(entry, per_owner - 1)]
            patch = code // held
            block = code % held
            centre_lon = (lon_first + patch // lat_patches) * (2 * PSIDE) + (PSIDE - 1)
            centre_lat = (lat_first + patch % lat_patches) * (2 * PSIDE) + (PSIDE - 1)
            row = pl.ds(block, 1)
            lon_gap = jnp.abs(fields_ref[0, row, :] - centre_lon.astype(F32))
            lon_gap = jnp.minimum(lon_gap, 2.0 * grid_lon - lon_gap)
            lat_gap = fields_ref[1, row, :] - centre_lat.astype(F32)
            square = lon_gap * lon_gap + lat_gap * lat_gap
            rinv = jnp.where(entry < number, fields_ref[2, row, :], 0.0)
            weight = rinv * jnp.exp(square * (-1.0 / (8.0 * LOC_SCALE * LOC_SCALE)))
            left = left_ref[block]
            scaled = (left[:members].astype(F32) * weight).astype(BF16)
            product = lax.dot_general(left, scaled, NT, preferred_element_type=F32)
            products.append((patch, product[: members + 8]))
        for patch, product in products:
            acc_ref[patch] += product
        return 0

    lax.fori_loop(0, (number + GROUP - 1) // GROUP, group, 0)

    row = lax.broadcasted_iota(jnp.int32, (members, members), 0)
    column = lax.broadcasted_iota(jnp.int32, (members, members), 1)
    line = lax.broadcasted_iota(jnp.int32, (8, members), 0)
    for pair in range(patches // 2):
        first = acc_ref[2 * pair]
        second = acc_ref[2 * pair + 1]
        packed = jnp.where(row < column, first[:members], second[:members])
        out_ref[0, pair, :members, :] = packed.astype(BF16)
        rows = totals_ref[...]
        for place, values in ((0, first), (2, second)):
            diagonal = jnp.sum(
                jnp.where(row == column, values[:members], 0.0), axis=0, keepdims=True
            )
            projected = values[members : members + 1] + values[members + 1 : members + 2]
            rows = jnp.where(line == place, diagonal, rows)
            rows = jnp.where(line == place + 1, projected, rows)
        high = rows.astype(BF16).astype(F32)
        out_ref[0, pair, members:, :] = jnp.concatenate([high, rows - high], axis=0).astype(BF16)


def partial_grams(sizes, targets, requests, staged):
    patches, per_owner = sizes[0], sizes[5]
    count = targets.shape[0]
    members = staged[0].shape[2]
    rows = members + EXT
    block = (1, patches // 2, rows, members)
    return pl.pallas_call(
        functools.partial(gram_kernel, sizes),
        out_shape=jax.ShapeDtypeStruct((count, *block[1:]), BF16),
        grid_spec=pltpu.PrefetchScalarGridSpec(
            num_scalar_prefetch=2,
            grid=(count,),
            in_specs=[pl.BlockSpec(memory_space=pltpu.VMEM)] * 3,
            out_specs=pl.BlockSpec(block, lambda i, *_: (i, 0, 0, 0)),
            scratch_shapes=[pltpu.VMEM((patches, members + 8, members), F32)],
        ),
        compiler_params=pltpu.CompilerParams(vmem_limit_bytes=6 * 2**20),
        cost_estimate=pl.CostEstimate(
            flops=count * per_owner * 40 * members**3, bytes_accessed=0, transcendentals=0
        ),
        name="partial_grams",
    )(targets, requests, *staged)


def added(left, right):
    members = left.shape[-1]
    total = left.astype(F32) + right.astype(F32)
    rows = total[:, members : members + 8] + total[:, members + 8 :]
    high = rows.astype(BF16).astype(F32)
    rows = jnp.concatenate([high, rows - high], axis=1)
    return total[:, :members].astype(BF16), rows.astype(BF16)


def add_kernel(count, *refs):
    keep, got, outs = refs[:count], refs[count : 2 * count], refs[2 * count :]
    for i in range(count):
        members = keep[i].shape[-1]
        body, rows = added(keep[i][0], got[i][0])
        outs[i][0, :, :members, :] = body
        outs[i][0, :, members:, :] = rows


def add_all(keep, got):
    count = len(keep)
    shape = keep[0].shape
    spec = pl.BlockSpec((1, *shape[1:]), lambda i: (i, 0, 0, 0))
    size = keep[0].size * count
    return pl.pallas_call(
        functools.partial(add_kernel, count),
        out_shape=[jax.ShapeDtypeStruct(shape, BF16)] * count,
        grid=(shape[0],),
        in_specs=[spec] * (2 * count),
        out_specs=[spec] * count,
        compiler_params=pltpu.CompilerParams(vmem_limit_bytes=16 * 2**20),
        cost_estimate=pl.CostEstimate(flops=size * 4, bytes_accessed=size * 6, transcendentals=0),
        name="add_partials",
    )(*keep, *got)


def product(left, right):
    left_high, left_low = left
    right_high, right_low = right
    return jnp.dot(
        jnp.concatenate([left_high, left_low, left_high], axis=1),
        jnp.concatenate([right_high, right_high, right_low], axis=0),
        preferred_element_type=F32,
    )


def solve_kernel(count, total_obs, *refs):
    parts, (out_ref,) = refs[:count], refs[count:]
    pairs, rows, members = parts[0].shape
    row = lax.broadcasted_iota(jnp.int32, (members, members), 0)
    column = lax.broadcasted_iota(jnp.int32, (members, members), 1)
    identity = (row == column).astype(F32)

    def gathered(pair):
        total = parts[0][pair].astype(F32)
        for part in parts[1:]:
            total = total + part[pair].astype(F32)
        return total[:members], total[members : members + 8] + total[members + 8 :]

    def some(step, _):
        systems, projected = [], []
        for pair in (2 * step, 2 * step + 1):
            packed, values = gathered(pair)
            flipped = packed.T
            innovation = jnp.sum(values[4:5], axis=1, keepdims=True)
            spread = jnp.sum(values[5:6], axis=1, keepdims=True)
            ridge = (members - 1) * (spread + total_obs) / innovation
            for place, full in (
                (0, jnp.where(row < column, packed, flipped)),
                (2, jnp.where(row > column, packed, flipped)),
            ):
                full = jnp.where(row == column, values[place : place + 1], full)
                systems.append(full + ridge * identity)
                projected.append(values[place + 1 : place + 2])
        scalings, roots, inverses = [], [], []
        for system in systems:
            squares = jnp.sum(system * system, axis=0, keepdims=True)
            scaling = jnp.sqrt(jnp.sum(squares, axis=1, keepdims=True))
            scalings.append(scaling)
            roots.append(system / scaling)
        factors = [1.5 * identity - 0.5 * root for root in roots]
        roots = [product(halves(f), halves(r)) for f, r in zip(factors, roots)]
        inverses = factors
        for iteration in range(1, NS_ITERS):
            split_roots = [halves(r) for r in roots]
            split_inverses = [halves(z) for z in inverses]
            factors = [
                halves(1.5 * identity - 0.5 * product(z, r))
                for z, r in zip(split_inverses, split_roots)
            ]
            if iteration < NS_ITERS - 1:
                both = [
                    product(f, [jnp.concatenate([a, b], axis=1) for a, b in zip(r, z)])
                    for f, r, z in zip(factors, split_roots, split_inverses)
                ]
                roots = [b[:, :members] for b in both]
                inverses = [b[:, members:] for b in both]
            else:
                inverses = [product(f, z) for f, z in zip(factors, split_inverses)]
        for i in range(4):
            inverse_sqrt = inverses[i] * lax.rsqrt(scalings[i])
            inner = jnp.sum(inverse_sqrt * projected[i], axis=1, keepdims=True)
            mean = jnp.sum(inverse_sqrt * inner, axis=0, keepdims=True)
            out_ref[4 * step + i] = (
                jnp.sqrt(F32(members - 1)) * inverse_sqrt + mean
            ).astype(BF16)
        return 0

    lax.fori_loop(0, pairs // 2, some, 0)


def solve(parts, total_obs):
    pairs, rows, members = parts[0].shape
    whole = pl.BlockSpec(memory_space=pltpu.VMEM)
    return pl.pallas_call(
        functools.partial(solve_kernel, len(parts), total_obs),
        out_shape=jax.ShapeDtypeStruct((2 * pairs, members, members), BF16),
        in_specs=[whole] * len(parts),
        out_specs=whole,
        compiler_params=pltpu.CompilerParams(vmem_limit_bytes=32 * 2**20),
        name="solve",
    )(*parts)


def analysis_kernel(weights_ref, pert_ref, mean_ref, out_ref):
    for field in range(pert_ref.shape[1]):
        change = jnp.dot(weights_ref[0], pert_ref[0, field], preferred_element_type=F32)
        out_ref[0, field] = change + mean_ref[0, field : field + 1]


def analysis(weights, pert, mean):
    patches, fields, members, columns = pert.shape
    return pl.pallas_call(
        analysis_kernel,
        out_shape=jax.ShapeDtypeStruct(pert.shape, F32),
        grid=(patches,),
        in_specs=[
            pl.BlockSpec((1, members, members), lambda i: (i, 0, 0)),
            pl.BlockSpec((1, fields, members, columns), lambda i: (i, 0, 0, 0)),
            pl.BlockSpec((1, fields, columns), lambda i: (i, 0, 0)),
        ],
        out_specs=pl.BlockSpec((1, fields, members, columns), lambda i: (i, 0, 0, 0)),
        compiler_params=pltpu.CompilerParams(vmem_limit_bytes=16 * 2**20),
        name="analysis",
    )(weights, pert, mean)


def swap(value, axis, flip):
    size = lax.axis_size(axis)
    return lax.ppermute(value, axis, [(i, i ^ flip) for i in range(size)])


def on_device(
    state_pert, state_mean, obs_anom, innov, obs_rinv, obs_lon, obs_lat, block_list, block_count
):
    lon_devices, lat_devices = lax.axis_size("lon"), lax.axis_size("lat")
    holders = lon_devices * lat_devices
    lon_patches, lat_patches, fields, members, columns = state_pert.shape
    patches = lon_patches * lat_patches
    length = block_list.shape[2]
    held, _, block_obs = obs_anom.shape
    per_owner = patches * length // holders
    table = request_table(
        block_list.reshape(patches, length), block_count.reshape(patches), holders, held
    )
    requests = lax.all_to_all(table, ("lon", "lat"), split_axis=0, concat_axis=0, tiled=True)

    staged = stage(obs_anom, innov, obs_rinv, obs_lon, obs_lat)
    staged = [pltpu.with_memory_space_constraint(v, pltpu.VMEM) for v in staged]

    me_lon, me_lat = lax.axis_index("lon"), lax.axis_index("lat")
    sizes = (
        patches,
        lat_patches,
        lon_patches,
        lat_devices,
        held,
        per_owner,
        lon_devices * lon_patches * PSIDE,
    )

    y_count = lon_devices // 2

    def grams(far, core, after):
        order = [(2 * y + core, 2 * far + near) for y in range(y_count) for near in range(2)]
        targets = jnp.stack(
            [(me_lon ^ lon) * lat_devices + (me_lat ^ lat) for lon, lat in order]
        ).astype(jnp.int32)
        targets, _ = lax.optimization_barrier((targets, after))
        return partial_grams(sizes, targets, requests, staged)

    def steps(far):
        send = yield far, 1
        got = swap(send, "lon", 1)
        keep = yield far, 0
        [total] = add_all([keep], [got])
        total = total.reshape(y_count, 2, *total.shape[1:])
        cut = patches // 4
        first, second = total[:, :, :cut], total[:, :, cut:]
        shape = (-1, *first.shape[2:])
        left = y_count // 2
        keeps = [first[:, 0], second[:left].reshape(shape)]
        gots = [
            swap(first[:, 1], "lat", 1),
            swap(second[left:].reshape(shape), "lon", lon_devices // 2),
        ]
        gots = yield gots, [total]
        first, second = add_all(keeps, gots)
        sums = [first, second]
        second = second.reshape(left, 2, *second.shape[1:])
        keeps = [first[:left], second[:, 0]]
        gots = [
            swap(first[left:], "lon", lon_devices // 2),
            swap(second[:, 1], "lat", 1),
        ]
        gots = yield gots, sums
        first, second = add_all(keeps, gots)
        while left > 1:
            left //= 2
            keeps = [first[:left], second[:left]]
            gots = [swap(v[left:], "lon", 2 * left) for v in (first, second)]
            first, second = add_all(keeps, gots)
        total = jnp.concatenate([first[0], second[0]], axis=0)
        yield (swap(total, "lat", 2 * far) if far else total), total

    parts, open_chunks, after = [], [], []

    def advance(latest):
        nonlocal open_chunks, after
        still, after = [], []
        for chunk, waits in open_chunks:
            if latest is not None:
                waits, _ = lax.optimization_barrier((waits, latest))
            waits, sums = chunk.send(waits)
            if isinstance(sums, list):
                still.append((chunk, waits))
                after += sums
            else:
                parts.append(waits)
                after.append(sums)
        open_chunks = still

    latest = None
    for far in reversed(range(lat_devices // 2)):
        chunk = steps(far)
        send = grams(*next(chunk), after)
        request = chunk.send(send)
        advance(send)
        keep = grams(*request, after)
        waits, sums = chunk.send(keep)
        advance(keep)
        open_chunks.append((chunk, waits))
        after += sums
    while open_chunks:
        advance(None)
    weights = solve(parts, holders * held * block_obs)
    updated = analysis(
        weights,
        state_pert.reshape(patches, fields, members, columns),
        state_mean.reshape(patches, fields, columns),
    )
    return updated.reshape(lon_patches, lat_patches, fields, members, columns)


def solution(mesh):
    in_specs = (
        P("lon", "lat", None, None, None),
        P("lon", "lat", None, None),
        P(("lon", "lat"), None, None),
        P(("lon", "lat"), None),
        P(("lon", "lat"), None),
        P(("lon", "lat"), None),
        P(("lon", "lat"), None),
        P("lon", "lat", None),
        P("lon", "lat"),
    )
    out_specs = P("lon", "lat", None, None, None)
    return jax.shard_map(
        on_device, mesh=mesh, in_specs=in_specs, out_specs=out_specs, check_vma=False
    )
```

```python
import functools

import jax
import jax.numpy as jnp
from jax import lax
from jax.experimental import pallas as pl
from jax.experimental.pallas import tpu as pltpu
from jax.sharding import PartitionSpec as P

PSIDE = 16
NS_ITERS = 5
LOC_SCALE = 48.0
GROUP = 4
EXT = 16
F32 = jnp.float32
BF16 = jnp.bfloat16
NT = (((1,), (1,)), ((), ()))


def halves(value):
    high = value.astype(BF16)
    return high, (value - high.astype(F32)).astype(BF16)


def request_table(block_list, block_count, holders, held_blocks):
    patches, length = block_list.shape
    slots = patches * length
    per_owner = slots // holders
    wanted = block_list.reshape(slots)
    used = (lax.broadcasted_iota(jnp.int32, (patches, length), 1) < block_count[:, None]).reshape(
        slots
    )
    holder = jnp.where(used, wanted // held_blocks, holders)
    order = jnp.arange(slots)
    before = (holder[:, None] == holder[None, :]) & (order[None, :] < order[:, None])
    rank = jnp.sum(before.astype(jnp.int32), axis=1)
    code = (order // length) * held_blocks + wanted % held_blocks
    place = holder * per_owner + rank
    hit = (place[None, :] == jnp.arange(holders * per_owner)[:, None]) & used[None, :]
    table = jnp.sum(jnp.where(hit, code[None, :], 0), axis=1).reshape(holders, per_owner)
    number = jnp.sum((holder[None, :] == jnp.arange(holders)[:, None]).astype(jnp.int32), axis=1)
    return jnp.concatenate([table, number[:, None]], axis=1)


def stage_kernel(
    chunk,
    anom_hbm,
    innov_hbm,
    rinv_hbm,
    lon_hbm,
    lat_hbm,
    left_ref,
    rinv_ref,
    lon_ref,
    lat_ref,
    totals_ref,
    innov_ref,
    sems,
):
    held, members, block_obs = anom_hbm.shape
    pairs = [(rinv_hbm, rinv_ref), (innov_hbm, innov_ref)]
    for i in range(held // chunk):
        span = pl.ds(i * chunk, chunk)
        pairs.append((anom_hbm.at[span], left_ref.at[span, pl.ds(0, members), :]))
    pairs += [(lon_hbm, lon_ref), (lat_hbm, lat_ref)]
    copies = [pltpu.make_async_copy(a, b, sems.at[i]) for i, (a, b) in enumerate(pairs)]
    for copy in copies:
        copy.start()
    copies[0].wait()
    copies[1].wait()
    line = lax.broadcasted_iota(jnp.int32, (EXT, block_obs), 0)
    sums = jnp.zeros((8, block_obs), F32)
    for i, copy in enumerate(copies[2:-2]):
        copy.wait()

        def block(j, total, first=i * chunk):
            at = first + j
            values = left_ref[at, :members, :].astype(F32)
            squares = jnp.sum((values * values).reshape(members // 8, 8, block_obs), axis=0)
            innov = innov_ref[pl.ds(at, 1), :]
            high = innov.astype(BF16).astype(F32)
            rows = jnp.where(line == 0, high, jnp.where(line == 1, innov - high, 0.0))
            left_ref[at, members:, :] = rows.astype(BF16)
            return total + squares * rinv_ref[pl.ds(at, 1), :]

        sums = lax.fori_loop(0, chunk, block, sums, unroll=4)
    innovation = jnp.sum(rinv_ref[...] * innov_ref[...] * innov_ref[...], axis=0, keepdims=True)
    spread = jnp.sum(sums, axis=0, keepdims=True) / (members - 1)
    line = lax.broadcasted_iota(jnp.int32, (8, block_obs), 0)
    totals_ref[...] = jnp.where(line == 4, innovation, jnp.where(line == 5, spread, 0.0))
    copies[-2].wait()
    copies[-1].wait()


def stage(anom, innov, rinv, lon, lat):
    held, members, block_obs = anom.shape
    chunk = 16 if held % 16 == 0 else held
    operands = [pltpu.with_memory_space_constraint(v, pltpu.HBM) for v in (anom, innov, rinv, lon, lat)]
    return pl.pallas_call(
        functools.partial(stage_kernel, chunk),
        out_shape=[
            pltpu.VMEM((held, members + EXT, block_obs), BF16),
            pltpu.VMEM((held, block_obs), F32),
            pltpu.VMEM((held, block_obs), jnp.int32),
            pltpu.VMEM((held, block_obs), jnp.int32),
            pltpu.VMEM((8, block_obs), F32),
        ],
        in_specs=[pl.BlockSpec(memory_space=pltpu.HBM)] * 5,
        out_specs=[pl.BlockSpec(memory_space=pltpu.VMEM)] * 5,
        scratch_shapes=[
            pltpu.VMEM((held, block_obs), F32),
            pltpu.SemaphoreType.DMA((held // chunk + 4,)),
        ],
        compiler_params=pltpu.CompilerParams(vmem_limit_bytes=4 * 2**20),
        cost_estimate=pl.CostEstimate(flops=0, bytes_accessed=anom.size * 4, transcendentals=0),
        name="stage",
    )(*operands)


def gram_kernel(
    sizes,
    far,
    core,
    requests_ref,
    left_ref,
    rinv_ref,
    obs_lon_ref,
    obs_lat_ref,
    totals_ref,
    out_ref,
    acc_ref,
):
    patches, lat_patches, lon_patches, lat_devices, held, per_owner, grid_lon = sizes
    step = pl.program_id(0)
    me = requests_ref[0, per_owner + 1]
    distance = (2 * (step // 2) + core) * lat_devices + (2 * far + step % 2)
    target = me ^ distance
    lon_first = (target // lat_devices) * lon_patches
    lat_first = (target % lat_devices) * lat_patches
    members = left_ref.shape[2]
    acc_ref[...] = jnp.zeros_like(acc_ref)
    number = requests_ref[target, per_owner]

    def group(start, _):
        products = []
        for i in range(GROUP):
            entry = start * GROUP + i
            code = requests_ref[target, jnp.minimum(entry, per_owner - 1)]
            patch = code // held
            block = code % held
            centre_lon = (lon_first + patch // lat_patches) * (2 * PSIDE) + (PSIDE - 1)
            centre_lat = (lat_first + patch % lat_patches) * (2 * PSIDE) + (PSIDE - 1)
            row = pl.ds(block, 1)
            lon_gap = jnp.abs(2 * obs_lon_ref[row, :] - centre_lon)
            lon_gap = jnp.minimum(lon_gap, 2 * grid_lon - lon_gap)
            lat_gap = 2 * obs_lat_ref[row, :] - centre_lat
            square = (lon_gap * lon_gap + lat_gap * lat_gap).astype(F32)
            rinv = jnp.where(entry < number, rinv_ref[row, :], 0.0)
            weight = rinv * jnp.exp(square * (-1.0 / (8.0 * LOC_SCALE * LOC_SCALE)))
            left = left_ref[block]
            scaled = (left[:members].astype(F32) * weight).astype(BF16)
            product = lax.dot_general(left, scaled, NT, preferred_element_type=F32)
            products.append((patch, product[: members + 8]))
        for patch, product in products:
            acc_ref[patch] += product
        return 0

    lax.fori_loop(0, (number + GROUP - 1) // GROUP, group, 0)

    row = lax.broadcasted_iota(jnp.int32, (members, members), 0)
    column = lax.broadcasted_iota(jnp.int32, (members, members), 1)
    line = lax.broadcasted_iota(jnp.int32, (8, members), 0)
    for pair in range(patches // 2):
        first = acc_ref[2 * pair]
        second = acc_ref[2 * pair + 1]
        packed = jnp.where(row < column, first[:members], second[:members])
        out_ref[0, pair, :members, :] = packed.astype(BF16)
        rows = totals_ref[...]
        for place, values in ((0, first), (2, second)):
            diagonal = jnp.sum(
                jnp.where(row == column, values[:members], 0.0), axis=0, keepdims=True
            )
            projected = values[members : members + 1] + values[members + 1 : members + 2]
            rows = jnp.where(line == place, diagonal, rows)
            rows = jnp.where(line == place + 1, projected, rows)
        high = rows.astype(BF16).astype(F32)
        out_ref[0, pair, members:, :] = jnp.concatenate([high, rows - high], axis=0).astype(BF16)


def partial_grams(sizes, far, core, count, requests, staged):
    patches, per_owner = sizes[0], sizes[5]
    members = staged[0].shape[2]
    rows = members + EXT
    block = (1, patches // 2, rows, members)
    return pl.pallas_call(
        functools.partial(gram_kernel, sizes, far, core),
        out_shape=jax.ShapeDtypeStruct((count, *block[1:]), BF16),
        grid_spec=pltpu.PrefetchScalarGridSpec(
            num_scalar_prefetch=1,
            grid=(count,),
            in_specs=[pl.BlockSpec(memory_space=pltpu.VMEM)] * 5,
            out_specs=pl.BlockSpec(block, lambda i, *_: (i, 0, 0, 0)),
            scratch_shapes=[pltpu.VMEM((patches, members + 8, members), F32)],
        ),
        compiler_params=pltpu.CompilerParams(vmem_limit_bytes=6 * 2**20),
        cost_estimate=pl.CostEstimate(
            flops=count * per_owner * 100 * members**3, bytes_accessed=0, transcendentals=0
        ),
        name="partial_grams",
    )(requests, *staged)


def added(left, right):
    members = left.shape[-1]
    total = left.astype(F32) + right.astype(F32)
    rows = total[:, members : members + 8] + total[:, members + 8 :]
    high = rows.astype(BF16).astype(F32)
    rows = jnp.concatenate([high, rows - high], axis=1)
    return total[:, :members].astype(BF16), rows.astype(BF16)


def add_kernel(count, plan, *refs):
    keep, got, outs = refs[:count], refs[count : 2 * count], refs[2 * count :]
    for part, index, low, high, out, place, at in plan:
        members = keep[part].shape[-1]
        body, rows = added(keep[part][index, low:high], got[part][index, low:high])
        to = slice(at, at + high - low)
        outs[out][place, to, :members, :] = body
        outs[out][place, to, members:, :] = rows


def add_all(keep, got, plan, shapes):
    count = len(keep)
    inner = keep[0].shape[2:]
    whole = pl.BlockSpec(memory_space=pltpu.VMEM)
    size = sum(v.size for v in keep)
    return pl.pallas_call(
        functools.partial(add_kernel, count, plan),
        out_shape=[jax.ShapeDtypeStruct((*shape, *inner), BF16) for shape in shapes],
        in_specs=[whole] * (2 * count),
        out_specs=[whole] * len(shapes),
        compiler_params=pltpu.CompilerParams(vmem_limit_bytes=8 * 2**20),
        cost_estimate=pl.CostEstimate(flops=size * 4, bytes_accessed=size * 6, transcendentals=0),
        name="add_partials",
    )(*keep, *got)


def product(left, right):
    left_high, left_low = left
    right_high, right_low = right
    return jnp.dot(
        jnp.concatenate([left_high, left_low, left_high], axis=1),
        jnp.concatenate([right_high, right_high, right_low], axis=0),
        preferred_element_type=F32,
    )


def solve_kernel(count, total_obs, *refs):
    parts, (out_ref,) = refs[:count], refs[count:]
    pairs, rows, members = parts[0].shape
    row = lax.broadcasted_iota(jnp.int32, (members, members), 0)
    column = lax.broadcasted_iota(jnp.int32, (members, members), 1)
    identity = (row == column).astype(F32)

    def gathered(pair):
        total = parts[0][pair].astype(F32)
        for part in parts[1:]:
            total = total + part[pair].astype(F32)
        return total[:members], total[members : members + 8] + total[members + 8 :]

    def some(step, _):
        systems, projected = [], []
        for pair in (2 * step, 2 * step + 1):
            packed, values = gathered(pair)
            flipped = packed.T
            innovation = jnp.sum(values[4:5], axis=1, keepdims=True)
            spread = jnp.sum(values[5:6], axis=1, keepdims=True)
            ridge = (members - 1) * (spread + total_obs) / innovation
            for place, full in (
                (0, jnp.where(row < column, packed, flipped)),
                (2, jnp.where(row > column, packed, flipped)),
            ):
                full = jnp.where(row == column, values[place : place + 1], full)
                systems.append(full + ridge * identity)
                projected.append(values[place + 1 : place + 2])
        scalings, roots, inverses = [], [], []
        for system in systems:
            squares = jnp.sum(system * system, axis=0, keepdims=True)
            scaling = jnp.sqrt(jnp.sum(squares, axis=1, keepdims=True))
            scalings.append(scaling)
            roots.append(system / scaling)
        factors = [1.5 * identity - 0.5 * root for root in roots]
        roots = [product(halves(f), halves(r)) for f, r in zip(factors, roots)]
        inverses = factors
        for iteration in range(1, NS_ITERS):
            split_roots = [halves(r) for r in roots]
            split_inverses = [halves(z) for z in inverses]
            factors = [
                halves(1.5 * identity - 0.5 * product(z, r))
                for z, r in zip(split_inverses, split_roots)
            ]
            if iteration < NS_ITERS - 1:
                both = [
                    product(f, [jnp.concatenate([a, b], axis=1) for a, b in zip(r, z)])
                    for f, r, z in zip(factors, split_roots, split_inverses)
                ]
                roots = [b[:, :members] for b in both]
                inverses = [b[:, members:] for b in both]
            else:
                inverses = [product(f, z) for f, z in zip(factors, split_inverses)]
        for i in range(4):
            inverse_sqrt = inverses[i] * lax.rsqrt(scalings[i])
            inner = jnp.sum(inverse_sqrt * projected[i], axis=1, keepdims=True)
            mean = jnp.sum(inverse_sqrt * inner, axis=0, keepdims=True)
            out_ref[4 * step + i] = (
                jnp.sqrt(F32(members - 1)) * inverse_sqrt + mean
            ).astype(BF16)
        return 0

    lax.fori_loop(0, pairs // 2, some, 0)


def solve(parts, total_obs):
    pairs, rows, members = parts[0].shape
    whole = pl.BlockSpec(memory_space=pltpu.VMEM)
    return pl.pallas_call(
        functools.partial(solve_kernel, len(parts), total_obs),
        out_shape=jax.ShapeDtypeStruct((2 * pairs, members, members), BF16),
        in_specs=[whole] * len(parts),
        out_specs=whole,
        compiler_params=pltpu.CompilerParams(vmem_limit_bytes=8 * 2**20),
        name="solve",
    )(*parts)


def analysis_kernel(weights_ref, pert_ref, mean_ref, out_ref):
    for field in range(pert_ref.shape[1]):
        change = jnp.dot(weights_ref[0], pert_ref[0, field], preferred_element_type=F32)
        out_ref[0, field] = change + mean_ref[0, field : field + 1]


def analysis(weights, pert, mean):
    patches, fields, members, columns = pert.shape
    return pl.pallas_call(
        analysis_kernel,
        out_shape=jax.ShapeDtypeStruct(pert.shape, F32),
        grid=(patches,),
        in_specs=[
            pl.BlockSpec((1, members, members), lambda i: (i, 0, 0)),
            pl.BlockSpec((1, fields, members, columns), lambda i: (i, 0, 0, 0)),
            pl.BlockSpec((1, fields, columns), lambda i: (i, 0, 0)),
        ],
        out_specs=pl.BlockSpec((1, fields, members, columns), lambda i: (i, 0, 0, 0)),
        compiler_params=pltpu.CompilerParams(vmem_limit_bytes=8 * 2**20),
        name="analysis",
    )(weights, pert, mean)


def swap(value, axis, flip):
    size = lax.axis_size(axis)
    return lax.ppermute(value, axis, [(i, i ^ flip) for i in range(size)])


def on_device(
    state_pert, state_mean, obs_anom, innov, obs_rinv, obs_lon, obs_lat, block_list, block_count
):
    lon_devices, lat_devices = lax.axis_size("lon"), lax.axis_size("lat")
    holders = lon_devices * lat_devices
    lon_patches, lat_patches, fields, members, columns = state_pert.shape
    patches = lon_patches * lat_patches
    length = block_list.shape[2]
    held, _, block_obs = obs_anom.shape
    per_owner = patches * length // holders
    table = request_table(
        block_list.reshape(patches, length), block_count.reshape(patches), holders, held
    )
    requests = lax.all_to_all(table, ("lon", "lat"), split_axis=0, concat_axis=0, tiled=True)

    me = lax.axis_index(("lon", "lat")).astype(jnp.int32)
    requests = jnp.concatenate([requests, jnp.full((holders, 1), me)], axis=1)
    requests, observed = lax.optimization_barrier(
        (requests, (obs_anom, innov, obs_rinv, obs_lon, obs_lat))
    )
    staged = stage(*observed)
    sizes = (
        patches,
        lat_patches,
        lon_patches,
        lat_devices,
        held,
        per_owner,
        lon_devices * lon_patches * PSIDE,
    )
    y_count = lon_devices // 2
    pairs = patches // 2
    cut = pairs // 2

    def grams(far, core, after):
        tied, _ = lax.optimization_barrier((requests, after))
        return partial_grams(sizes, far, core, lon_devices, tied, staged)

    def steps(far):
        send = yield far, 1
        got = swap(send, "lon", 1)
        keep = yield [got], [send]
        left = y_count // 2
        plan = []
        for y in range(y_count):
            for near in range(2):
                plan.append((0, 2 * y + near, 0, cut, near, y, 0))
                far_y, place = divmod(y, left)
                plan.append((0, 2 * y + near, cut, pairs, 2 + far_y, 2 * place + near, 0))
        keep_a, send_a, keep_b, send_b = add_all(
            [keep[0]],
            [keep[1]],
            plan,
            [(y_count, cut)] * 2 + [(2 * left, pairs - cut)] * 2,
        )
        got_a, got_b = yield [swap(send_a, "lat", 1), swap(send_b, "lon", y_count)], [send_a, send_b]
        plan = []
        for y in range(y_count):
            far_y, place = divmod(y, left)
            plan.append((0, y, 0, cut, far_y, place, 0))
        for y in range(left):
            for near in range(2):
                plan.append((1, 2 * y + near, 0, pairs - cut, 2 + near, y, 0))
        keep_a, send_a, keep_b, send_b = add_all(
            [keep_a, keep_b],
            [got_a, got_b],
            plan,
            [(left, cut)] * 2 + [(left, pairs - cut)] * 2,
        )
        got_a, got_b = yield [swap(send_a, "lon", y_count), swap(send_b, "lat", 1)], [send_a, send_b]
        while left > 1:
            left //= 2
            plan = []
            for part in range(2):
                for y in range(2 * left):
                    far_y, place = divmod(y, left)
                    plan.append((part, y, 0, keep_a.shape[1] if part == 0 else pairs - cut, 2 * part + far_y, place, 0))
            keep_a, send_a, keep_b, send_b = add_all(
                [keep_a, keep_b],
                [got_a, got_b],
                plan,
                [(left, cut)] * 2 + [(left, pairs - cut)] * 2,
            )
            got_a, got_b = yield (
                [swap(send_a, "lon", 2 * left), swap(send_b, "lon", 2 * left)],
                [send_a, send_b],
            )
        plan = [(0, 0, 0, cut, 0, 0, 0), (1, 0, 0, pairs - cut, 0, 0, cut)]
        [total] = add_all([keep_a, keep_b], [got_a, got_b], plan, [(1, pairs)])
        if far:
            [total] = yield [swap(total, "lat", 2 * far)], [total]
        parts.append(total)

    parts, open_chunks, sent = [], [], []

    def advance(latest):
        nonlocal open_chunks, sent
        flat = [w for _, waits in open_chunks for w in waits]
        if latest is not None:
            latest, flat = lax.optimization_barrier((latest, flat))
        still, sent = [], []
        for chunk, waits in open_chunks:
            now, flat = flat[: len(waits)], flat[len(waits) :]
            if latest is not None and chunk is newest:
                now = [latest, *now]
            try:
                waits, sums = chunk.send(now)
                still.append((chunk, waits))
                sent += sums
            except StopIteration:
                pass
        open_chunks = still

    newest = None
    for far in reversed(range(lat_devices // 2)):
        chunk = steps(far)
        send = grams(*next(chunk), sent)
        advance(send)
        waits, sums = chunk.send(send)
        newest = chunk
        open_chunks.append((chunk, waits))
        keep = grams(far, 0, sent + sums)
        advance(keep)
        newest = None
    while open_chunks:
        advance(None)
    weights = solve([v[0] for v in parts], holders * held * block_obs)
    updated = analysis(
        weights,
        state_pert.reshape(patches, fields, members, columns),
        state_mean.reshape(patches, fields, columns),
    )
    return updated.reshape(lon_patches, lat_patches, fields, members, columns)


def solution(mesh):
    in_specs = (
        P("lon", "lat", None, None, None),
        P("lon", "lat", None, None),
        P(("lon", "lat"), None, None),
        P(("lon", "lat"), None),
        P(("lon", "lat"), None),
        P(("lon", "lat"), None),
        P(("lon", "lat"), None),
        P("lon", "lat", None),
        P("lon", "lat"),
    )
    out_specs = P("lon", "lat", None, None, None)
    return jax.shard_map(
        on_device, mesh=mesh, in_specs=in_specs, out_specs=out_specs, check_vma=False
    )
```

```python
import functools

import jax
import jax.numpy as jnp
from jax import lax
from jax.experimental import pallas as pl
from jax.experimental.pallas import tpu as pltpu
from jax.sharding import PartitionSpec as P

PSIDE = 16
NS_ITERS = 5
LOC_SCALE = 48.0
EXT = 16
F32 = jnp.float32
BF16 = jnp.bfloat16
NT = (((1,), (1,)), ((), ()))


def halves(value):
    high = value.astype(BF16)
    return high, (value - high.astype(F32)).astype(BF16)


def request_table(block_list, block_count, holders, held_blocks):
    patches, length = block_list.shape
    slots = patches * length
    per_owner = slots // holders
    wanted = block_list.reshape(slots)
    used = (lax.broadcasted_iota(jnp.int32, (patches, length), 1) < block_count[:, None]).reshape(
        slots
    )
    holder = jnp.where(used, wanted // held_blocks, holders)
    order = jnp.arange(slots)
    before = (holder[:, None] == holder[None, :]) & (order[None, :] < order[:, None])
    rank = jnp.sum(before.astype(jnp.int32), axis=1)
    code = (order // length) * held_blocks + wanted % held_blocks
    place = holder * per_owner + rank
    hit = (place[None, :] == jnp.arange(holders * per_owner)[:, None]) & used[None, :]
    table = jnp.sum(jnp.where(hit, code[None, :], 0), axis=1).reshape(holders, per_owner)
    number = jnp.sum((holder[None, :] == jnp.arange(holders)[:, None]).astype(jnp.int32), axis=1)
    return jnp.concatenate([table, number[:, None]], axis=1)


def stage_kernel(
    chunk,
    anom_hbm,
    innov_hbm,
    rinv_hbm,
    lon_hbm,
    lat_hbm,
    left_ref,
    rinv_ref,
    lon_ref,
    lat_ref,
    totals_ref,
    innov_ref,
    sems,
):
    held, members, block_obs = anom_hbm.shape
    pairs = [(rinv_hbm, rinv_ref), (innov_hbm, innov_ref)]
    for i in range(held // chunk):
        span = pl.ds(i * chunk, chunk)
        pairs.append((anom_hbm.at[span], left_ref.at[span, pl.ds(0, members), :]))
    pairs += [(lon_hbm, lon_ref), (lat_hbm, lat_ref)]
    copies = [pltpu.make_async_copy(a, b, sems.at[i]) for i, (a, b) in enumerate(pairs)]
    for copy in copies:
        copy.start()
    copies[0].wait()
    copies[1].wait()
    line = lax.broadcasted_iota(jnp.int32, (EXT, block_obs), 0)
    sums = jnp.zeros((8, block_obs), F32)
    for i, copy in enumerate(copies[2:-2]):
        copy.wait()

        def block(j, total, first=i * chunk):
            at = first + j
            values = left_ref[at, :members, :].astype(F32)
            squares = jnp.sum((values * values).reshape(members // 8, 8, block_obs), axis=0)
            innov = innov_ref[pl.ds(at, 1), :]
            high = innov.astype(BF16).astype(F32)
            rows = jnp.where(line == 0, high, jnp.where(line == 1, innov - high, 0.0))
            left_ref[at, members:, :] = rows.astype(BF16)
            return total + squares * rinv_ref[pl.ds(at, 1), :]

        sums = lax.fori_loop(0, chunk, block, sums, unroll=4)
    innovation = jnp.sum(rinv_ref[...] * innov_ref[...] * innov_ref[...], axis=0, keepdims=True)
    spread = jnp.sum(sums, axis=0, keepdims=True) / (members - 1)
    line = lax.broadcasted_iota(jnp.int32, (8, block_obs), 0)
    totals_ref[...] = jnp.where(line == 4, innovation, jnp.where(line == 5, spread, 0.0))
    copies[-2].wait()
    copies[-1].wait()


def stage(anom, innov, rinv, lon, lat):
    held, members, block_obs = anom.shape
    chunk = 16 if held % 16 == 0 else held
    operands = [pltpu.with_memory_space_constraint(v, pltpu.HBM) for v in (anom, innov, rinv, lon, lat)]
    return pl.pallas_call(
        functools.partial(stage_kernel, chunk),
        out_shape=[
            pltpu.VMEM((held, members + EXT, block_obs), BF16),
            pltpu.VMEM((held, block_obs), F32),
            pltpu.VMEM((held, block_obs), jnp.int32),
            pltpu.VMEM((held, block_obs), jnp.int32),
            pltpu.VMEM((8, block_obs), F32),
        ],
        in_specs=[pl.BlockSpec(memory_space=pltpu.HBM)] * 5,
        out_specs=[pl.BlockSpec(memory_space=pltpu.VMEM)] * 5,
        scratch_shapes=[
            pltpu.VMEM((held, block_obs), F32),
            pltpu.SemaphoreType.DMA((held // chunk + 4,)),
        ],
        compiler_params=pltpu.CompilerParams(vmem_limit_bytes=4 * 2**20),
        cost_estimate=pl.CostEstimate(flops=0, bytes_accessed=anom.size * 4, transcendentals=0),
        name="stage",
    )(*operands)


def gram_kernel(
    sizes,
    far,
    core,
    requests_ref,
    left_ref,
    rinv_ref,
    obs_lon_ref,
    obs_lat_ref,
    totals_ref,
    out_ref,
    acc_ref,
):
    patches, lat_patches, lon_patches, lat_devices, held, per_owner, grid_lon = sizes
    step = pl.program_id(0)
    me = requests_ref[0, per_owner + 1]
    distance = (2 * (step // 2) + core) * lat_devices + (2 * far + step % 2)
    target = me ^ distance
    lon_first = (target // lat_devices) * lon_patches
    lat_first = (target % lat_devices) * lat_patches
    members = left_ref.shape[2]
    acc_ref[...] = jnp.zeros_like(acc_ref)
    number = requests_ref[target, per_owner]

    products = []
    for entry in range(per_owner):
        code = requests_ref[target, entry]
        patch = code // held
        block = code % held
        centre_lon = (lon_first + patch // lat_patches) * (2 * PSIDE) + (PSIDE - 1)
        centre_lat = (lat_first + patch % lat_patches) * (2 * PSIDE) + (PSIDE - 1)
        row = pl.ds(block, 1)
        lon_gap = jnp.abs(2 * obs_lon_ref[row, :] - centre_lon)
        lon_gap = jnp.minimum(lon_gap, 2 * grid_lon - lon_gap)
        lat_gap = 2 * obs_lat_ref[row, :] - centre_lat
        square = (lon_gap * lon_gap + lat_gap * lat_gap).astype(F32)
        rinv = jnp.where(entry < number, rinv_ref[row, :], 0.0)
        weight = rinv * jnp.exp(square * (-1.0 / (8.0 * LOC_SCALE * LOC_SCALE)))
        left = left_ref[block]
        scaled = (left[:members].astype(F32) * weight).astype(BF16)
        product = lax.dot_general(left, scaled, NT, preferred_element_type=F32)
        products.append((patch, product[: members + 8]))
    for patch, product in products:
        acc_ref[patch] += product

    row = lax.broadcasted_iota(jnp.int32, (members, members), 0)
    column = lax.broadcasted_iota(jnp.int32, (members, members), 1)
    line = lax.broadcasted_iota(jnp.int32, (8, members), 0)
    for pair in range(patches // 2):
        first = acc_ref[2 * pair]
        second = acc_ref[2 * pair + 1]
        packed = jnp.where(row < column, first[:members], second[:members])
        out_ref[0, pair, :members, :] = packed.astype(BF16)
        rows = totals_ref[...]
        for place, values in ((0, first), (2, second)):
            diagonal = jnp.sum(
                jnp.where(row == column, values[:members], 0.0), axis=0, keepdims=True
            )
            projected = values[members : members + 1] + values[members + 1 : members + 2]
            rows = jnp.where(line == place, diagonal, rows)
            rows = jnp.where(line == place + 1, projected, rows)
        high = rows.astype(BF16).astype(F32)
        out_ref[0, pair, members:, :] = jnp.concatenate([high, rows - high], axis=0).astype(BF16)


def hold_kernel(table_hbm, held_ref, sem):
    copy = pltpu.make_async_copy(table_hbm, held_ref, sem)
    copy.start()
    copy.wait()


def hold(table):
    return pl.pallas_call(
        hold_kernel,
        out_shape=pltpu.SMEM(table.shape, table.dtype),
        in_specs=[pl.BlockSpec(memory_space=pl.ANY)],
        out_specs=pl.BlockSpec(memory_space=pltpu.SMEM),
        scratch_shapes=[pltpu.SemaphoreType.DMA(())],
        name="hold",
    )(table)


def partial_grams(sizes, far, core, count, requests, staged):
    patches, per_owner = sizes[0], sizes[5]
    members = staged[0].shape[2]
    rows = members + EXT
    block = (1, patches // 2, rows, members)
    return pl.pallas_call(
        functools.partial(gram_kernel, sizes, far, core),
        out_shape=jax.ShapeDtypeStruct((count, *block[1:]), BF16),
        grid_spec=pltpu.PrefetchScalarGridSpec(
            num_scalar_prefetch=0,
            grid=(count,),
            in_specs=[pl.BlockSpec(memory_space=pltpu.SMEM)] + [pl.BlockSpec(memory_space=pltpu.VMEM)] * 5,
            out_specs=pl.BlockSpec(block, lambda i, *_: (i, 0, 0, 0)),
            scratch_shapes=[pltpu.VMEM((patches, members + 8, members), F32)],
        ),
        compiler_params=pltpu.CompilerParams(vmem_limit_bytes=8 * 2**20),
        cost_estimate=pl.CostEstimate(
            flops=count * per_owner * 100 * members**3, bytes_accessed=0, transcendentals=0
        ),
        name="partial_grams",
    )(requests, *staged)


def added(left, right):
    members = left.shape[-1]
    total = left.astype(F32) + right.astype(F32)
    rows = total[:, members : members + 8] + total[:, members + 8 :]
    high = rows.astype(BF16).astype(F32)
    rows = jnp.concatenate([high, rows - high], axis=1)
    return total[:, :members].astype(BF16), rows.astype(BF16)


def add_kernel(count, plan, *refs):
    keep, got, outs = refs[:count], refs[count : 2 * count], refs[2 * count :]
    for part, index, low, high, out, place, at in plan:
        members = keep[part].shape[-1]
        body, rows = added(keep[part][index, low:high], got[part][index, low:high])
        to = slice(at, at + high - low)
        outs[out][place, to, :members, :] = body
        outs[out][place, to, members:, :] = rows


def add_all(keep, got, plan, shapes):
    count = len(keep)
    inner = keep[0].shape[2:]
    whole = pl.BlockSpec(memory_space=pltpu.VMEM)
    size = sum(v.size for v in keep)
    return pl.pallas_call(
        functools.partial(add_kernel, count, plan),
        out_shape=[jax.ShapeDtypeStruct((*shape, *inner), BF16) for shape in shapes],
        in_specs=[whole] * (2 * count),
        out_specs=[whole] * len(shapes),
        compiler_params=pltpu.CompilerParams(vmem_limit_bytes=8 * 2**20),
        cost_estimate=pl.CostEstimate(flops=size * 4, bytes_accessed=size * 6, transcendentals=0),
        name="add_partials",
    )(*keep, *got)


def product(left, right):
    left_high, left_low = left
    right_high, right_low = right
    return jnp.dot(
        jnp.concatenate([left_high, left_low, left_high], axis=1),
        jnp.concatenate([right_high, right_high, right_low], axis=0),
        preferred_element_type=F32,
    )


def solve_kernel(count, total_obs, *refs):
    parts, (out_ref,) = refs[:count], refs[count:]
    pairs, rows, members = parts[0].shape
    row = lax.broadcasted_iota(jnp.int32, (members, members), 0)
    column = lax.broadcasted_iota(jnp.int32, (members, members), 1)
    identity = (row == column).astype(F32)

    def gathered(pair):
        total = parts[0][pair].astype(F32)
        for part in parts[1:]:
            total = total + part[pair].astype(F32)
        return total[:members], total[members : members + 8] + total[members + 8 :]

    def some(step, _):
        systems, projected = [], []
        for pair in (2 * step, 2 * step + 1):
            packed, values = gathered(pair)
            flipped = packed.T
            innovation = jnp.sum(values[4:5], axis=1, keepdims=True)
            spread = jnp.sum(values[5:6], axis=1, keepdims=True)
            ridge = (members - 1) * (spread + total_obs) / innovation
            for place, full in (
                (0, jnp.where(row < column, packed, flipped)),
                (2, jnp.where(row > column, packed, flipped)),
            ):
                full = jnp.where(row == column, values[place : place + 1], full)
                systems.append(full + ridge * identity)
                projected.append(values[place + 1 : place + 2])
        scalings, roots, inverses = [], [], []
        for system in systems:
            squares = jnp.sum(system * system, axis=0, keepdims=True)
            scaling = jnp.sqrt(jnp.sum(squares, axis=1, keepdims=True))
            scalings.append(scaling)
            roots.append(system / scaling)
        factors = [1.5 * identity - 0.5 * root for root in roots]
        roots = [product(halves(f), halves(r)) for f, r in zip(factors, roots)]
        inverses = factors
        for iteration in range(1, NS_ITERS):
            split_roots = [halves(r) for r in roots]
            split_inverses = [halves(z) for z in inverses]
            factors = [
                halves(1.5 * identity - 0.5 * product(z, r))
                for z, r in zip(split_inverses, split_roots)
            ]
            if iteration < NS_ITERS - 1:
                both = [
                    product(f, [jnp.concatenate([a, b], axis=1) for a, b in zip(r, z)])
                    for f, r, z in zip(factors, split_roots, split_inverses)
                ]
                roots = [b[:, :members] for b in both]
                inverses = [b[:, members:] for b in both]
            else:
                inverses = [product(f, z) for f, z in zip(factors, split_inverses)]
        for i in range(4):
            inverse_sqrt = inverses[i] * lax.rsqrt(scalings[i])
            inner = jnp.sum(inverse_sqrt * projected[i], axis=1, keepdims=True)
            mean = jnp.sum(inverse_sqrt * inner, axis=0, keepdims=True)
            out_ref[4 * step + i] = (
                jnp.sqrt(F32(members - 1)) * inverse_sqrt + mean
            ).astype(BF16)
        return 0

    lax.fori_loop(0, pairs // 2, some, 0)


def solve(parts, total_obs):
    pairs, rows, members = parts[0].shape
    whole = pl.BlockSpec(memory_space=pltpu.VMEM)
    return pl.pallas_call(
        functools.partial(solve_kernel, len(parts), total_obs),
        out_shape=jax.ShapeDtypeStruct((2 * pairs, members, members), BF16),
        in_specs=[whole] * len(parts),
        out_specs=whole,
        compiler_params=pltpu.CompilerParams(vmem_limit_bytes=8 * 2**20),
        name="solve",
    )(*parts)


def analysis_kernel(weights_ref, pert_ref, mean_ref, out_ref):
    for field in range(pert_ref.shape[1]):
        change = jnp.dot(weights_ref[0], pert_ref[0, field], preferred_element_type=F32)
        out_ref[0, field] = change + mean_ref[0, field : field + 1]


def analysis(weights, pert, mean):
    patches, fields, members, columns = pert.shape
    return pl.pallas_call(
        analysis_kernel,
        out_shape=jax.ShapeDtypeStruct(pert.shape, F32),
        grid=(patches,),
        in_specs=[
            pl.BlockSpec((1, members, members), lambda i: (i, 0, 0)),
            pl.BlockSpec((1, fields, members, columns), lambda i: (i, 0, 0, 0)),
            pl.BlockSpec((1, fields, columns), lambda i: (i, 0, 0)),
        ],
        out_specs=pl.BlockSpec((1, fields, members, columns), lambda i: (i, 0, 0, 0)),
        compiler_params=pltpu.CompilerParams(vmem_limit_bytes=8 * 2**20),
        name="analysis",
    )(weights, pert, mean)


def swap(value, axis, flip):
    size = lax.axis_size(axis)
    return lax.ppermute(value, axis, [(i, i ^ flip) for i in range(size)])


def on_device(
    state_pert, state_mean, obs_anom, innov, obs_rinv, obs_lon, obs_lat, block_list, block_count
):
    lon_devices, lat_devices = lax.axis_size("lon"), lax.axis_size("lat")
    holders = lon_devices * lat_devices
    lon_patches, lat_patches, fields, members, columns = state_pert.shape
    patches = lon_patches * lat_patches
    length = block_list.shape[2]
    held, _, block_obs = obs_anom.shape
    per_owner = patches * length // holders
    table = request_table(
        block_list.reshape(patches, length), block_count.reshape(patches), holders, held
    )
    requests = lax.all_to_all(table, ("lon", "lat"), split_axis=0, concat_axis=0, tiled=True)

    me = lax.axis_index(("lon", "lat")).astype(jnp.int32)
    requests = jnp.concatenate([requests, jnp.full((holders, 1), me)], axis=1)
    requests, observed = lax.optimization_barrier(
        (requests, (obs_anom, innov, obs_rinv, obs_lon, obs_lat))
    )
    requests = hold(requests)
    staged = stage(*observed)
    sizes = (
        patches,
        lat_patches,
        lon_patches,
        lat_devices,
        held,
        per_owner,
        lon_devices * lon_patches * PSIDE,
    )
    y_count = lon_devices // 2
    pairs = patches // 2
    cut = pairs // 2

    def grams(far, core, after):
        rows, _ = lax.optimization_barrier((staged[-1], after))
        return partial_grams(sizes, far, core, lon_devices, requests, [*staged[:-1], rows])

    def steps(far):
        send = yield far, 1
        got = swap(send, "lon", 1)
        keep = yield [got], [send]
        left = y_count // 2
        plan = []
        for y in range(y_count):
            for near in range(2):
                plan.append((0, 2 * y + near, 0, cut, near, y, 0))
                far_y, place = divmod(y, left)
                plan.append((0, 2 * y + near, cut, pairs, 2 + far_y, 2 * place + near, 0))
        keep_a, send_a, keep_b, send_b = add_all(
            [keep[0]],
            [keep[1]],
            plan,
            [(y_count, cut)] * 2 + [(2 * left, pairs - cut)] * 2,
        )
        got_a, got_b = yield [swap(send_a, "lat", 1), swap(send_b, "lon", y_count)], [send_a, send_b]
        plan = []
        for y in range(y_count):
            far_y, place = divmod(y, left)
            plan.append((0, y, 0, cut, far_y, place, 0))
        for y in range(left):
            for near in range(2):
                plan.append((1, 2 * y + near, 0, pairs - cut, 2 + near, y, 0))
        keep_a, send_a, keep_b, send_b = add_all(
            [keep_a, keep_b],
            [got_a, got_b],
            plan,
            [(left, cut)] * 2 + [(left, pairs - cut)] * 2,
        )
        got_a, got_b = yield [swap(send_a, "lon", y_count), swap(send_b, "lat", 1)], [send_a, send_b]
        while left > 1:
            left //= 2
            plan = []
            for part in range(2):
                for y in range(2 * left):
                    far_y, place = divmod(y, left)
                    plan.append((part, y, 0, keep_a.shape[1] if part == 0 else pairs - cut, 2 * part + far_y, place, 0))
            keep_a, send_a, keep_b, send_b = add_all(
                [keep_a, keep_b],
                [got_a, got_b],
                plan,
                [(left, cut)] * 2 + [(left, pairs - cut)] * 2,
            )
            got_a, got_b = yield (
                [swap(send_a, "lon", 2 * left), swap(send_b, "lon", 2 * left)],
                [send_a, send_b],
            )
        plan = [(0, 0, 0, cut, 0, 0, 0), (1, 0, 0, pairs - cut, 0, 0, cut)]
        [total] = add_all([keep_a, keep_b], [got_a, got_b], plan, [(1, pairs)])
        if far:
            [total] = yield [swap(total, "lat", 2 * far)], [total]
        parts.append(total)

    parts, open_chunks, sent = [], [], []

    def advance(latest):
        nonlocal open_chunks, sent
        flat = [w for _, waits in open_chunks for w in waits]
        if latest is not None:
            latest, flat = lax.optimization_barrier((latest, flat))
        still, sent = [], []
        for chunk, waits in open_chunks:
            now, flat = flat[: len(waits)], flat[len(waits) :]
            if latest is not None and chunk is newest:
                now = [latest, *now]
            try:
                waits, sums = chunk.send(now)
                still.append((chunk, waits))
                sent += sums
            except StopIteration:
                pass
        open_chunks = still

    newest = None
    for far in reversed(range(lat_devices // 2)):
        chunk = steps(far)
        send = grams(*next(chunk), sent)
        advance(send)
        waits, sums = chunk.send(send)
        newest = chunk
        open_chunks.append((chunk, waits))
        keep = grams(far, 0, sent + sums)
        advance(keep)
        newest = None
    while open_chunks:
        advance(None)
    weights = solve([v[0] for v in parts], holders * held * block_obs)
    updated = analysis(
        weights,
        state_pert.reshape(patches, fields, members, columns),
        state_mean.reshape(patches, fields, columns),
    )
    return updated.reshape(lon_patches, lat_patches, fields, members, columns)


def solution(mesh):
    in_specs = (
        P("lon", "lat", None, None, None),
        P("lon", "lat", None, None),
        P(("lon", "lat"), None, None),
        P(("lon", "lat"), None),
        P(("lon", "lat"), None),
        P(("lon", "lat"), None),
        P(("lon", "lat"), None),
        P("lon", "lat", None),
        P("lon", "lat"),
    )
    out_specs = P("lon", "lat", None, None, None)
    return jax.shard_map(
        on_device, mesh=mesh, in_specs=in_specs, out_specs=out_specs, check_vma=False
    )
```

```python
import functools

import jax
import jax.numpy as jnp
from jax import lax
from jax.experimental import pallas as pl
from jax.experimental.pallas import tpu as pltpu
from jax.sharding import PartitionSpec as P

PSIDE = 16
NS_ITERS = 5
LOC_SCALE = 48.0
EXT = 16
F32 = jnp.float32
BF16 = jnp.bfloat16
NT = (((1,), (1,)), ((), ()))


def halves(value):
    high = value.astype(BF16)
    return high, (value - high.astype(F32)).astype(BF16)


def request_table(block_list, block_count, holders, held_blocks):
    patches, length = block_list.shape
    slots = patches * length
    per_owner = slots // holders
    wanted = block_list.reshape(slots)
    used = (lax.broadcasted_iota(jnp.int32, (patches, length), 1) < block_count[:, None]).reshape(
        slots
    )
    holder = jnp.where(used, wanted // held_blocks, holders)
    order = jnp.arange(slots)
    before = (holder[:, None] == holder[None, :]) & (order[None, :] < order[:, None])
    rank = jnp.sum(before.astype(jnp.int32), axis=1)
    code = (order // length) * held_blocks + wanted % held_blocks
    place = holder * per_owner + rank
    hit = (place[None, :] == jnp.arange(holders * per_owner)[:, None]) & used[None, :]
    table = jnp.sum(jnp.where(hit, code[None, :], 0), axis=1).reshape(holders, per_owner)
    number = jnp.sum((holder[None, :] == jnp.arange(holders)[:, None]).astype(jnp.int32), axis=1)
    return jnp.concatenate([table, number[:, None]], axis=1)


def stage_kernel(
    chunk,
    anom_hbm,
    innov_hbm,
    rinv_hbm,
    lon_hbm,
    lat_hbm,
    left_ref,
    rinv_ref,
    lon_ref,
    lat_ref,
    totals_ref,
    innov_ref,
    sems,
):
    held, members, block_obs = anom_hbm.shape
    pairs = [(rinv_hbm, rinv_ref), (innov_hbm, innov_ref)]
    for i in range(held // chunk):
        span = pl.ds(i * chunk, chunk)
        pairs.append((anom_hbm.at[span], left_ref.at[span, pl.ds(0, members), :]))
    pairs += [(lon_hbm, lon_ref), (lat_hbm, lat_ref)]
    copies = [pltpu.make_async_copy(a, b, sems.at[i]) for i, (a, b) in enumerate(pairs)]
    for copy in copies:
        copy.start()
    copies[0].wait()
    copies[1].wait()
    line = lax.broadcasted_iota(jnp.int32, (EXT, block_obs), 0)
    sums = jnp.zeros((8, block_obs), F32)
    for i, copy in enumerate(copies[2:-2]):
        copy.wait()

        def block(j, total, first=i * chunk):
            at = first + j
            values = left_ref[at, :members, :].astype(F32)
            squares = jnp.sum((values * values).reshape(members // 8, 8, block_obs), axis=0)
            innov = innov_ref[pl.ds(at, 1), :]
            high = innov.astype(BF16).astype(F32)
            rows = jnp.where(line == 0, high, jnp.where(line == 1, innov - high, 0.0))
            left_ref[at, members:, :] = rows.astype(BF16)
            return total + squares * rinv_ref[pl.ds(at, 1), :]

        sums = lax.fori_loop(0, chunk, block, sums, unroll=4)
    innovation = jnp.sum(rinv_ref[...] * innov_ref[...] * innov_ref[...], axis=0, keepdims=True)
    spread = jnp.sum(sums, axis=0, keepdims=True) / (members - 1)
    line = lax.broadcasted_iota(jnp.int32, (8, block_obs), 0)
    totals_ref[...] = jnp.where(line == 4, innovation, jnp.where(line == 5, spread, 0.0))
    copies[-2].wait()
    copies[-1].wait()


def stage(anom, innov, rinv, lon, lat):
    held, members, block_obs = anom.shape
    chunk = 16 if held % 16 == 0 else held
    operands = [pltpu.with_memory_space_constraint(v, pltpu.HBM) for v in (anom, innov, rinv, lon, lat)]
    return pl.pallas_call(
        functools.partial(stage_kernel, chunk),
        out_shape=[
            pltpu.VMEM((held, members + EXT, block_obs), BF16),
            pltpu.VMEM((held, block_obs), F32),
            pltpu.VMEM((held, block_obs), jnp.int32),
            pltpu.VMEM((held, block_obs), jnp.int32),
            pltpu.VMEM((8, block_obs), F32),
        ],
        in_specs=[pl.BlockSpec(memory_space=pltpu.HBM)] * 5,
        out_specs=[pl.BlockSpec(memory_space=pltpu.VMEM)] * 5,
        scratch_shapes=[
            pltpu.VMEM((held, block_obs), F32),
            pltpu.SemaphoreType.DMA((held // chunk + 4,)),
        ],
        compiler_params=pltpu.CompilerParams(vmem_limit_bytes=4 * 2**20),
        cost_estimate=pl.CostEstimate(flops=0, bytes_accessed=anom.size * 4, transcendentals=0),
        name="stage",
    )(*operands)


def gram_kernel(
    sizes,
    far,
    core,
    requests_ref,
    left_ref,
    rinv_ref,
    obs_lon_ref,
    obs_lat_ref,
    totals_ref,
    out_ref,
    acc_ref,
):
    patches, lat_patches, lon_patches, lat_devices, held, per_owner, grid_lon = sizes
    step = pl.program_id(0)
    me = requests_ref[0, per_owner + 1]
    distance = (2 * (step // 2) + core) * lat_devices + (2 * far + step % 2)
    target = me ^ distance
    lon_first = (target // lat_devices) * lon_patches
    lat_first = (target % lat_devices) * lat_patches
    members = left_ref.shape[2]
    acc_ref[...] = jnp.zeros_like(acc_ref)
    number = requests_ref[target, per_owner]

    products = []
    for entry in range(per_owner):
        code = requests_ref[target, entry]
        patch = code // held
        block = code % held
        centre_lon = (lon_first + patch // lat_patches) * (2 * PSIDE) + (PSIDE - 1)
        centre_lat = (lat_first + patch % lat_patches) * (2 * PSIDE) + (PSIDE - 1)
        row = pl.ds(block, 1)
        lon_gap = jnp.abs(2 * obs_lon_ref[row, :] - centre_lon)
        lon_gap = jnp.minimum(lon_gap, 2 * grid_lon - lon_gap)
        lat_gap = 2 * obs_lat_ref[row, :] - centre_lat
        square = (lon_gap * lon_gap + lat_gap * lat_gap).astype(F32)
        rinv = jnp.where(entry < number, rinv_ref[row, :], 0.0)
        weight = rinv * jnp.exp(square * (-1.0 / (8.0 * LOC_SCALE * LOC_SCALE)))
        left = left_ref[block]
        scaled = (left[:members].astype(F32) * weight).astype(BF16)
        product = lax.dot_general(left, scaled, NT, preferred_element_type=F32)
        products.append((patch, product[: members + 8]))
    for patch, product in products:
        acc_ref[patch] += product

    row = lax.broadcasted_iota(jnp.int32, (members, members), 0)
    column = lax.broadcasted_iota(jnp.int32, (members, members), 1)
    line = lax.broadcasted_iota(jnp.int32, (8, members), 0)
    for pair in range(patches // 2):
        first = acc_ref[2 * pair]
        second = acc_ref[2 * pair + 1]
        packed = jnp.where(row < column, first[:members], second[:members])
        out_ref[0, pair, :members, :] = packed.astype(BF16)
        rows = totals_ref[...]
        for place, values in ((0, first), (2, second)):
            diagonal = jnp.sum(
                jnp.where(row == column, values[:members], 0.0), axis=0, keepdims=True
            )
            projected = values[members : members + 1] + values[members + 1 : members + 2]
            rows = jnp.where(line == place, diagonal, rows)
            rows = jnp.where(line == place + 1, projected, rows)
        high = rows.astype(BF16).astype(F32)
        out_ref[0, pair, members:, :] = jnp.concatenate([high, rows - high], axis=0).astype(BF16)


def hold_kernel(table_hbm, held_ref, sem):
    copy = pltpu.make_async_copy(table_hbm, held_ref, sem)
    copy.start()
    copy.wait()


def hold(table):
    return pl.pallas_call(
        hold_kernel,
        out_shape=pltpu.SMEM(table.shape, table.dtype),
        in_specs=[pl.BlockSpec(memory_space=pl.ANY)],
        out_specs=pl.BlockSpec(memory_space=pltpu.SMEM),
        scratch_shapes=[pltpu.SemaphoreType.DMA(())],
        name="hold",
    )(table)


def partial_grams(sizes, far, core, count, requests, staged):
    patches, per_owner = sizes[0], sizes[5]
    members = staged[0].shape[2]
    rows = members + EXT
    block = (1, patches // 2, rows, members)
    return pl.pallas_call(
        functools.partial(gram_kernel, sizes, far, core),
        out_shape=jax.ShapeDtypeStruct((count, *block[1:]), BF16),
        grid_spec=pltpu.PrefetchScalarGridSpec(
            num_scalar_prefetch=0,
            grid=(count,),
            in_specs=[pl.BlockSpec(memory_space=pltpu.SMEM)] + [pl.BlockSpec(memory_space=pltpu.VMEM)] * 5,
            out_specs=pl.BlockSpec(block, lambda i, *_: (i, 0, 0, 0)),
            scratch_shapes=[pltpu.VMEM((patches, members + 8, members), F32)],
        ),
        compiler_params=pltpu.CompilerParams(vmem_limit_bytes=8 * 2**20),
        cost_estimate=pl.CostEstimate(
            flops=count * per_owner * 100 * members**3, bytes_accessed=0, transcendentals=0
        ),
        name="partial_grams",
    )(requests, *staged)


def added(left, right):
    members = left.shape[-1]
    total = left.astype(F32) + right.astype(F32)
    rows = total[:, members : members + 8] + total[:, members + 8 :]
    high = rows.astype(BF16).astype(F32)
    rows = jnp.concatenate([high, rows - high], axis=1)
    return total[:, :members].astype(BF16), rows.astype(BF16)


def add_kernel(count, plan, *refs):
    keep, got, outs = refs[:count], refs[count : 2 * count], refs[2 * count :]
    for part, index, low, high, out, place, at in plan:
        members = keep[part].shape[-1]
        body, rows = added(keep[part][index, low:high], got[part][index, low:high])
        to = slice(at, at + high - low)
        outs[out][place, to, :members, :] = body
        outs[out][place, to, members:, :] = rows


def add_all(keep, got, plan, shapes):
    count = len(keep)
    inner = keep[0].shape[2:]
    whole = pl.BlockSpec(memory_space=pltpu.VMEM)
    size = sum(v.size for v in keep)
    return pl.pallas_call(
        functools.partial(add_kernel, count, plan),
        out_shape=[jax.ShapeDtypeStruct((*shape, *inner), BF16) for shape in shapes],
        in_specs=[whole] * (2 * count),
        out_specs=[whole] * len(shapes),
        compiler_params=pltpu.CompilerParams(vmem_limit_bytes=8 * 2**20),
        cost_estimate=pl.CostEstimate(flops=size * 4, bytes_accessed=size * 6, transcendentals=0),
        name="add_partials",
    )(*keep, *got)


def product(left, right):
    left_high, left_low = left
    right_high, right_low = right
    return jnp.dot(
        jnp.concatenate([left_high, left_low, left_high], axis=1),
        jnp.concatenate([right_high, right_high, right_low], axis=0),
        preferred_element_type=F32,
    )


def solve_group(parts, total_obs, first, count):
    members = parts[0].shape[-1]
    row = lax.broadcasted_iota(jnp.int32, (members, members), 0)
    column = lax.broadcasted_iota(jnp.int32, (members, members), 1)
    identity = (row == column).astype(F32)
    systems, projected = [], []
    for pair in range(count):
        total = parts[0][0, first + pair].astype(F32)
        for part in parts[1:]:
            total = total + part[0, first + pair].astype(F32)
        packed = total[:members]
        values = total[members : members + 8] + total[members + 8 :]
        flipped = packed.T
        innovation = jnp.sum(values[4:5], axis=1, keepdims=True)
        spread = jnp.sum(values[5:6], axis=1, keepdims=True)
        ridge = (members - 1) * (spread + total_obs) / innovation
        for place, full in (
            (0, jnp.where(row < column, packed, flipped)),
            (2, jnp.where(row > column, packed, flipped)),
        ):
            systems.append(jnp.where(row == column, values[place : place + 1] + ridge, full))
            projected.append(values[place + 1 : place + 2])
    scalings, roots = [], []
    for system in systems:
        squares = jnp.sum(system * system, axis=0, keepdims=True)
        scaling = jnp.sqrt(jnp.sum(squares, axis=1, keepdims=True))
        scalings.append(scaling)
        roots.append(system * (1.0 / scaling))
    factors = [1.5 * identity - 0.5 * root for root in roots]
    roots = [product(halves(f), halves(r)) for f, r in zip(factors, roots)]
    inverses = factors
    for iteration in range(1, NS_ITERS):
        split_roots = [halves(r) for r in roots]
        split_inverses = [halves(z) for z in inverses]
        factors = [
            halves(1.5 * identity - 0.5 * product(z, r))
            for z, r in zip(split_inverses, split_roots)
        ]
        if iteration < NS_ITERS - 1:
            both = [
                product(f, [jnp.concatenate([a, b], axis=1) for a, b in zip(r, z)])
                for f, r, z in zip(factors, split_roots, split_inverses)
            ]
            roots = [b[:, :members] for b in both]
            inverses = [b[:, members:] for b in both]
        else:
            inverses = [product(f, z) for f, z in zip(factors, split_inverses)]
    weights = []
    for scaling, inverse, values in zip(scalings, inverses, projected):
        inverse_sqrt = inverse * lax.rsqrt(scaling)
        inner = jnp.sum(inverse_sqrt * values, axis=1, keepdims=True)
        mean = jnp.sum(inverse_sqrt * inner, axis=0, keepdims=True)
        weights.append((jnp.sqrt(F32(members - 1)) * inverse_sqrt + mean).astype(BF16))
    return weights


def analysis_kernel(count, total_obs, group, *refs):
    parts, (pert_ref, mean_ref, out_ref, weights_ref) = refs[:count], refs[count:]
    step = pl.program_id(0)
    size, fields = pert_ref.shape[:2]
    now, before = lax.rem(step, 2), lax.rem(step + 1, 2)
    for patch in range(size):
        held = weights_ref[before, patch]
        for field in range(fields):
            change = jnp.dot(held, pert_ref[patch, field], preferred_element_type=F32)
            out_ref[patch, field] = change + mean_ref[patch, field : field + 1]
    groups = pl.num_programs(0) - 1
    first = jnp.minimum(step, groups - 1) * (group // 2)
    for patch, weights in enumerate(solve_group(parts, total_obs, first, group // 2)):
        weights_ref[now, patch] = weights


def analysis(parts, total_obs, pert, mean):
    patches, fields, members, columns = pert.shape
    group = patches // 2
    whole = pl.BlockSpec(memory_space=pltpu.VMEM)
    return pl.pallas_call(
        functools.partial(analysis_kernel, len(parts), total_obs, group),
        out_shape=jax.ShapeDtypeStruct(pert.shape, F32),
        grid=(patches // group + 1,),
        in_specs=[whole] * len(parts)
        + [
            pl.BlockSpec(
                (group, fields, members, columns), lambda i: (jnp.maximum(i - 1, 0), 0, 0, 0)
            ),
            pl.BlockSpec((group, fields, columns), lambda i: (jnp.maximum(i - 1, 0), 0, 0)),
        ],
        out_specs=pl.BlockSpec(
            (group, fields, members, columns), lambda i: (jnp.maximum(i - 1, 0), 0, 0, 0)
        ),
        scratch_shapes=[pltpu.VMEM((2, group, members, members), BF16)],
        compiler_params=pltpu.CompilerParams(vmem_limit_bytes=40 * 2**20),
        name="analysis",
    )(*parts, pert, mean)


def swap(value, axis, flip):
    size = lax.axis_size(axis)
    return lax.ppermute(value, axis, [(i, i ^ flip) for i in range(size)])


def on_device(
    state_pert, state_mean, obs_anom, innov, obs_rinv, obs_lon, obs_lat, block_list, block_count
):
    lon_devices, lat_devices = lax.axis_size("lon"), lax.axis_size("lat")
    holders = lon_devices * lat_devices
    lon_patches, lat_patches, fields, members, columns = state_pert.shape
    patches = lon_patches * lat_patches
    length = block_list.shape[2]
    held, _, block_obs = obs_anom.shape
    per_owner = patches * length // holders
    table = request_table(
        block_list.reshape(patches, length), block_count.reshape(patches), holders, held
    )
    requests = lax.all_to_all(table, ("lon", "lat"), split_axis=0, concat_axis=0, tiled=True)

    me = lax.axis_index(("lon", "lat")).astype(jnp.int32)
    requests = jnp.concatenate([requests, jnp.full((holders, 1), me)], axis=1)
    requests, observed = lax.optimization_barrier(
        (requests, (obs_anom, innov, obs_rinv, obs_lon, obs_lat))
    )
    requests = hold(requests)
    staged = stage(*observed)
    sizes = (
        patches,
        lat_patches,
        lon_patches,
        lat_devices,
        held,
        per_owner,
        lon_devices * lon_patches * PSIDE,
    )
    y_count = lon_devices // 2
    pairs = patches // 2
    cut = pairs // 2

    def grams(far, core, after):
        rows, _ = lax.optimization_barrier((staged[-1], after))
        return partial_grams(sizes, far, core, lon_devices, requests, [*staged[:-1], rows])

    def steps(far):
        send = yield far, 1
        got = swap(send, "lon", 1)
        keep = yield [got], [send]
        left = y_count // 2
        plan = []
        for y in range(y_count):
            for near in range(2):
                plan.append((0, 2 * y + near, 0, cut, near, y, 0))
                far_y, place = divmod(y, left)
                plan.append((0, 2 * y + near, cut, pairs, 2 + far_y, 2 * place + near, 0))
        keep_a, send_a, keep_b, send_b = add_all(
            [keep[0]],
            [keep[1]],
            plan,
            [(y_count, cut)] * 2 + [(2 * left, pairs - cut)] * 2,
        )
        got_a, got_b = yield [swap(send_a, "lat", 1), swap(send_b, "lon", y_count)], [send_a, send_b]
        plan = []
        for y in range(y_count):
            far_y, place = divmod(y, left)
            plan.append((0, y, 0, cut, far_y, place, 0))
        for y in range(left):
            for near in range(2):
                plan.append((1, 2 * y + near, 0, pairs - cut, 2 + near, y, 0))
        keep_a, send_a, keep_b, send_b = add_all(
            [keep_a, keep_b],
            [got_a, got_b],
            plan,
            [(left, cut)] * 2 + [(left, pairs - cut)] * 2,
        )
        got_a, got_b = yield [swap(send_a, "lon", y_count), swap(send_b, "lat", 1)], [send_a, send_b]
        while left > 1:
            left //= 2
            plan = []
            for part in range(2):
                for y in range(2 * left):
                    far_y, place = divmod(y, left)
                    plan.append((part, y, 0, keep_a.shape[1] if part == 0 else pairs - cut, 2 * part + far_y, place, 0))
            keep_a, send_a, keep_b, send_b = add_all(
                [keep_a, keep_b],
                [got_a, got_b],
                plan,
                [(left, cut)] * 2 + [(left, pairs - cut)] * 2,
            )
            got_a, got_b = yield (
                [swap(send_a, "lon", 2 * left), swap(send_b, "lon", 2 * left)],
                [send_a, send_b],
            )
        plan = [(0, 0, 0, cut, 0, 0, 0), (1, 0, 0, pairs - cut, 0, 0, cut)]
        [total] = add_all([keep_a, keep_b], [got_a, got_b], plan, [(1, pairs)])
        if far:
            [total] = yield [swap(total, "lat", 2 * far)], [total]
        parts.append(total)

    parts, open_chunks, sent = [], [], []

    def advance(latest):
        nonlocal open_chunks, sent
        flat = [w for _, waits in open_chunks for w in waits]
        if latest is not None:
            latest, flat = lax.optimization_barrier((latest, flat))
        still, sent = [], []
        for chunk, waits in open_chunks:
            now, flat = flat[: len(waits)], flat[len(waits) :]
            if latest is not None and chunk is newest:
                now = [latest, *now]
            try:
                waits, sums = chunk.send(now)
                still.append((chunk, waits))
                sent += sums
            except StopIteration:
                pass
        open_chunks = still

    newest = None
    for far in reversed(range(lat_devices // 2)):
        chunk = steps(far)
        send = grams(*next(chunk), sent)
        waits, sums = chunk.send(send)
        newest = chunk
        open_chunks.append((chunk, waits))
        keep = grams(far, 0, sums)
        advance(keep)
        newest = None
    while open_chunks:
        advance(None)
    updated = analysis(
        parts,
        holders * held * block_obs,
        state_pert.reshape(patches, fields, members, columns),
        state_mean.reshape(patches, fields, columns),
    )
    return updated.reshape(lon_patches, lat_patches, fields, members, columns)


def solution(mesh):
    in_specs = (
        P("lon", "lat", None, None, None),
        P("lon", "lat", None, None),
        P(("lon", "lat"), None, None),
        P(("lon", "lat"), None),
        P(("lon", "lat"), None),
        P(("lon", "lat"), None),
        P(("lon", "lat"), None),
        P("lon", "lat", None),
        P("lon", "lat"),
    )
    out_specs = P("lon", "lat", None, None, None)
    return jax.shard_map(
        on_device, mesh=mesh, in_specs=in_specs, out_specs=out_specs, check_vma=False
    )
```

```python
import functools

import jax
import jax.numpy as jnp
from jax import lax
from jax.experimental import pallas as pl
from jax.experimental.pallas import tpu as pltpu
from jax.sharding import PartitionSpec as P

PSIDE = 16
NS_ITERS = 5
LOC_SCALE = 48.0
EXT = 16
F32 = jnp.float32
BF16 = jnp.bfloat16
NT = (((1,), (1,)), ((), ()))


def halves(value):
    high = value.astype(BF16)
    return high, (value - high.astype(F32)).astype(BF16)


def request_table(block_list, block_count, holders, held_blocks):
    patches, length = block_list.shape
    slots = patches * length
    per_owner = slots // holders
    wanted = block_list.reshape(slots)
    used = (lax.broadcasted_iota(jnp.int32, (patches, length), 1) < block_count[:, None]).reshape(
        slots
    )
    holder = jnp.where(used, wanted // held_blocks, holders)
    order = jnp.arange(slots)
    before = (holder[:, None] == holder[None, :]) & (order[None, :] < order[:, None])
    rank = jnp.sum(before.astype(jnp.int32), axis=1)
    code = (order // length) * held_blocks + wanted % held_blocks
    place = holder * per_owner + rank
    hit = (place[None, :] == jnp.arange(holders * per_owner)[:, None]) & used[None, :]
    table = jnp.sum(jnp.where(hit, code[None, :], 0), axis=1).reshape(holders, per_owner)
    number = jnp.sum((holder[None, :] == jnp.arange(holders)[:, None]).astype(jnp.int32), axis=1)
    return jnp.concatenate([table, number[:, None]], axis=1)


def stage_kernel(
    chunk,
    anom_hbm,
    innov_hbm,
    rinv_hbm,
    lon_hbm,
    lat_hbm,
    left_ref,
    rinv_ref,
    lon_ref,
    lat_ref,
    totals_ref,
    innov_ref,
    sems,
):
    held, members, block_obs = anom_hbm.shape
    pairs = [(rinv_hbm, rinv_ref), (innov_hbm, innov_ref)]
    for i in range(held // chunk):
        span = pl.ds(i * chunk, chunk)
        pairs.append((anom_hbm.at[span], left_ref.at[span, pl.ds(0, members), :]))
    pairs += [(lon_hbm, lon_ref), (lat_hbm, lat_ref)]
    copies = [pltpu.make_async_copy(a, b, sems.at[i]) for i, (a, b) in enumerate(pairs)]
    for copy in copies:
        copy.start()
    copies[0].wait()
    copies[1].wait()
    line = lax.broadcasted_iota(jnp.int32, (EXT, block_obs), 0)
    sums = jnp.zeros((8, block_obs), F32)
    for i, copy in enumerate(copies[2:-2]):
        copy.wait()

        def block(j, total, first=i * chunk):
            at = first + j
            values = left_ref[at, :members, :].astype(F32)
            squares = jnp.sum((values * values).reshape(members // 8, 8, block_obs), axis=0)
            innov = innov_ref[pl.ds(at, 1), :]
            high = innov.astype(BF16).astype(F32)
            rows = jnp.where(line == 0, high, jnp.where(line == 1, innov - high, 0.0))
            left_ref[at, members:, :] = rows.astype(BF16)
            return total + squares * rinv_ref[pl.ds(at, 1), :]

        sums = lax.fori_loop(0, chunk, block, sums, unroll=4)
    innovation = jnp.sum(rinv_ref[...] * innov_ref[...] * innov_ref[...], axis=0, keepdims=True)
    spread = jnp.sum(sums, axis=0, keepdims=True) / (members - 1)
    line = lax.broadcasted_iota(jnp.int32, (8, block_obs), 0)
    totals_ref[...] = jnp.where(line == 4, innovation, jnp.where(line == 5, spread, 0.0))
    copies[-2].wait()
    copies[-1].wait()


def stage(anom, innov, rinv, lon, lat):
    held, members, block_obs = anom.shape
    chunk = 16 if held % 16 == 0 else held
    operands = [pltpu.with_memory_space_constraint(v, pltpu.HBM) for v in (anom, innov, rinv, lon, lat)]
    return pl.pallas_call(
        functools.partial(stage_kernel, chunk),
        out_shape=[
            pltpu.VMEM((held, members + EXT, block_obs), BF16),
            pltpu.VMEM((held, block_obs), F32),
            pltpu.VMEM((held, block_obs), jnp.int32),
            pltpu.VMEM((held, block_obs), jnp.int32),
            pltpu.VMEM((8, block_obs), F32),
        ],
        in_specs=[pl.BlockSpec(memory_space=pltpu.HBM)] * 5,
        out_specs=[pl.BlockSpec(memory_space=pltpu.VMEM)] * 5,
        scratch_shapes=[
            pltpu.VMEM((held, block_obs), F32),
            pltpu.SemaphoreType.DMA((held // chunk + 4,)),
        ],
        compiler_params=pltpu.CompilerParams(vmem_limit_bytes=4 * 2**20),
        cost_estimate=pl.CostEstimate(flops=0, bytes_accessed=anom.size * 4, transcendentals=0),
        name="stage",
    )(*operands)


def gram_kernel(
    sizes,
    far,
    core,
    requests_ref,
    left_ref,
    rinv_ref,
    obs_lon_ref,
    obs_lat_ref,
    totals_ref,
    out_ref,
    acc_ref,
):
    patches, lat_patches, lon_patches, lat_devices, held, per_owner, grid_lon = sizes
    step = pl.program_id(0)
    me = requests_ref[0, per_owner + 1]
    distance = (2 * (step // 2) + core) * lat_devices + (2 * far + step % 2)
    target = me ^ distance
    lon_first = (target // lat_devices) * lon_patches
    lat_first = (target % lat_devices) * lat_patches
    members = left_ref.shape[2]
    acc_ref[...] = jnp.zeros_like(acc_ref)
    number = requests_ref[target, per_owner]

    products = []
    for entry in range(per_owner):
        code = requests_ref[target, entry]
        patch = code // held
        block = code % held
        centre_lon = (lon_first + patch // lat_patches) * (2 * PSIDE) + (PSIDE - 1)
        centre_lat = (lat_first + patch % lat_patches) * (2 * PSIDE) + (PSIDE - 1)
        row = pl.ds(block, 1)
        lon_gap = jnp.abs(2 * obs_lon_ref[row, :] - centre_lon)
        lon_gap = jnp.minimum(lon_gap, 2 * grid_lon - lon_gap)
        lat_gap = 2 * obs_lat_ref[row, :] - centre_lat
        square = (lon_gap * lon_gap + lat_gap * lat_gap).astype(F32)
        rinv = jnp.where(entry < number, rinv_ref[row, :], 0.0)
        weight = rinv * jnp.exp(square * (-1.0 / (8.0 * LOC_SCALE * LOC_SCALE)))
        left = left_ref[block]
        scaled = (left[:members].astype(F32) * weight).astype(BF16)
        product = lax.dot_general(left, scaled, NT, preferred_element_type=F32)
        products.append((patch, product[: members + 8]))
    for patch, product in products:
        acc_ref[patch] += product

    row = lax.broadcasted_iota(jnp.int32, (members, members), 0)
    column = lax.broadcasted_iota(jnp.int32, (members, members), 1)
    line = lax.broadcasted_iota(jnp.int32, (8, members), 0)
    for pair in range(patches // 2):
        first = acc_ref[2 * pair]
        second = acc_ref[2 * pair + 1]
        packed = jnp.where(row < column, first[:members], second[:members])
        out_ref[0, pair, :members, :] = packed.astype(BF16)
        rows = totals_ref[...]
        for place, values in ((0, first), (2, second)):
            diagonal = jnp.sum(
                jnp.where(row == column, values[:members], 0.0), axis=0, keepdims=True
            )
            projected = values[members : members + 1] + values[members + 1 : members + 2]
            rows = jnp.where(line == place, diagonal, rows)
            rows = jnp.where(line == place + 1, projected, rows)
        high = rows.astype(BF16).astype(F32)
        out_ref[0, pair, members:, :] = jnp.concatenate([high, rows - high], axis=0).astype(BF16)


def hold_kernel(table_hbm, held_ref, sem):
    copy = pltpu.make_async_copy(table_hbm, held_ref, sem)
    copy.start()
    copy.wait()


def hold(table):
    return pl.pallas_call(
        hold_kernel,
        out_shape=pltpu.SMEM(table.shape, table.dtype),
        in_specs=[pl.BlockSpec(memory_space=pl.ANY)],
        out_specs=pl.BlockSpec(memory_space=pltpu.SMEM),
        scratch_shapes=[pltpu.SemaphoreType.DMA(())],
        name="hold",
    )(table)


def partial_grams(sizes, far, core, count, requests, staged):
    patches, per_owner = sizes[0], sizes[5]
    members = staged[0].shape[2]
    rows = members + EXT
    block = (1, patches // 2, rows, members)
    return pl.pallas_call(
        functools.partial(gram_kernel, sizes, far, core),
        out_shape=jax.ShapeDtypeStruct((count, *block[1:]), BF16),
        grid_spec=pltpu.PrefetchScalarGridSpec(
            num_scalar_prefetch=0,
            grid=(count,),
            in_specs=[pl.BlockSpec(memory_space=pltpu.SMEM)] + [pl.BlockSpec(memory_space=pltpu.VMEM)] * 5,
            out_specs=pl.BlockSpec(block, lambda i, *_: (i, 0, 0, 0)),
            scratch_shapes=[pltpu.VMEM((patches, members + 8, members), F32)],
        ),
        compiler_params=pltpu.CompilerParams(vmem_limit_bytes=8 * 2**20),
        cost_estimate=pl.CostEstimate(
            flops=count * per_owner * 100 * members**3, bytes_accessed=0, transcendentals=0
        ),
        name="partial_grams",
    )(requests, *staged)


def added(left, right):
    members = left.shape[-1]
    total = left.astype(F32) + right.astype(F32)
    rows = total[:, members : members + 8] + total[:, members + 8 :]
    high = rows.astype(BF16).astype(F32)
    rows = jnp.concatenate([high, rows - high], axis=1)
    return total[:, :members].astype(BF16), rows.astype(BF16)


def add_kernel(inputs, size, jobs, *refs):
    for left, left_row, right, right_row, at, out, row, place in jobs:
        out_ref = refs[inputs + out]
        members = out_ref.shape[-1]
        span, to = slice(at, at + size), slice(place, place + size)
        body, rows = added(refs[left][left_row, span], refs[right][right_row, span])
        out_ref[row, to, :members, :] = body
        out_ref[row, to, members:, :] = rows


def add_all(arrays, size, jobs, shapes):
    inner = arrays[0].shape[2:]
    whole = pl.BlockSpec(memory_space=pltpu.VMEM)
    work = len(jobs) * size * inner[0] * inner[1]
    return pl.pallas_call(
        functools.partial(add_kernel, len(arrays), size, jobs),
        out_shape=[jax.ShapeDtypeStruct((*shape, *inner), BF16) for shape in shapes],
        in_specs=[whole] * len(arrays),
        out_specs=[whole] * len(shapes),
        compiler_params=pltpu.CompilerParams(vmem_limit_bytes=8 * 2**20),
        cost_estimate=pl.CostEstimate(flops=work * 4, bytes_accessed=work * 6, transcendentals=0),
        name="add_partials",
    )(*arrays)


def product(left, right):
    left_high, left_low = left
    right_high, right_low = right
    return jnp.dot(
        jnp.concatenate([left_high, left_low, left_high], axis=1),
        jnp.concatenate([right_high, right_high, right_low], axis=0),
        preferred_element_type=F32,
    )


def solve_group(parts, total_obs, first, count):
    members = parts[0].shape[-1]
    row = lax.broadcasted_iota(jnp.int32, (members, members), 0)
    column = lax.broadcasted_iota(jnp.int32, (members, members), 1)
    identity = (row == column).astype(F32)
    systems, projected = [], []
    for pair in range(count):
        total = parts[0][0, first + pair].astype(F32)
        for part in parts[1:]:
            total = total + part[0, first + pair].astype(F32)
        packed = total[:members]
        values = total[members : members + 8] + total[members + 8 :]
        flipped = packed.T
        innovation = jnp.sum(values[4:5], axis=1, keepdims=True)
        spread = jnp.sum(values[5:6], axis=1, keepdims=True)
        ridge = (members - 1) * (spread + total_obs) / innovation
        for place, full in (
            (0, jnp.where(row < column, packed, flipped)),
            (2, jnp.where(row > column, packed, flipped)),
        ):
            systems.append(jnp.where(row == column, values[place : place + 1] + ridge, full))
            projected.append(values[place + 1 : place + 2])
    scalings, roots = [], []
    for system in systems:
        squares = jnp.sum(system * system, axis=0, keepdims=True)
        scaling = jnp.sqrt(jnp.sum(squares, axis=1, keepdims=True))
        scalings.append(scaling)
        roots.append(system * (1.0 / scaling))
    factors = [1.5 * identity - 0.5 * root for root in roots]
    roots = [product(halves(f), halves(r)) for f, r in zip(factors, roots)]
    inverses = factors
    for iteration in range(1, NS_ITERS):
        split_roots = [halves(r) for r in roots]
        split_inverses = [halves(z) for z in inverses]
        factors = [
            halves(1.5 * identity - 0.5 * product(z, r))
            for z, r in zip(split_inverses, split_roots)
        ]
        if iteration < NS_ITERS - 1:
            both = [
                product(f, [jnp.concatenate([a, b], axis=1) for a, b in zip(r, z)])
                for f, r, z in zip(factors, split_roots, split_inverses)
            ]
            roots = [b[:, :members] for b in both]
            inverses = [b[:, members:] for b in both]
        else:
            inverses = [product(f, z) for f, z in zip(factors, split_inverses)]
    weights = []
    for scaling, inverse, values in zip(scalings, inverses, projected):
        inverse_sqrt = inverse * lax.rsqrt(scaling)
        inner = jnp.sum(inverse_sqrt * values, axis=1, keepdims=True)
        mean = jnp.sum(inverse_sqrt * inner, axis=0, keepdims=True)
        weights.append((jnp.sqrt(F32(members - 1)) * inverse_sqrt + mean).astype(BF16))
    return weights


def analysis_kernel(count, total_obs, group, *refs):
    parts, (pert_ref, mean_ref, out_ref, weights_ref) = refs[:count], refs[count:]
    step = pl.program_id(0)
    size, fields = pert_ref.shape[:2]
    now, before = lax.rem(step, 2), lax.rem(step + 1, 2)
    for patch in range(size):
        held = weights_ref[before, patch]
        for field in range(fields):
            change = jnp.dot(held, pert_ref[patch, field], preferred_element_type=F32)
            out_ref[patch, field] = change + mean_ref[patch, field : field + 1]
    groups = pl.num_programs(0) - 1
    first = jnp.minimum(step, groups - 1) * (group // 2)
    for patch, weights in enumerate(solve_group(parts, total_obs, first, group // 2)):
        weights_ref[now, patch] = weights


def analysis(parts, total_obs, pert, mean):
    patches, fields, members, columns = pert.shape
    group = patches // 2
    whole = pl.BlockSpec(memory_space=pltpu.VMEM)
    return pl.pallas_call(
        functools.partial(analysis_kernel, len(parts), total_obs, group),
        out_shape=jax.ShapeDtypeStruct(pert.shape, F32),
        grid=(patches // group + 1,),
        in_specs=[whole] * len(parts)
        + [
            pl.BlockSpec(
                (group, fields, members, columns), lambda i: (jnp.maximum(i - 1, 0), 0, 0, 0)
            ),
            pl.BlockSpec((group, fields, columns), lambda i: (jnp.maximum(i - 1, 0), 0, 0)),
        ],
        out_specs=pl.BlockSpec(
            (group, fields, members, columns), lambda i: (jnp.maximum(i - 1, 0), 0, 0, 0)
        ),
        scratch_shapes=[pltpu.VMEM((2, group, members, members), BF16)],
        compiler_params=pltpu.CompilerParams(vmem_limit_bytes=40 * 2**20),
        name="analysis",
    )(*parts, pert, mean)


def swap(value, axis, flip):
    size = lax.axis_size(axis)
    return lax.ppermute(value, axis, [(i, i ^ flip) for i in range(size)])


def on_device(
    state_pert, state_mean, obs_anom, innov, obs_rinv, obs_lon, obs_lat, block_list, block_count
):
    lon_devices, lat_devices = lax.axis_size("lon"), lax.axis_size("lat")
    holders = lon_devices * lat_devices
    lon_patches, lat_patches, fields, members, columns = state_pert.shape
    patches = lon_patches * lat_patches
    length = block_list.shape[2]
    held, _, block_obs = obs_anom.shape
    per_owner = patches * length // holders
    table = request_table(
        block_list.reshape(patches, length), block_count.reshape(patches), holders, held
    )
    requests = lax.all_to_all(table, ("lon", "lat"), split_axis=0, concat_axis=0, tiled=True)

    me = lax.axis_index(("lon", "lat")).astype(jnp.int32)
    requests = jnp.concatenate([requests, jnp.full((holders, 1), me)], axis=1)
    requests, observed = lax.optimization_barrier(
        (requests, (obs_anom, innov, obs_rinv, obs_lon, obs_lat))
    )
    requests = hold(requests)
    staged = stage(*observed)
    sizes = (
        patches,
        lat_patches,
        lon_patches,
        lat_devices,
        held,
        per_owner,
        lon_devices * lon_patches * PSIDE,
    )
    y_count = lon_devices // 2
    pairs = patches // 2
    cut = pairs // 2

    def grams(far, core, after):
        rows, _ = lax.optimization_barrier((staged[-1], after))
        return partial_grams(sizes, far, core, lon_devices, requests, [*staged[:-1], rows])

    along_lon = []
    while 2 ** (len(along_lon) + 1) <= y_count:
        along_lon.append(("lon", y_count >> len(along_lon)))
    routes = [[("lat", 1), *along_lon], [*along_lon[:1], ("lat", 1), *along_lon[1:]]]

    def leaves(target, axis, flip):
        y, near = target
        return near == 1 if axis == "lat" else (2 * y) & flip != 0

    parts, open_chunks, on_their_way = {}, [], [[], []]

    def exchange(merge):
        nonlocal open_chunks
        arrays, jobs, lengths, where = [], [], {}, {}

        def slot(array):
            for i, known in enumerate(arrays):
                if known is array:
                    return i
            arrays.append(array)
            return len(arrays) - 1

        def take(key):
            row = lengths.get(key, 0)
            lengths[key] = row + 1
            return row

        for far, level, parcels in open_chunks:
            for half, (targets, at, keep, keep_rows, got, got_rows) in enumerate(parcels):
                for target, keep_row, got_row in zip(targets, keep_rows, got_rows):
                    place = 0
                    if level == len(routes[half]):
                        key, row, place = ("total", far), 0, half * cut
                        lengths[key] = 1
                    elif leaves(target, *routes[half][level]):
                        key = ("send", *routes[half][level], 0 if merge else level)
                        row = take(key)
                    else:
                        key = ("keep", far, half)
                        row = take(key)
                    where[far, half, target] = key, row
                    jobs.append((slot(keep), keep_row, slot(got), got_row, at, key, row, place))
        keys = sorted(lengths, key=lambda k: (k[0], -k[-1] if k[0] == "send" else 0))
        jobs = [(*job[:5], keys.index(job[5]), *job[6:]) for job in jobs]
        shapes = [(lengths[k], pairs if k[0] == "total" else cut) for k in keys]
        due = on_their_way.pop(0)
        on_their_way.append([])
        arrays[0], arrived = lax.optimization_barrier((arrays[0], [parts[far] for far in due]))
        parts.update(zip(due, arrived))
        outs = dict(zip(keys, add_all(arrays, cut, jobs, shapes)))
        gots = {k: swap(v, k[1], k[2]) for k, v in outs.items() if k[0] == "send"}
        still = []
        for far, level, parcels in open_chunks:
            if level == len(routes[0]):
                total = outs["total", far]
                parts[far] = swap(total, "lat", 2 * far) if far else total
                if far:
                    on_their_way[1].append(far)
                continue
            following = []
            for half, (targets, *_) in enumerate(parcels):
                staying = [t for t in targets if not leaves(t, *routes[half][level])]
                leaving = [t for t in targets if leaves(t, *routes[half][level])]
                keep_rows = [where[far, half, t][1] for t in staying]
                got_rows = [where[far, half, t][1] for t in leaving]
                got = gots[where[far, half, leaving[0]][0]]
                following.append((staying, 0, outs["keep", far, half], keep_rows, got, got_rows))
            still.append((far, level + 1, following))
        open_chunks = still
        return [v for k, v in outs.items() if k[0] != "keep"]

    sent = []
    for far in reversed(range(lat_devices // 2)):
        send = grams(far, 1, sent)
        got = swap(send, "lon", 1)
        keep = grams(far, 0, [send])
        targets = [(y, near) for y in range(y_count) for near in range(2)]
        rows = range(len(targets))
        open_chunks.append(
            (far, 0, [(targets, at, keep, rows, got, rows) for at in (0, cut)])
        )
        sent = exchange(far > 0)
    while open_chunks:
        exchange(False)
    updated = analysis(
        list(parts.values()),
        holders * held * block_obs,
        state_pert.reshape(patches, fields, members, columns),
        state_mean.reshape(patches, fields, columns),
    )
    return updated.reshape(lon_patches, lat_patches, fields, members, columns)


def solution(mesh):
    in_specs = (
        P("lon", "lat", None, None, None),
        P("lon", "lat", None, None),
        P(("lon", "lat"), None, None),
        P(("lon", "lat"), None),
        P(("lon", "lat"), None),
        P(("lon", "lat"), None),
        P(("lon", "lat"), None),
        P("lon", "lat", None),
        P("lon", "lat"),
    )
    out_specs = P("lon", "lat", None, None, None)
    return jax.shard_map(
        on_device, mesh=mesh, in_specs=in_specs, out_specs=out_specs, check_vma=False
    )
```

```python
import functools

import jax
import jax.numpy as jnp
from jax import lax
from jax.experimental import pallas as pl
from jax.experimental.pallas import tpu as pltpu
from jax.sharding import PartitionSpec as P

PSIDE = 16
NS_ITERS = 5
LOC_SCALE = 48.0
EXT = 16
F32 = jnp.float32
BF16 = jnp.bfloat16
NT = (((1,), (1,)), ((), ()))


def halves(value):
    high = value.astype(BF16)
    return high, (value - high.astype(F32)).astype(BF16)


def request_table(block_list, block_count, holders, held_blocks):
    length = block_list.shape[2]
    slots = block_list.size
    per_owner = slots // holders
    used = lax.broadcasted_iota(jnp.int32, block_list.shape, 2) < block_count[:, :, None]
    wanted = jnp.where(used, block_list, -1).reshape(slots)
    holder = jnp.where(wanted < 0, holders, lax.div(wanted, held_blocks))
    order = jnp.arange(slots)
    before = (holder[:, None] == holder[None, :]) & (order[None, :] < order[:, None])
    rank = jnp.sum(before.astype(jnp.int32), axis=1)
    code = lax.div(order, length) * held_blocks + lax.rem(wanted, held_blocks)
    place = lax.broadcasted_iota(jnp.int32, (holders, per_owner + 2, 1), 1)
    asked = lax.broadcasted_iota(jnp.int32, (holders, per_owner + 2, 1), 0)
    entry = jnp.where(place == per_owner, 1, jnp.where(rank == place, code, 0))
    table = jnp.sum(jnp.where(holder == asked, entry, 0), axis=2)
    return table + jnp.where(place == per_owner + 1, asked, 0)[:, :, 0]


def stage_kernel(
    chunk,
    anom_hbm,
    innov_hbm,
    rinv_hbm,
    lon_hbm,
    lat_hbm,
    left_ref,
    rinv_ref,
    lon_ref,
    lat_ref,
    totals_ref,
    innov_ref,
    sems,
):
    held, members, block_obs = anom_hbm.shape
    pairs = [(rinv_hbm, rinv_ref), (innov_hbm, innov_ref)]
    for i in range(held // chunk):
        span = pl.ds(i * chunk, chunk)
        pairs.append((anom_hbm.at[span], left_ref.at[span, pl.ds(0, members), :]))
    pairs += [(lon_hbm, lon_ref), (lat_hbm, lat_ref)]
    copies = [pltpu.make_async_copy(a, b, sems.at[i]) for i, (a, b) in enumerate(pairs)]
    for copy in copies:
        copy.start()
    copies[0].wait()
    copies[1].wait()
    line = lax.broadcasted_iota(jnp.int32, (EXT, block_obs), 0)
    sums = jnp.zeros((8, block_obs), F32)
    for i, copy in enumerate(copies[2:-2]):
        copy.wait()

        def block(j, total, first=i * chunk):
            at = first + j
            values = left_ref[at, :members, :].astype(F32)
            squares = jnp.sum((values * values).reshape(members // 8, 8, block_obs), axis=0)
            innov = innov_ref[pl.ds(at, 1), :]
            high = innov.astype(BF16).astype(F32)
            rows = jnp.where(line == 0, high, jnp.where(line == 1, innov - high, 0.0))
            left_ref[at, members:, :] = rows.astype(BF16)
            return total + squares * rinv_ref[pl.ds(at, 1), :]

        sums = lax.fori_loop(0, chunk, block, sums, unroll=4)
    innovation = jnp.sum(rinv_ref[...] * innov_ref[...] * innov_ref[...], axis=0, keepdims=True)
    spread = jnp.sum(sums, axis=0, keepdims=True) / (members - 1)
    line = lax.broadcasted_iota(jnp.int32, (8, block_obs), 0)
    totals_ref[...] = jnp.where(line == 4, innovation, jnp.where(line == 5, spread, 0.0))
    copies[-2].wait()
    copies[-1].wait()


def stage(anom, innov, rinv, lon, lat):
    held, members, block_obs = anom.shape
    chunk = 16 if held % 16 == 0 else held
    operands = [pltpu.with_memory_space_constraint(v, pltpu.HBM) for v in (anom, innov, rinv, lon, lat)]
    return pl.pallas_call(
        functools.partial(stage_kernel, chunk),
        out_shape=[
            pltpu.VMEM((held, members + EXT, block_obs), BF16),
            pltpu.VMEM((held, block_obs), F32),
            pltpu.VMEM((held, block_obs), jnp.int32),
            pltpu.VMEM((held, block_obs), jnp.int32),
            pltpu.VMEM((8, block_obs), F32),
        ],
        in_specs=[pl.BlockSpec(memory_space=pltpu.HBM)] * 5,
        out_specs=[pl.BlockSpec(memory_space=pltpu.VMEM)] * 5,
        scratch_shapes=[
            pltpu.VMEM((held, block_obs), F32),
            pltpu.SemaphoreType.DMA((held // chunk + 4,)),
        ],
        compiler_params=pltpu.CompilerParams(vmem_limit_bytes=4 * 2**20),
        cost_estimate=pl.CostEstimate(flops=0, bytes_accessed=anom.size * 4, transcendentals=0),
        name="stage",
    )(*operands)


def gram_kernel(
    sizes,
    far,
    core,
    requests_ref,
    left_ref,
    rinv_ref,
    obs_lon_ref,
    obs_lat_ref,
    totals_ref,
    out_ref,
    acc_ref,
):
    patches, lat_patches, lon_patches, lat_devices, held, per_owner, grid_lon = sizes
    step = pl.program_id(0)
    me = requests_ref[0, per_owner + 1]
    distance = (2 * (step // 2) + core) * lat_devices + (2 * far + step % 2)
    target = me ^ distance
    lon_first = (target // lat_devices) * lon_patches
    lat_first = (target % lat_devices) * lat_patches
    members = left_ref.shape[2]
    acc_ref[...] = jnp.zeros_like(acc_ref)
    number = requests_ref[target, per_owner]

    products = []
    for entry in range(per_owner):
        code = requests_ref[target, entry]
        patch = code // held
        block = code % held
        centre_lon = (lon_first + patch // lat_patches) * (2 * PSIDE) + (PSIDE - 1)
        centre_lat = (lat_first + patch % lat_patches) * (2 * PSIDE) + (PSIDE - 1)
        row = pl.ds(block, 1)
        lon_gap = jnp.abs(2 * obs_lon_ref[row, :] - centre_lon)
        lon_gap = jnp.minimum(lon_gap, 2 * grid_lon - lon_gap)
        lat_gap = 2 * obs_lat_ref[row, :] - centre_lat
        square = (lon_gap * lon_gap + lat_gap * lat_gap).astype(F32)
        rinv = jnp.where(entry < number, rinv_ref[row, :], 0.0)
        weight = rinv * jnp.exp(square * (-1.0 / (8.0 * LOC_SCALE * LOC_SCALE)))
        left = left_ref[block]
        scaled = (left[:members].astype(F32) * weight).astype(BF16)
        product = lax.dot_general(left, scaled, NT, preferred_element_type=F32)
        products.append((patch, product[: members + 8]))
    for patch, product in products:
        acc_ref[patch] += product

    row = lax.broadcasted_iota(jnp.int32, (members, members), 0)
    column = lax.broadcasted_iota(jnp.int32, (members, members), 1)
    line = lax.broadcasted_iota(jnp.int32, (8, members), 0)
    for pair in range(patches // 2):
        first = acc_ref[2 * pair]
        second = acc_ref[2 * pair + 1]
        packed = jnp.where(row < column, first[:members], second[:members])
        out_ref[0, pair, :members, :] = packed.astype(BF16)
        rows = totals_ref[...]
        for place, values in ((0, first), (2, second)):
            diagonal = jnp.sum(
                jnp.where(row == column, values[:members], 0.0), axis=0, keepdims=True
            )
            projected = values[members : members + 1] + values[members + 1 : members + 2]
            rows = jnp.where(line == place, diagonal, rows)
            rows = jnp.where(line == place + 1, projected, rows)
        high = rows.astype(BF16).astype(F32)
        out_ref[0, pair, members:, :] = jnp.concatenate([high, rows - high], axis=0).astype(BF16)


def hold_kernel(table_hbm, held_ref, sem):
    copy = pltpu.make_async_copy(table_hbm, held_ref, sem)
    copy.start()
    copy.wait()


def hold(table):
    return pl.pallas_call(
        hold_kernel,
        out_shape=pltpu.SMEM(table.shape, table.dtype),
        in_specs=[pl.BlockSpec(memory_space=pl.ANY)],
        out_specs=pl.BlockSpec(memory_space=pltpu.SMEM),
        scratch_shapes=[pltpu.SemaphoreType.DMA(())],
        compiler_params=pltpu.CompilerParams(vmem_limit_bytes=2**20),
        name="hold",
    )(table)


def partial_grams(sizes, far, core, count, requests, staged):
    patches, per_owner = sizes[0], sizes[5]
    members = staged[0].shape[2]
    rows = members + EXT
    block = (1, patches // 2, rows, members)
    return pl.pallas_call(
        functools.partial(gram_kernel, sizes, far, core),
        out_shape=jax.ShapeDtypeStruct((count, *block[1:]), BF16),
        grid_spec=pltpu.PrefetchScalarGridSpec(
            num_scalar_prefetch=0,
            grid=(count,),
            in_specs=[pl.BlockSpec(memory_space=pltpu.SMEM)] + [pl.BlockSpec(memory_space=pltpu.VMEM)] * 5,
            out_specs=pl.BlockSpec(block, lambda i, *_: (i, 0, 0, 0)),
            scratch_shapes=[pltpu.VMEM((patches, members + 8, members), F32)],
        ),
        compiler_params=pltpu.CompilerParams(vmem_limit_bytes=8 * 2**20),
        cost_estimate=pl.CostEstimate(
            flops=count * per_owner * 100 * members**3, bytes_accessed=0, transcendentals=0
        ),
        name="partial_grams",
    )(requests, *staged)


def added(left, right):
    members = left.shape[-1]
    total = left.astype(F32) + right.astype(F32)
    rows = total[:, members : members + 8] + total[:, members + 8 :]
    high = rows.astype(BF16).astype(F32)
    rows = jnp.concatenate([high, rows - high], axis=1)
    return total[:, :members].astype(BF16), rows.astype(BF16)


def add_kernel(inputs, size, jobs, *refs):
    for left, left_row, right, right_row, at, out, row, place in jobs:
        out_ref = refs[inputs + out]
        members = out_ref.shape[-1]
        span, to = slice(at, at + size), slice(place, place + size)
        body, rows = added(refs[left][left_row, span], refs[right][right_row, span])
        out_ref[row, to, :members, :] = body
        out_ref[row, to, members:, :] = rows


def add_all(arrays, size, jobs, shapes):
    inner = arrays[0].shape[2:]
    whole = pl.BlockSpec(memory_space=pltpu.VMEM)
    work = len(jobs) * size * inner[0] * inner[1]
    return pl.pallas_call(
        functools.partial(add_kernel, len(arrays), size, jobs),
        out_shape=[jax.ShapeDtypeStruct((*shape, *inner), BF16) for shape in shapes],
        in_specs=[whole] * len(arrays),
        out_specs=[whole] * len(shapes),
        compiler_params=pltpu.CompilerParams(vmem_limit_bytes=8 * 2**20),
        cost_estimate=pl.CostEstimate(flops=work * 4, bytes_accessed=work * 6, transcendentals=0),
        name="add_partials",
    )(*arrays)


def product(left, right):
    left_high, left_low = left
    right_high, right_low = right
    return jnp.dot(
        jnp.concatenate([left_high, left_low, left_high], axis=1),
        jnp.concatenate([right_high, right_high, right_low], axis=0),
        preferred_element_type=F32,
    )


def solve_group(parts, total_obs, first, count):
    members = parts[0].shape[-1]
    row = lax.broadcasted_iota(jnp.int32, (members, members), 0)
    column = lax.broadcasted_iota(jnp.int32, (members, members), 1)
    identity = (row == column).astype(F32)
    systems, projected = [], []
    for pair in range(count):
        total = parts[0][0, first + pair].astype(F32)
        for part in parts[1:]:
            total = total + part[0, first + pair].astype(F32)
        packed = total[:members]
        values = total[members : members + 8] + total[members + 8 :]
        flipped = packed.T
        innovation = jnp.sum(values[4:5], axis=1, keepdims=True)
        spread = jnp.sum(values[5:6], axis=1, keepdims=True)
        ridge = (members - 1) * (spread + total_obs) / innovation
        for place, full in (
            (0, jnp.where(row < column, packed, flipped)),
            (2, jnp.where(row > column, packed, flipped)),
        ):
            systems.append(jnp.where(row == column, values[place : place + 1] + ridge, full))
            projected.append(values[place + 1 : place + 2])
    scalings, roots = [], []
    for system in systems:
        squares = jnp.sum(system * system, axis=0, keepdims=True)
        scaling = jnp.sqrt(jnp.sum(squares, axis=1, keepdims=True))
        scalings.append(scaling)
        roots.append(system * (1.0 / scaling))
    factors = [1.5 * identity - 0.5 * root for root in roots]
    roots = [product(halves(f), halves(r)) for f, r in zip(factors, roots)]
    inverses = factors
    for iteration in range(1, NS_ITERS):
        split_roots = [halves(r) for r in roots]
        split_inverses = [halves(z) for z in inverses]
        factors = [
            halves(1.5 * identity - 0.5 * product(z, r))
            for z, r in zip(split_inverses, split_roots)
        ]
        if iteration < NS_ITERS - 1:
            both = [
                product(f, [jnp.concatenate([a, b], axis=1) for a, b in zip(r, z)])
                for f, r, z in zip(factors, split_roots, split_inverses)
            ]
            roots = [b[:, :members] for b in both]
            inverses = [b[:, members:] for b in both]
        else:
            inverses = [product(f, z) for f, z in zip(factors, split_inverses)]
    weights = []
    for scaling, inverse, values in zip(scalings, inverses, projected):
        inverse_sqrt = inverse * lax.rsqrt(scaling)
        inner = jnp.sum(inverse_sqrt * values, axis=1, keepdims=True)
        mean = jnp.sum(inverse_sqrt * inner, axis=0, keepdims=True)
        weights.append((jnp.sqrt(F32(members - 1)) * inverse_sqrt + mean).astype(BF16))
    return weights


def analysis_kernel(count, total_obs, group, *refs):
    parts, (pert_ref, mean_ref, out_ref, weights_ref) = refs[:count], refs[count:]
    step = pl.program_id(0)
    size, fields = pert_ref.shape[:2]
    now, before = lax.rem(step, 2), lax.rem(step + 1, 2)
    for patch in range(size):
        held = weights_ref[before, patch]
        for field in range(fields):
            change = jnp.dot(held, pert_ref[patch, field], preferred_element_type=F32)
            out_ref[patch, field] = change + mean_ref[patch, field : field + 1]
    groups = pl.num_programs(0) - 1
    first = jnp.minimum(step, groups - 1) * (group // 2)
    for patch, weights in enumerate(solve_group(parts, total_obs, first, group // 2)):
        weights_ref[now, patch] = weights


def analysis(parts, total_obs, pert, mean):
    patches, fields, members, columns = pert.shape
    group = patches // 2
    whole = pl.BlockSpec(memory_space=pltpu.VMEM)
    return pl.pallas_call(
        functools.partial(analysis_kernel, len(parts), total_obs, group),
        out_shape=jax.ShapeDtypeStruct(pert.shape, F32),
        grid=(patches // group + 1,),
        in_specs=[whole] * len(parts)
        + [
            pl.BlockSpec(
                (group, fields, members, columns), lambda i: (jnp.maximum(i - 1, 0), 0, 0, 0)
            ),
            pl.BlockSpec((group, fields, columns), lambda i: (jnp.maximum(i - 1, 0), 0, 0)),
        ],
        out_specs=pl.BlockSpec(
            (group, fields, members, columns), lambda i: (jnp.maximum(i - 1, 0), 0, 0, 0)
        ),
        scratch_shapes=[pltpu.VMEM((2, group, members, members), BF16)],
        compiler_params=pltpu.CompilerParams(vmem_limit_bytes=40 * 2**20),
        name="analysis",
    )(*parts, pert, mean)


def swap(value, axis, flip):
    size = lax.axis_size(axis)
    return lax.ppermute(value, axis, [(i, i ^ flip) for i in range(size)])


def on_device(
    state_pert, state_mean, obs_anom, innov, obs_rinv, obs_lon, obs_lat, block_list, block_count
):
    lon_devices, lat_devices = lax.axis_size("lon"), lax.axis_size("lat")
    holders = lon_devices * lat_devices
    lon_patches, lat_patches, fields, members, columns = state_pert.shape
    patches = lon_patches * lat_patches
    length = block_list.shape[2]
    held, _, block_obs = obs_anom.shape
    per_owner = patches * length // holders
    table = request_table(block_list, block_count, holders, held)
    requests = lax.all_to_all(table, ("lon", "lat"), split_axis=0, concat_axis=0, tiled=True)

    requests, observed = lax.optimization_barrier(
        (requests, (obs_anom, innov, obs_rinv, obs_lon, obs_lat))
    )
    requests = hold(requests)
    staged = stage(*observed)
    sizes = (
        patches,
        lat_patches,
        lon_patches,
        lat_devices,
        held,
        per_owner,
        lon_devices * lon_patches * PSIDE,
    )
    y_count = lon_devices // 2
    pairs = patches // 2
    cut = pairs // 2

    def grams(far, core, after):
        rows, _ = lax.optimization_barrier((staged[-1], after))
        return partial_grams(sizes, far, core, lon_devices, requests, [*staged[:-1], rows])

    along_lon = []
    while 2 ** (len(along_lon) + 1) <= y_count:
        along_lon.append(("lon", y_count >> len(along_lon)))
    routes = [[("lat", 1), *along_lon], [*along_lon[:1], ("lat", 1), *along_lon[1:]]]

    def leaves(target, axis, flip):
        y, near = target
        return near == 1 if axis == "lat" else (2 * y) & flip != 0

    parts, open_chunks, on_their_way = {}, [], [[], []]

    def exchange(merge):
        nonlocal open_chunks
        arrays, jobs, lengths, where = [], [], {}, {}

        def slot(array):
            for i, known in enumerate(arrays):
                if known is array:
                    return i
            arrays.append(array)
            return len(arrays) - 1

        def take(key):
            row = lengths.get(key, 0)
            lengths[key] = row + 1
            return row

        for far, level, parcels in open_chunks:
            for half, (targets, at, keep, keep_rows, got, got_rows) in enumerate(parcels):
                for target, keep_row, got_row in zip(targets, keep_rows, got_rows):
                    place = 0
                    if level == len(routes[half]):
                        key, row, place = ("total", far), 0, half * cut
                        lengths[key] = 1
                    elif leaves(target, *routes[half][level]):
                        key = ("send", *routes[half][level], 0 if merge else level)
                        row = take(key)
                    else:
                        key = ("keep", far, half)
                        row = take(key)
                    where[far, half, target] = key, row
                    jobs.append((slot(keep), keep_row, slot(got), got_row, at, key, row, place))
        keys = sorted(lengths, key=lambda k: (k[0], -k[-1] if k[0] == "send" else 0))
        jobs = [(*job[:5], keys.index(job[5]), *job[6:]) for job in jobs]
        shapes = [(lengths[k], pairs if k[0] == "total" else cut) for k in keys]
        due = on_their_way.pop(0)
        on_their_way.append([])
        arrays[0], arrived = lax.optimization_barrier((arrays[0], [parts[far] for far in due]))
        parts.update(zip(due, arrived))
        outs = dict(zip(keys, add_all(arrays, cut, jobs, shapes)))
        gots = {k: swap(v, k[1], k[2]) for k, v in outs.items() if k[0] == "send"}
        still = []
        for far, level, parcels in open_chunks:
            if level == len(routes[0]):
                total = outs["total", far]
                parts[far] = swap(total, "lat", 2 * far) if far else total
                if far:
                    on_their_way[1].append(far)
                continue
            following = []
            for half, (targets, *_) in enumerate(parcels):
                staying = [t for t in targets if not leaves(t, *routes[half][level])]
                leaving = [t for t in targets if leaves(t, *routes[half][level])]
                keep_rows = [where[far, half, t][1] for t in staying]
                got_rows = [where[far, half, t][1] for t in leaving]
                got = gots[where[far, half, leaving[0]][0]]
                following.append((staying, 0, outs["keep", far, half], keep_rows, got, got_rows))
            still.append((far, level + 1, following))
        open_chunks = still
        return [v for k, v in outs.items() if k[0] != "keep"]

    sent = []
    for far in reversed(range(lat_devices // 2)):
        send = grams(far, 1, sent)
        got = swap(send, "lon", 1)
        keep = grams(far, 0, [send])
        targets = [(y, near) for y in range(y_count) for near in range(2)]
        rows = range(len(targets))
        open_chunks.append(
            (far, 0, [(targets, at, keep, rows, got, rows) for at in (0, cut)])
        )
        sent = exchange(far > 0)
    while open_chunks:
        exchange(False)
    updated = analysis(
        list(parts.values()),
        holders * held * block_obs,
        state_pert.reshape(patches, fields, members, columns),
        state_mean.reshape(patches, fields, columns),
    )
    return updated.reshape(lon_patches, lat_patches, fields, members, columns)


def solution(mesh):
    in_specs = (
        P("lon", "lat", None, None, None),
        P("lon", "lat", None, None),
        P(("lon", "lat"), None, None),
        P(("lon", "lat"), None),
        P(("lon", "lat"), None),
        P(("lon", "lat"), None),
        P(("lon", "lat"), None),
        P("lon", "lat", None),
        P("lon", "lat"),
    )
    out_specs = P("lon", "lat", None, None, None)
    return jax.shard_map(
        on_device, mesh=mesh, in_specs=in_specs, out_specs=out_specs, check_vma=False
    )
```

```python
import functools

import jax
import jax.numpy as jnp
from jax import lax
from jax.experimental import pallas as pl
from jax.experimental.pallas import tpu as pltpu
from jax.sharding import PartitionSpec as P

PSIDE = 16
NS_ITERS = 5
LOC_SCALE = 48.0
EXT = 16
F32 = jnp.float32
BF16 = jnp.bfloat16
NT = (((1,), (1,)), ((), ()))


def halves(value):
    high = value.astype(BF16)
    return high, (value - high.astype(F32)).astype(BF16)


def request_table(block_list, block_count, holders, held_blocks):
    length = block_list.shape[2]
    slots = block_list.size
    per_owner = slots // holders
    used = lax.broadcasted_iota(jnp.int32, block_list.shape, 2) < block_count[:, :, None]
    wanted = jnp.where(used, block_list, -1).reshape(slots)
    holder = jnp.where(wanted < 0, holders, lax.div(wanted, held_blocks))
    order = jnp.arange(slots)
    before = (holder[:, None] == holder[None, :]) & (order[None, :] < order[:, None])
    rank = jnp.sum(before.astype(jnp.int32), axis=1)
    code = lax.div(order, length) * held_blocks + lax.rem(wanted, held_blocks)
    place = lax.broadcasted_iota(jnp.int32, (holders, per_owner + 2, 1), 1)
    asked = lax.broadcasted_iota(jnp.int32, (holders, per_owner + 2, 1), 0)
    entry = jnp.where(place == per_owner, 1, jnp.where(rank == place, code, 0))
    table = jnp.sum(jnp.where(holder == asked, entry, 0), axis=2)
    return table + jnp.where(place == per_owner + 1, asked, 0)[:, :, 0]


def stage_kernel(
    chunk,
    anom_hbm,
    innov_hbm,
    rinv_hbm,
    lon_hbm,
    lat_hbm,
    left_ref,
    rinv_ref,
    lon_ref,
    lat_ref,
    totals_ref,
    innov_ref,
    sems,
):
    held, members, block_obs = anom_hbm.shape
    pairs = [(rinv_hbm, rinv_ref), (innov_hbm, innov_ref)]
    for i in range(held // chunk):
        span = pl.ds(i * chunk, chunk)
        pairs.append((anom_hbm.at[span], left_ref.at[span, pl.ds(0, members), :]))
    pairs += [(lon_hbm, lon_ref), (lat_hbm, lat_ref)]
    copies = [pltpu.make_async_copy(a, b, sems.at[i]) for i, (a, b) in enumerate(pairs)]
    for copy in copies:
        copy.start()
    copies[0].wait()
    copies[1].wait()
    line = lax.broadcasted_iota(jnp.int32, (EXT, block_obs), 0)
    sums = jnp.zeros((8, block_obs), F32)
    for i, copy in enumerate(copies[2:-2]):
        copy.wait()

        def block(j, total, first=i * chunk):
            at = first + j
            values = left_ref[at, :members, :].astype(F32)
            squares = jnp.sum((values * values).reshape(members // 8, 8, block_obs), axis=0)
            innov = innov_ref[pl.ds(at, 1), :]
            high = innov.astype(BF16).astype(F32)
            rows = jnp.where(line == 0, high, jnp.where(line == 1, innov - high, 0.0))
            left_ref[at, members:, :] = rows.astype(BF16)
            return total + squares * rinv_ref[pl.ds(at, 1), :]

        sums = lax.fori_loop(0, chunk, block, sums, unroll=4)
    innovation = jnp.sum(rinv_ref[...] * innov_ref[...] * innov_ref[...], axis=0, keepdims=True)
    spread = jnp.sum(sums, axis=0, keepdims=True) / (members - 1)
    line = lax.broadcasted_iota(jnp.int32, (8, block_obs), 0)
    totals_ref[...] = jnp.where(line == 4, innovation, jnp.where(line == 5, spread, 0.0))
    copies[-2].wait()
    copies[-1].wait()


def stage(anom, innov, rinv, lon, lat):
    held, members, block_obs = anom.shape
    chunk = 16 if held % 16 == 0 else held
    operands = [pltpu.with_memory_space_constraint(v, pltpu.HBM) for v in (anom, innov, rinv, lon, lat)]
    return pl.pallas_call(
        functools.partial(stage_kernel, chunk),
        out_shape=[
            pltpu.VMEM((held, members + EXT, block_obs), BF16),
            pltpu.VMEM((held, block_obs), F32),
            pltpu.VMEM((held, block_obs), jnp.int32),
            pltpu.VMEM((held, block_obs), jnp.int32),
            pltpu.VMEM((8, block_obs), F32),
        ],
        in_specs=[pl.BlockSpec(memory_space=pltpu.HBM)] * 5,
        out_specs=[pl.BlockSpec(memory_space=pltpu.VMEM)] * 5,
        scratch_shapes=[
            pltpu.VMEM((held, block_obs), F32),
            pltpu.SemaphoreType.DMA((held // chunk + 4,)),
        ],
        compiler_params=pltpu.CompilerParams(vmem_limit_bytes=4 * 2**20),
        cost_estimate=pl.CostEstimate(flops=0, bytes_accessed=anom.size * 4, transcendentals=0),
        name="stage",
    )(*operands)


def gram_kernel(
    sizes,
    far,
    core,
    requests_ref,
    left_ref,
    rinv_ref,
    obs_lon_ref,
    obs_lat_ref,
    totals_ref,
    out_ref,
    acc_ref,
):
    patches, lat_patches, lon_patches, lat_devices, held, per_owner, grid_lon = sizes
    step = pl.program_id(0)
    me = requests_ref[0, per_owner + 1]
    distance = (2 * (step // 2) + core) * lat_devices + (2 * far + step % 2)
    target = me ^ distance
    lon_first = (target // lat_devices) * lon_patches
    lat_first = (target % lat_devices) * lat_patches
    members = left_ref.shape[2]
    acc_ref[...] = jnp.zeros_like(acc_ref)
    number = requests_ref[target, per_owner]

    products = []
    for entry in range(per_owner):
        code = requests_ref[target, entry]
        patch = code // held
        block = code % held
        centre_lon = (lon_first + patch // lat_patches) * (2 * PSIDE) + (PSIDE - 1)
        centre_lat = (lat_first + patch % lat_patches) * (2 * PSIDE) + (PSIDE - 1)
        row = pl.ds(block, 1)
        lon_gap = jnp.abs(2 * obs_lon_ref[row, :] - centre_lon)
        lon_gap = jnp.minimum(lon_gap, 2 * grid_lon - lon_gap)
        lat_gap = 2 * obs_lat_ref[row, :] - centre_lat
        square = (lon_gap * lon_gap + lat_gap * lat_gap).astype(F32)
        rinv = jnp.where(entry < number, rinv_ref[row, :], 0.0)
        weight = rinv * jnp.exp(square * (-1.0 / (8.0 * LOC_SCALE * LOC_SCALE)))
        left = left_ref[block]
        scaled = (left[:members].astype(F32) * weight).astype(BF16)
        product = lax.dot_general(left, scaled, NT, preferred_element_type=F32)
        products.append((patch, product[: members + 8]))
    for patch, product in products:
        acc_ref[patch] += product

    row = lax.broadcasted_iota(jnp.int32, (members, members), 0)
    column = lax.broadcasted_iota(jnp.int32, (members, members), 1)
    line = lax.broadcasted_iota(jnp.int32, (8, members), 0)
    for pair in range(patches // 2):
        first = acc_ref[2 * pair]
        second = acc_ref[2 * pair + 1]
        packed = jnp.where(row < column, first[:members], second[:members])
        out_ref[0, pair, :members, :] = packed.astype(BF16)
        rows = totals_ref[...]
        for place, values in ((0, first), (2, second)):
            diagonal = jnp.sum(
                jnp.where(row == column, values[:members], 0.0), axis=0, keepdims=True
            )
            projected = values[members : members + 1] + values[members + 1 : members + 2]
            rows = jnp.where(line == place, diagonal, rows)
            rows = jnp.where(line == place + 1, projected, rows)
        high = rows.astype(BF16).astype(F32)
        out_ref[0, pair, members:, :] = jnp.concatenate([high, rows - high], axis=0).astype(BF16)


def hold_kernel(table_hbm, held_ref, sem):
    copy = pltpu.make_async_copy(table_hbm, held_ref, sem)
    copy.start()
    copy.wait()


def hold(table):
    return pl.pallas_call(
        hold_kernel,
        out_shape=pltpu.SMEM(table.shape, table.dtype),
        in_specs=[pl.BlockSpec(memory_space=pl.ANY)],
        out_specs=pl.BlockSpec(memory_space=pltpu.SMEM),
        scratch_shapes=[pltpu.SemaphoreType.DMA(())],
        compiler_params=pltpu.CompilerParams(vmem_limit_bytes=2**20),
        name="hold",
    )(table)


def partial_grams(sizes, far, core, count, requests, staged):
    patches, per_owner = sizes[0], sizes[5]
    members = staged[0].shape[2]
    rows = members + EXT
    block = (1, patches // 2, rows, members)
    return pl.pallas_call(
        functools.partial(gram_kernel, sizes, far, core),
        out_shape=jax.ShapeDtypeStruct((count, *block[1:]), BF16),
        grid_spec=pltpu.PrefetchScalarGridSpec(
            num_scalar_prefetch=0,
            grid=(count,),
            in_specs=[pl.BlockSpec(memory_space=pltpu.SMEM)] + [pl.BlockSpec(memory_space=pltpu.VMEM)] * 5,
            out_specs=pl.BlockSpec(block, lambda i, *_: (i, 0, 0, 0)),
            scratch_shapes=[pltpu.VMEM((patches, members + 8, members), F32)],
        ),
        compiler_params=pltpu.CompilerParams(vmem_limit_bytes=8 * 2**20),
        cost_estimate=pl.CostEstimate(
            flops=count * per_owner * 100 * members**3, bytes_accessed=0, transcendentals=0
        ),
        name="partial_grams",
    )(requests, *staged)


def added(left, right):
    members = left.shape[-1]
    total = left.astype(F32) + right.astype(F32)
    rows = total[:, members : members + 8] + total[:, members + 8 :]
    high = rows.astype(BF16).astype(F32)
    rows = jnp.concatenate([high, rows - high], axis=1)
    return total[:, :members].astype(BF16), rows.astype(BF16)


def add_kernel(inputs, size, jobs, *refs):
    for left, left_row, right, right_row, at, out, row, place in jobs:
        out_ref = refs[inputs + out]
        members = out_ref.shape[-1]
        span, to = slice(at, at + size), slice(place, place + size)
        body, rows = added(refs[left][left_row, span], refs[right][right_row, span])
        out_ref[row, to, :members, :] = body
        out_ref[row, to, members:, :] = rows


def add_all(arrays, size, jobs, shapes):
    inner = arrays[0].shape[2:]
    whole = pl.BlockSpec(memory_space=pltpu.VMEM)
    work = len(jobs) * size * inner[0] * inner[1]
    return pl.pallas_call(
        functools.partial(add_kernel, len(arrays), size, jobs),
        out_shape=[jax.ShapeDtypeStruct((*shape, *inner), BF16) for shape in shapes],
        in_specs=[whole] * len(arrays),
        out_specs=[whole] * len(shapes),
        compiler_params=pltpu.CompilerParams(vmem_limit_bytes=8 * 2**20),
        cost_estimate=pl.CostEstimate(flops=work * 4, bytes_accessed=work * 6, transcendentals=0),
        name="add_partials",
    )(*arrays)


def product(left, right):
    left_high, left_low = left
    right_high, right_low = right
    return jnp.dot(
        jnp.concatenate([left_high, left_low, left_high], axis=1),
        jnp.concatenate([right_high, right_high, right_low], axis=0),
        preferred_element_type=F32,
    )


def solve_group(parts, total_obs, first, count):
    members = parts[0].shape[-1]
    row = lax.broadcasted_iota(jnp.int32, (members, members), 0)
    column = lax.broadcasted_iota(jnp.int32, (members, members), 1)
    identity = (row == column).astype(F32)
    systems, projected = [], []
    for pair in range(count):
        total = parts[0][0, first + pair].astype(F32)
        for part in parts[1:]:
            total = total + part[0, first + pair].astype(F32)
        packed = total[:members]
        values = total[members : members + 8] + total[members + 8 :]
        flipped = packed.T
        innovation = jnp.sum(values[4:5], axis=1, keepdims=True)
        spread = jnp.sum(values[5:6], axis=1, keepdims=True)
        ridge = (members - 1) * (spread + total_obs) / innovation
        for place, full in (
            (0, jnp.where(row < column, packed, flipped)),
            (2, jnp.where(row > column, packed, flipped)),
        ):
            systems.append(jnp.where(row == column, values[place : place + 1] + ridge, full))
            projected.append(values[place + 1 : place + 2])
    scalings, roots = [], []
    for system in systems:
        squares = jnp.sum(system * system, axis=0, keepdims=True)
        scaling = jnp.sqrt(jnp.sum(squares, axis=1, keepdims=True))
        scalings.append(scaling)
        roots.append(system * (1.0 / scaling))
    factors = [1.5 * identity - 0.5 * root for root in roots]
    roots = [product(halves(f), halves(r)) for f, r in zip(factors, roots)]
    inverses = factors
    for iteration in range(1, NS_ITERS):
        split_roots = [halves(r) for r in roots]
        split_inverses = [halves(z) for z in inverses]
        factors = [
            halves(1.5 * identity - 0.5 * product(z, r))
            for z, r in zip(split_inverses, split_roots)
        ]
        if iteration < NS_ITERS - 1:
            both = [
                product(f, [jnp.concatenate([a, b], axis=1) for a, b in zip(r, z)])
                for f, r, z in zip(factors, split_roots, split_inverses)
            ]
            roots = [b[:, :members] for b in both]
            inverses = [b[:, members:] for b in both]
        else:
            inverses = [product(f, z) for f, z in zip(factors, split_inverses)]
    weights = []
    for scaling, inverse, values in zip(scalings, inverses, projected):
        inverse_sqrt = inverse * lax.rsqrt(scaling)
        inner = jnp.sum(inverse_sqrt * values, axis=1, keepdims=True)
        mean = jnp.sum(inverse_sqrt * inner, axis=0, keepdims=True)
        weights.append((jnp.sqrt(F32(members - 1)) * inverse_sqrt + mean).astype(BF16))
    return weights


def analysis_kernel(count, total_obs, group, *refs):
    parts, (pert_ref, mean_ref, out_ref, weights_ref) = refs[:count], refs[count:]
    step = pl.program_id(0)
    size, fields = pert_ref.shape[:2]
    now, before = lax.rem(step, 2), lax.rem(step + 1, 2)
    for patch in range(size):
        held = weights_ref[before, patch]
        for field in range(fields):
            change = jnp.dot(held, pert_ref[patch, field], preferred_element_type=F32)
            out_ref[patch, field] = change + mean_ref[patch, field : field + 1]
    groups = pl.num_programs(0) - 1
    first = jnp.minimum(step, groups - 1) * (group // 2)
    for patch, weights in enumerate(solve_group(parts, total_obs, first, group // 2)):
        weights_ref[now, patch] = weights


def analysis(parts, total_obs, pert, mean):
    patches, fields, members, columns = pert.shape
    group = patches // 2
    whole = pl.BlockSpec(memory_space=pltpu.VMEM)
    return pl.pallas_call(
        functools.partial(analysis_kernel, len(parts), total_obs, group),
        out_shape=jax.ShapeDtypeStruct(pert.shape, F32),
        grid=(patches // group + 1,),
        in_specs=[whole] * len(parts)
        + [
            pl.BlockSpec(
                (group, fields, members, columns), lambda i: (jnp.maximum(i - 1, 0), 0, 0, 0)
            ),
            pl.BlockSpec((group, fields, columns), lambda i: (jnp.maximum(i - 1, 0), 0, 0)),
        ],
        out_specs=pl.BlockSpec(
            (group, fields, members, columns), lambda i: (jnp.maximum(i - 1, 0), 0, 0, 0)
        ),
        scratch_shapes=[pltpu.VMEM((2, group, members, members), BF16)],
        compiler_params=pltpu.CompilerParams(vmem_limit_bytes=40 * 2**20),
        name="analysis",
    )(*parts, pert, mean)


def swap(value, axis, flip):
    size = lax.axis_size(axis)
    return lax.ppermute(value, axis, [(i, i ^ flip) for i in range(size)])


def on_device(
    state_pert, state_mean, obs_anom, innov, obs_rinv, obs_lon, obs_lat, block_list, block_count
):
    lon_devices, lat_devices = lax.axis_size("lon"), lax.axis_size("lat")
    holders = lon_devices * lat_devices
    lon_patches, lat_patches, fields, members, columns = state_pert.shape
    patches = lon_patches * lat_patches
    length = block_list.shape[2]
    held, _, block_obs = obs_anom.shape
    per_owner = patches * length // holders
    table = request_table(block_list, block_count, holders, held)
    requests = lax.all_to_all(table, ("lon", "lat"), split_axis=0, concat_axis=0, tiled=True)

    requests, observed = lax.optimization_barrier(
        (requests, (obs_anom, innov, obs_rinv, obs_lon, obs_lat))
    )
    requests = hold(requests)
    staged = stage(*observed)
    sizes = (
        patches,
        lat_patches,
        lon_patches,
        lat_devices,
        held,
        per_owner,
        lon_devices * lon_patches * PSIDE,
    )
    y_count = lon_devices // 2
    pairs = patches // 2
    cut = pairs // 2

    def grams(far, core, after):
        rows, _ = lax.optimization_barrier((staged[-1], after))
        return partial_grams(sizes, far, core, lon_devices, requests, [*staged[:-1], rows])

    along_lon = []
    while 2 ** (len(along_lon) + 1) <= y_count:
        along_lon.append(("lon", y_count >> len(along_lon)))
    routes = [[("lat", 1), *along_lon], [*along_lon[:1], ("lat", 1), *along_lon[1:]]]

    def leaves(target, axis, flip):
        y, near = target
        return near == 1 if axis == "lat" else (2 * y) & flip != 0

    parts, open_chunks, on_their_way = {}, [], [[], []]

    def exchange(chunks, merge):
        arrays, jobs, lengths, where = [], [], {}, {}

        def slot(array):
            for i, known in enumerate(arrays):
                if known is array:
                    return i
            arrays.append(array)
            return len(arrays) - 1

        def take(key):
            row = lengths.get(key, 0)
            lengths[key] = row + 1
            return row

        for far, level, parcels in chunks:
            for half, (targets, at, keep, keep_rows, got, got_rows) in enumerate(parcels):
                for target, keep_row, got_row in zip(targets, keep_rows, got_rows):
                    place = 0
                    if level == len(routes[half]):
                        key, row, place = ("total", far), 0, half * cut
                        lengths[key] = 1
                    elif leaves(target, *routes[half][level]):
                        key = ("send", *routes[half][level], 0 if merge else level)
                        row = take(key)
                    else:
                        key = ("keep", far, half)
                        row = take(key)
                    where[far, half, target] = key, row
                    jobs.append((slot(keep), keep_row, slot(got), got_row, at, key, row, place))
        keys = sorted(lengths, key=lambda k: (k[0], -k[-1] if k[0] == "send" else 0))
        jobs = [(*job[:5], keys.index(job[5]), *job[6:]) for job in jobs]
        shapes = [(lengths[k], pairs if k[0] == "total" else cut) for k in keys]
        due = on_their_way.pop(0)
        on_their_way.append([])
        arrays[0], arrived = lax.optimization_barrier((arrays[0], [parts[far] for far in due]))
        parts.update(zip(due, arrived))
        outs = dict(zip(keys, add_all(arrays, cut, jobs, shapes)))
        gots = {k: swap(v, k[1], k[2]) for k, v in outs.items() if k[0] == "send"}
        still = []
        for far, level, parcels in chunks:
            if level == len(routes[0]):
                total = outs["total", far]
                parts[far] = swap(total, "lat", 2 * far) if far else total
                if far and merge:
                    on_their_way[1].append(far)
                continue
            following = []
            for half, (targets, *_) in enumerate(parcels):
                staying = [t for t in targets if not leaves(t, *routes[half][level])]
                leaving = [t for t in targets if leaves(t, *routes[half][level])]
                keep_rows = [where[far, half, t][1] for t in staying]
                got_rows = [where[far, half, t][1] for t in leaving]
                got = gots[where[far, half, leaving[0]][0]]
                following.append((staying, 0, outs["keep", far, half], keep_rows, got, got_rows))
            still.append((far, level + 1, following))
        return still, [v for k, v in outs.items() if k[0] != "keep"]

    sent = []
    for far in reversed(range(lat_devices // 2)):
        send = grams(far, 1, sent)
        got = swap(send, "lon", 1)
        keep = grams(far, 0, [send])
        targets = [(y, near) for y in range(y_count) for near in range(2)]
        rows = range(len(targets))
        open_chunks.append(
            (far, 0, [(targets, at, keep, rows, got, rows) for at in (0, cut)])
        )
        open_chunks, sent = exchange(open_chunks, far > 0)
    while open_chunks:
        open_chunks = [c for chunk in open_chunks for c in exchange([chunk], False)[0]]
    updated = analysis(
        list(parts.values()),
        holders * held * block_obs,
        state_pert.reshape(patches, fields, members, columns),
        state_mean.reshape(patches, fields, columns),
    )
    return updated.reshape(lon_patches, lat_patches, fields, members, columns)


def solution(mesh):
    in_specs = (
        P("lon", "lat", None, None, None),
        P("lon", "lat", None, None),
        P(("lon", "lat"), None, None),
        P(("lon", "lat"), None),
        P(("lon", "lat"), None),
        P(("lon", "lat"), None),
        P(("lon", "lat"), None),
        P("lon", "lat", None),
        P("lon", "lat"),
    )
    out_specs = P("lon", "lat", None, None, None)
    return jax.shard_map(
        on_device, mesh=mesh, in_specs=in_specs, out_specs=out_specs, check_vma=False
    )
```

```python
import functools

import jax
import jax.numpy as jnp
from jax import lax
from jax.experimental import pallas as pl
from jax.experimental.pallas import tpu as pltpu
from jax.sharding import PartitionSpec as P

PSIDE = 16
NS_ITERS = 5
LOC_SCALE = 48.0
EXT = 16
F32 = jnp.float32
BF16 = jnp.bfloat16
NT = (((1,), (1,)), ((), ()))


def halves(value):
    high = value.astype(BF16)
    return high, (value - high.astype(F32)).astype(BF16)


def request_table(block_list, block_count, holders, held_blocks):
    length = block_list.shape[2]
    slots = block_list.size
    per_owner = slots // holders
    used = lax.broadcasted_iota(jnp.int32, block_list.shape, 2) < block_count[:, :, None]
    wanted = jnp.where(used, block_list, -1).reshape(slots)
    holder = jnp.where(wanted < 0, holders, lax.div(wanted, held_blocks))
    order = jnp.arange(slots)
    before = (holder[:, None] == holder[None, :]) & (order[None, :] < order[:, None])
    rank = jnp.sum(before.astype(jnp.int32), axis=1)
    code = lax.div(order, length) * held_blocks + lax.rem(wanted, held_blocks)
    place = lax.broadcasted_iota(jnp.int32, (holders, per_owner + 2, 1), 1)
    asked = lax.broadcasted_iota(jnp.int32, (holders, per_owner + 2, 1), 0)
    entry = jnp.where(place == per_owner, 1, jnp.where(rank == place, code, 0))
    table = jnp.sum(jnp.where(holder == asked, entry, 0), axis=2)
    return table + jnp.where(place == per_owner + 1, asked, 0)[:, :, 0]


def stage_kernel(
    chunk,
    anom_hbm,
    innov_hbm,
    rinv_hbm,
    lon_hbm,
    lat_hbm,
    left_ref,
    rinv_ref,
    lon_ref,
    lat_ref,
    totals_ref,
    innov_ref,
    sems,
):
    held, members, block_obs = anom_hbm.shape
    pairs = [(rinv_hbm, rinv_ref), (innov_hbm, innov_ref)]
    for i in range(held // chunk):
        span = pl.ds(i * chunk, chunk)
        pairs.append((anom_hbm.at[span], left_ref.at[span, pl.ds(0, members), :]))
    pairs += [(lon_hbm, lon_ref), (lat_hbm, lat_ref)]
    copies = [pltpu.make_async_copy(a, b, sems.at[i]) for i, (a, b) in enumerate(pairs)]
    for copy in copies:
        copy.start()
    copies[0].wait()
    copies[1].wait()
    line = lax.broadcasted_iota(jnp.int32, (EXT, block_obs), 0)
    sums = jnp.zeros((8, block_obs), F32)
    for i, copy in enumerate(copies[2:-2]):
        copy.wait()

        def block(j, total, first=i * chunk):
            at = first + j
            values = left_ref[at, :members, :].astype(F32)
            squares = jnp.sum((values * values).reshape(members // 8, 8, block_obs), axis=0)
            innov = innov_ref[pl.ds(at, 1), :]
            high = innov.astype(BF16).astype(F32)
            rows = jnp.where(line == 0, high, jnp.where(line == 1, innov - high, 0.0))
            left_ref[at, members:, :] = rows.astype(BF16)
            return total + squares * rinv_ref[pl.ds(at, 1), :]

        sums = lax.fori_loop(0, chunk, block, sums, unroll=4)
    innovation = jnp.sum(rinv_ref[...] * innov_ref[...] * innov_ref[...], axis=0, keepdims=True)
    spread = jnp.sum(sums, axis=0, keepdims=True) / (members - 1)
    line = lax.broadcasted_iota(jnp.int32, (8, block_obs), 0)
    totals_ref[...] = jnp.where(line == 4, innovation, jnp.where(line == 5, spread, 0.0))
    copies[-2].wait()
    copies[-1].wait()


def stage(anom, innov, rinv, lon, lat):
    held, members, block_obs = anom.shape
    chunk = 16 if held % 16 == 0 else held
    operands = [pltpu.with_memory_space_constraint(v, pltpu.HBM) for v in (anom, innov, rinv, lon, lat)]
    return pl.pallas_call(
        functools.partial(stage_kernel, chunk),
        out_shape=[
            pltpu.VMEM((held, members + EXT, block_obs), BF16),
            pltpu.VMEM((held, block_obs), F32),
            pltpu.VMEM((held, block_obs), jnp.int32),
            pltpu.VMEM((held, block_obs), jnp.int32),
            pltpu.VMEM((8, block_obs), F32),
        ],
        in_specs=[pl.BlockSpec(memory_space=pltpu.HBM)] * 5,
        out_specs=[pl.BlockSpec(memory_space=pltpu.VMEM)] * 5,
        scratch_shapes=[
            pltpu.VMEM((held, block_obs), F32),
            pltpu.SemaphoreType.DMA((held // chunk + 4,)),
        ],
        compiler_params=pltpu.CompilerParams(vmem_limit_bytes=4 * 2**20),
        cost_estimate=pl.CostEstimate(flops=0, bytes_accessed=anom.size * 4, transcendentals=0),
        name="stage",
    )(*operands)


def gram_kernel(
    sizes,
    far,
    core,
    requests_ref,
    left_ref,
    rinv_ref,
    obs_lon_ref,
    obs_lat_ref,
    totals_ref,
    out_ref,
    acc_ref,
):
    patches, lat_patches, lon_patches, lat_devices, held, per_owner, grid_lon = sizes
    step = pl.program_id(0)
    me = requests_ref[0, per_owner + 1]
    distance = (2 * (step // 2) + core) * lat_devices + (2 * far + step % 2)
    target = me ^ distance
    lon_first = (target // lat_devices) * lon_patches
    lat_first = (target % lat_devices) * lat_patches
    members = left_ref.shape[2]
    acc_ref[...] = jnp.zeros_like(acc_ref)
    number = requests_ref[target, per_owner]

    products = []
    for entry in range(per_owner):
        code = requests_ref[target, entry]
        patch = code // held
        block = code % held
        centre_lon = (lon_first + patch // lat_patches) * (2 * PSIDE) + (PSIDE - 1)
        centre_lat = (lat_first + patch % lat_patches) * (2 * PSIDE) + (PSIDE - 1)
        row = pl.ds(block, 1)
        lon_gap = jnp.abs(2 * obs_lon_ref[row, :] - centre_lon)
        lon_gap = jnp.minimum(lon_gap, 2 * grid_lon - lon_gap)
        lat_gap = 2 * obs_lat_ref[row, :] - centre_lat
        square = (lon_gap * lon_gap + lat_gap * lat_gap).astype(F32)
        rinv = jnp.where(entry < number, rinv_ref[row, :], 0.0)
        weight = rinv * jnp.exp(square * (-1.0 / (8.0 * LOC_SCALE * LOC_SCALE)))
        left = left_ref[block]
        scaled = (left[:members].astype(F32) * weight).astype(BF16)
        product = lax.dot_general(left, scaled, NT, preferred_element_type=F32)
        products.append((patch, product[: members + 8]))
    for patch, product in products:
        acc_ref[patch] += product

    row = lax.broadcasted_iota(jnp.int32, (members, members), 0)
    column = lax.broadcasted_iota(jnp.int32, (members, members), 1)
    line = lax.broadcasted_iota(jnp.int32, (8, members), 0)
    for pair in range(patches // 2):
        first = acc_ref[2 * pair]
        second = acc_ref[2 * pair + 1]
        packed = jnp.where(row < column, first[:members], second[:members])
        out_ref[0, pair, :members, :] = packed.astype(BF16)
        rows = totals_ref[...]
        for place, values in ((0, first), (2, second)):
            diagonal = jnp.sum(
                jnp.where(row == column, values[:members], 0.0), axis=0, keepdims=True
            )
            projected = values[members : members + 1] + values[members + 1 : members + 2]
            rows = jnp.where(line == place, diagonal, rows)
            rows = jnp.where(line == place + 1, projected, rows)
        high = rows.astype(BF16).astype(F32)
        out_ref[0, pair, members:, :] = jnp.concatenate([high, rows - high], axis=0).astype(BF16)


def hold_kernel(table_hbm, held_ref, sem):
    copy = pltpu.make_async_copy(table_hbm, held_ref, sem)
    copy.start()
    copy.wait()


def hold(table):
    return pl.pallas_call(
        hold_kernel,
        out_shape=pltpu.SMEM(table.shape, table.dtype),
        in_specs=[pl.BlockSpec(memory_space=pl.ANY)],
        out_specs=pl.BlockSpec(memory_space=pltpu.SMEM),
        scratch_shapes=[pltpu.SemaphoreType.DMA(())],
        compiler_params=pltpu.CompilerParams(vmem_limit_bytes=2**20),
        name="hold",
    )(table)


def partial_grams(sizes, far, core, count, requests, staged):
    patches, per_owner = sizes[0], sizes[5]
    members = staged[0].shape[2]
    rows = members + EXT
    block = (1, patches // 2, rows, members)
    return pl.pallas_call(
        functools.partial(gram_kernel, sizes, far, core),
        out_shape=jax.ShapeDtypeStruct((count, *block[1:]), BF16),
        grid_spec=pltpu.PrefetchScalarGridSpec(
            num_scalar_prefetch=0,
            grid=(count,),
            in_specs=[pl.BlockSpec(memory_space=pltpu.SMEM)] + [pl.BlockSpec(memory_space=pltpu.VMEM)] * 5,
            out_specs=pl.BlockSpec(block, lambda i, *_: (i, 0, 0, 0)),
            scratch_shapes=[pltpu.VMEM((patches, members + 8, members), F32)],
        ),
        compiler_params=pltpu.CompilerParams(vmem_limit_bytes=8 * 2**20),
        cost_estimate=pl.CostEstimate(
            flops=count * per_owner * 100 * members**3, bytes_accessed=0, transcendentals=0
        ),
        name="partial_grams",
    )(requests, *staged)


def added(left, right):
    members = left.shape[-1]
    total = left.astype(F32) + right.astype(F32)
    rows = total[:, members : members + 8] + total[:, members + 8 :]
    high = rows.astype(BF16).astype(F32)
    rows = jnp.concatenate([high, rows - high], axis=1)
    return total[:, :members].astype(BF16), rows.astype(BF16)


def add_kernel(inputs, size, jobs, *refs):
    for left, left_row, right, right_row, at, out, row, place in jobs:
        out_ref = refs[inputs + out]
        members = out_ref.shape[-1]
        span, to = slice(at, at + size), slice(place, place + size)
        body, rows = added(refs[left][left_row, span], refs[right][right_row, span])
        out_ref[row, to, :members, :] = body
        out_ref[row, to, members:, :] = rows


def add_all(arrays, size, jobs, shapes, hides):
    inner = arrays[0].shape[2:]
    whole = pl.BlockSpec(memory_space=pltpu.VMEM)
    work = len(jobs) * size * inner[0] * inner[1]
    return pl.pallas_call(
        functools.partial(add_kernel, len(arrays), size, jobs),
        out_shape=[jax.ShapeDtypeStruct((*shape, *inner), BF16) for shape in shapes],
        in_specs=[whole] * len(arrays),
        out_specs=[whole] * len(shapes),
        compiler_params=pltpu.CompilerParams(vmem_limit_bytes=8 * 2**20),
        cost_estimate=pl.CostEstimate(flops=work * (10000 if hides else 4), bytes_accessed=work * 6, transcendentals=0),
        name="add_partials",
    )(*arrays)


def product(left, right):
    left_high, left_low = left
    right_high, right_low = right
    return jnp.dot(
        jnp.concatenate([left_high, left_low, left_high], axis=1),
        jnp.concatenate([right_high, right_high, right_low], axis=0),
        preferred_element_type=F32,
    )


def solve_group(parts, total_obs, first, count):
    members = parts[0].shape[-1]
    row = lax.broadcasted_iota(jnp.int32, (members, members), 0)
    column = lax.broadcasted_iota(jnp.int32, (members, members), 1)
    identity = (row == column).astype(F32)
    systems, projected = [], []
    for pair in range(count):
        total = parts[0][0, first + pair].astype(F32)
        for part in parts[1:]:
            total = total + part[0, first + pair].astype(F32)
        packed = total[:members]
        values = total[members : members + 8] + total[members + 8 :]
        flipped = packed.T
        innovation = jnp.sum(values[4:5], axis=1, keepdims=True)
        spread = jnp.sum(values[5:6], axis=1, keepdims=True)
        ridge = (members - 1) * (spread + total_obs) / innovation
        for place, full in (
            (0, jnp.where(row < column, packed, flipped)),
            (2, jnp.where(row > column, packed, flipped)),
        ):
            systems.append(jnp.where(row == column, values[place : place + 1] + ridge, full))
            projected.append(values[place + 1 : place + 2])
    scalings, roots = [], []
    for system in systems:
        squares = jnp.sum(system * system, axis=0, keepdims=True)
        scaling = jnp.sqrt(jnp.sum(squares, axis=1, keepdims=True))
        scalings.append(scaling)
        roots.append(system * (1.0 / scaling))
    factors = [1.5 * identity - 0.5 * root for root in roots]
    roots = [product(halves(f), halves(r)) for f, r in zip(factors, roots)]
    inverses = factors
    for iteration in range(1, NS_ITERS):
        split_roots = [halves(r) for r in roots]
        split_inverses = [halves(z) for z in inverses]
        factors = [
            halves(1.5 * identity - 0.5 * product(z, r))
            for z, r in zip(split_inverses, split_roots)
        ]
        if iteration < NS_ITERS - 1:
            both = [
                product(f, [jnp.concatenate([a, b], axis=1) for a, b in zip(r, z)])
                for f, r, z in zip(factors, split_roots, split_inverses)
            ]
            roots = [b[:, :members] for b in both]
            inverses = [b[:, members:] for b in both]
        else:
            inverses = [product(f, z) for f, z in zip(factors, split_inverses)]
    weights = []
    for scaling, inverse, values in zip(scalings, inverses, projected):
        inverse_sqrt = inverse * lax.rsqrt(scaling)
        inner = jnp.sum(inverse_sqrt * values, axis=1, keepdims=True)
        mean = jnp.sum(inverse_sqrt * inner, axis=0, keepdims=True)
        weights.append((jnp.sqrt(F32(members - 1)) * inverse_sqrt + mean).astype(BF16))
    return weights


def analysis_kernel(count, total_obs, group, *refs):
    parts, (pert_ref, mean_ref, out_ref, weights_ref) = refs[:count], refs[count:]
    step = pl.program_id(0)
    size, fields = pert_ref.shape[:2]
    now, before = lax.rem(step, 2), lax.rem(step + 1, 2)
    for patch in range(size):
        held = weights_ref[before, patch]
        for field in range(fields):
            change = jnp.dot(held, pert_ref[patch, field], preferred_element_type=F32)
            out_ref[patch, field] = change + mean_ref[patch, field : field + 1]
    groups = pl.num_programs(0) - 1
    first = jnp.minimum(step, groups - 1) * (group // 2)
    for patch, weights in enumerate(solve_group(parts, total_obs, first, group // 2)):
        weights_ref[now, patch] = weights


def analysis(parts, total_obs, pert, mean):
    patches, fields, members, columns = pert.shape
    group = patches // 2
    whole = pl.BlockSpec(memory_space=pltpu.VMEM)
    return pl.pallas_call(
        functools.partial(analysis_kernel, len(parts), total_obs, group),
        out_shape=jax.ShapeDtypeStruct(pert.shape, F32),
        grid=(patches // group + 1,),
        in_specs=[whole] * len(parts)
        + [
            pl.BlockSpec(
                (group, fields, members, columns), lambda i: (jnp.maximum(i - 1, 0), 0, 0, 0)
            ),
            pl.BlockSpec((group, fields, columns), lambda i: (jnp.maximum(i - 1, 0), 0, 0)),
        ],
        out_specs=pl.BlockSpec(
            (group, fields, members, columns), lambda i: (jnp.maximum(i - 1, 0), 0, 0, 0)
        ),
        scratch_shapes=[pltpu.VMEM((2, group, members, members), BF16)],
        compiler_params=pltpu.CompilerParams(vmem_limit_bytes=40 * 2**20),
        name="analysis",
    )(*parts, pert, mean)


def swap(value, axis, flip):
    size = lax.axis_size(axis)
    return lax.ppermute(value, axis, [(i, i ^ flip) for i in range(size)])


def on_device(
    state_pert, state_mean, obs_anom, innov, obs_rinv, obs_lon, obs_lat, block_list, block_count
):
    lon_devices, lat_devices = lax.axis_size("lon"), lax.axis_size("lat")
    holders = lon_devices * lat_devices
    lon_patches, lat_patches, fields, members, columns = state_pert.shape
    patches = lon_patches * lat_patches
    length = block_list.shape[2]
    held, _, block_obs = obs_anom.shape
    per_owner = patches * length // holders
    table = request_table(block_list, block_count, holders, held)
    requests = lax.all_to_all(table, ("lon", "lat"), split_axis=0, concat_axis=0, tiled=True)

    requests, observed = lax.optimization_barrier(
        (requests, (obs_anom, innov, obs_rinv, obs_lon, obs_lat))
    )
    requests = hold(requests)
    staged = stage(*observed)
    sizes = (
        patches,
        lat_patches,
        lon_patches,
        lat_devices,
        held,
        per_owner,
        lon_devices * lon_patches * PSIDE,
    )
    y_count = lon_devices // 2
    pairs = patches // 2
    cut = pairs // 2

    def grams(far, core, after):
        rows, _ = lax.optimization_barrier((staged[-1], after))
        return partial_grams(sizes, far, core, lon_devices, requests, [*staged[:-1], rows])

    along_lon = []
    while 2 ** (len(along_lon) + 1) <= y_count:
        along_lon.append(("lon", y_count >> len(along_lon)))
    routes = [[("lat", 1), *along_lon], [*along_lon[:1], ("lat", 1), *along_lon[1:]]]

    def leaves(target, axis, flip):
        y, near = target
        return near == 1 if axis == "lat" else (2 * y) & flip != 0

    parts, open_chunks, on_their_way = {}, [], [[], [], []]

    def exchange(chunks, merge, behind=(), hides=False):
        arrays, jobs, lengths, where = [], [], {}, {}

        def slot(array):
            for i, known in enumerate(arrays):
                if known is array:
                    return i
            arrays.append(array)
            return len(arrays) - 1

        def take(key):
            row = lengths.get(key, 0)
            lengths[key] = row + 1
            return row

        for far, level, parcels in chunks:
            for half, (targets, at, keep, keep_rows, got, got_rows) in enumerate(parcels):
                for target, keep_row, got_row in zip(targets, keep_rows, got_rows):
                    place = 0
                    if level == len(routes[half]):
                        key, row, place = ("total", far), 0, half * cut
                        lengths[key] = 1
                    elif leaves(target, *routes[half][level]):
                        key = ("send", *routes[half][level], 0 if merge else level)
                        row = take(key)
                    else:
                        key = ("keep", far, half)
                        row = take(key)
                    where[far, half, target] = key, row
                    jobs.append((slot(keep), keep_row, slot(got), got_row, at, key, row, place))
        keys = sorted(lengths, key=lambda k: (k[0], -k[-1] if k[0] == "send" else 0))
        jobs = [(*job[:5], keys.index(job[5]), *job[6:]) for job in jobs]
        shapes = [(lengths[k], pairs if k[0] == "total" else cut) for k in keys]
        due = on_their_way.pop(0)
        on_their_way.append([])
        arrays[0], arrived, _ = lax.optimization_barrier(
            (arrays[0], [parts[far] for far in due], list(behind))
        )
        parts.update(zip(due, arrived))
        outs = dict(zip(keys, add_all(arrays, cut, jobs, shapes, hides)))
        gots = {k: swap(v, k[1], k[2]) for k, v in outs.items() if k[0] == "send"}
        still = []
        for far, level, parcels in chunks:
            if level == len(routes[0]):
                total = outs["total", far]
                parts[far] = swap(total, "lat", 2 * far) if far else total
                if far and merge:
                    on_their_way[2].append(far)
                continue
            following = []
            for half, (targets, *_) in enumerate(parcels):
                staying = [t for t in targets if not leaves(t, *routes[half][level])]
                leaving = [t for t in targets if leaves(t, *routes[half][level])]
                keep_rows = [where[far, half, t][1] for t in staying]
                got_rows = [where[far, half, t][1] for t in leaving]
                got = gots[where[far, half, leaving[0]][0]]
                following.append((staying, 0, outs["keep", far, half], keep_rows, got, got_rows))
            still.append((far, level + 1, following))
        return still, [v for k, v in outs.items() if k[0] != "keep"]

    sent = []
    for far in reversed(range(lat_devices // 2)):
        send = grams(far, 1, sent)
        got = swap(send, "lon", 1)
        keep = grams(far, 0, [send])
        targets = [(y, near) for y in range(y_count) for near in range(2)]
        rows = range(len(targets))
        if not far:
            open_chunks, sent = exchange(open_chunks, False, behind=[keep])
            keep, _ = lax.optimization_barrier((keep, sent))
        newest = (far, 0, [(targets, at, keep, rows, got, rows) for at in (0, cut)])
        if far:
            open_chunks, sent = exchange([*open_chunks, newest], True)
        else:
            open_chunks += exchange([newest], False, hides=False)[0]
    while open_chunks:
        open_chunks = [c for chunk in open_chunks for c in exchange([chunk], False, hides=len(open_chunks) > 1 and chunk is open_chunks[0])[0]]
    updated = analysis(
        list(parts.values()),
        holders * held * block_obs,
        state_pert.reshape(patches, fields, members, columns),
        state_mean.reshape(patches, fields, columns),
    )
    return updated.reshape(lon_patches, lat_patches, fields, members, columns)


def solution(mesh):
    in_specs = (
        P("lon", "lat", None, None, None),
        P("lon", "lat", None, None),
        P(("lon", "lat"), None, None),
        P(("lon", "lat"), None),
        P(("lon", "lat"), None),
        P(("lon", "lat"), None),
        P(("lon", "lat"), None),
        P("lon", "lat", None),
        P("lon", "lat"),
    )
    out_specs = P("lon", "lat", None, None, None)
    return jax.shard_map(
        on_device, mesh=mesh, in_specs=in_specs, out_specs=out_specs, check_vma=False
    )
```

```python
import functools

import jax
import jax.numpy as jnp
from jax import lax
from jax.experimental import pallas as pl
from jax.experimental.pallas import tpu as pltpu
from jax.sharding import PartitionSpec as P

PSIDE = 16
NS_ITERS = 5
LOC_SCALE = 48.0
EXT = 16
F32 = jnp.float32
BF16 = jnp.bfloat16
NT = (((1,), (1,)), ((), ()))


def halves(value):
    high = value.astype(BF16)
    return high, (value - high.astype(F32)).astype(BF16)


def request_table(block_list, block_count, holders, held_blocks):
    length = block_list.shape[2]
    slots = block_list.size
    per_owner = slots // holders
    used = lax.broadcasted_iota(jnp.int32, block_list.shape, 2) < block_count[:, :, None]
    wanted = jnp.where(used, block_list, -1).reshape(slots)
    holder = jnp.where(wanted < 0, holders, lax.div(wanted, held_blocks))
    order = jnp.arange(slots)
    before = (holder[:, None] == holder[None, :]) & (order[None, :] < order[:, None])
    rank = jnp.sum(before.astype(jnp.int32), axis=1)
    code = lax.div(order, length) * held_blocks + lax.rem(wanted, held_blocks)
    place = lax.broadcasted_iota(jnp.int32, (holders, per_owner + 2, 1), 1)
    asked = lax.broadcasted_iota(jnp.int32, (holders, per_owner + 2, 1), 0)
    entry = jnp.where(place == per_owner, 1, jnp.where(rank == place, code, 0))
    table = jnp.sum(jnp.where(holder == asked, entry, 0), axis=2)
    return table + jnp.where(place == per_owner + 1, asked, 0)[:, :, 0]


def stage_kernel(
    chunk,
    anom_hbm,
    innov_hbm,
    rinv_hbm,
    lon_hbm,
    lat_hbm,
    table_hbm,
    left_ref,
    rinv_ref,
    lon_ref,
    lat_ref,
    totals_ref,
    table_ref,
    innov_ref,
    sems,
):
    held, members, block_obs = anom_hbm.shape
    pairs = [(rinv_hbm, rinv_ref), (innov_hbm, innov_ref)]
    for i in range(held // chunk):
        span = pl.ds(i * chunk, chunk)
        pairs.append((anom_hbm.at[span], left_ref.at[span, pl.ds(0, members), :]))
    pairs += [(lon_hbm, lon_ref), (lat_hbm, lat_ref), (table_hbm, table_ref)]
    copies = [pltpu.make_async_copy(a, b, sems.at[i]) for i, (a, b) in enumerate(pairs)]
    for copy in copies:
        copy.start()
    copies[0].wait()
    copies[1].wait()
    line = lax.broadcasted_iota(jnp.int32, (EXT, block_obs), 0)
    sums = jnp.zeros((8, block_obs), F32)
    for i, copy in enumerate(copies[2:-3]):
        copy.wait()

        def block(j, total, first=i * chunk):
            at = first + j
            values = left_ref[at, :members, :].astype(F32)
            squares = jnp.sum((values * values).reshape(members // 8, 8, block_obs), axis=0)
            innov = innov_ref[pl.ds(at, 1), :]
            high = innov.astype(BF16).astype(F32)
            rows = jnp.where(line == 0, high, jnp.where(line == 1, innov - high, 0.0))
            left_ref[at, members:, :] = rows.astype(BF16)
            return total + squares * rinv_ref[pl.ds(at, 1), :]

        sums = lax.fori_loop(0, chunk, block, sums, unroll=4)
    innovation = jnp.sum(rinv_ref[...] * innov_ref[...] * innov_ref[...], axis=0, keepdims=True)
    spread = jnp.sum(sums, axis=0, keepdims=True) / (members - 1)
    line = lax.broadcasted_iota(jnp.int32, (8, block_obs), 0)
    totals_ref[...] = jnp.where(line == 4, innovation, jnp.where(line == 5, spread, 0.0))
    for copy in copies[-3:]:
        copy.wait()


def stage(anom, innov, rinv, lon, lat, table):
    held, members, block_obs = anom.shape
    chunk = 16 if held % 16 == 0 else held
    operands = [pltpu.with_memory_space_constraint(v, pltpu.HBM) for v in (anom, innov, rinv, lon, lat)]
    return pl.pallas_call(
        functools.partial(stage_kernel, chunk),
        out_shape=[
            pltpu.VMEM((held, members + EXT, block_obs), BF16),
            pltpu.VMEM((held, block_obs), F32),
            pltpu.VMEM((held, block_obs), jnp.int32),
            pltpu.VMEM((held, block_obs), jnp.int32),
            pltpu.VMEM((8, block_obs), F32),
            pltpu.SMEM(table.shape, table.dtype),
        ],
        in_specs=[pl.BlockSpec(memory_space=pltpu.HBM)] * 5 + [pl.BlockSpec(memory_space=pl.ANY)],
        out_specs=[pl.BlockSpec(memory_space=pltpu.VMEM)] * 5 + [pl.BlockSpec(memory_space=pltpu.SMEM)],
        scratch_shapes=[
            pltpu.VMEM((held, block_obs), F32),
            pltpu.SemaphoreType.DMA((held // chunk + 5,)),
        ],
        compiler_params=pltpu.CompilerParams(vmem_limit_bytes=4 * 2**20),
        cost_estimate=pl.CostEstimate(flops=0, bytes_accessed=anom.size * 4, transcendentals=0),
        name="stage",
    )(*operands, table)


def gram_kernel(
    sizes,
    far,
    core,
    requests_ref,
    left_ref,
    rinv_ref,
    obs_lon_ref,
    obs_lat_ref,
    totals_ref,
    out_ref,
    acc_ref,
):
    patches, lat_patches, lon_patches, lat_devices, held, per_owner, grid_lon = sizes
    step = pl.program_id(0)
    me = requests_ref[0, per_owner + 1]
    distance = (2 * (step // 2) + core) * lat_devices + (2 * far + step % 2)
    target = me ^ distance
    lon_first = (target // lat_devices) * lon_patches
    lat_first = (target % lat_devices) * lat_patches
    members = left_ref.shape[2]
    acc_ref[...] = jnp.zeros_like(acc_ref)
    number = requests_ref[target, per_owner]

    products = []
    for entry in range(per_owner):
        code = requests_ref[target, entry]
        patch = code // held
        block = code % held
        centre_lon = (lon_first + patch // lat_patches) * (2 * PSIDE) + (PSIDE - 1)
        centre_lat = (lat_first + patch % lat_patches) * (2 * PSIDE) + (PSIDE - 1)
        row = pl.ds(block, 1)
        lon_gap = jnp.abs(2 * obs_lon_ref[row, :] - centre_lon)
        lon_gap = jnp.minimum(lon_gap, 2 * grid_lon - lon_gap)
        lat_gap = 2 * obs_lat_ref[row, :] - centre_lat
        square = (lon_gap * lon_gap + lat_gap * lat_gap).astype(F32)
        rinv = jnp.where(entry < number, rinv_ref[row, :], 0.0)
        weight = rinv * jnp.exp(square * (-1.0 / (8.0 * LOC_SCALE * LOC_SCALE)))
        left = left_ref[block]
        scaled = (left[:members].astype(F32) * weight).astype(BF16)
        product = lax.dot_general(left, scaled, NT, preferred_element_type=F32)
        products.append((patch, product[: members + 8]))
    for patch, product in products:
        acc_ref[patch] += product

    row = lax.broadcasted_iota(jnp.int32, (members, members), 0)
    column = lax.broadcasted_iota(jnp.int32, (members, members), 1)
    line = lax.broadcasted_iota(jnp.int32, (8, members), 0)
    for pair in range(patches // 2):
        first = acc_ref[2 * pair]
        second = acc_ref[2 * pair + 1]
        packed = jnp.where(row < column, first[:members], second[:members])
        out_ref[0, pair, :members, :] = packed.astype(BF16)
        rows = totals_ref[...]
        for place, values in ((0, first), (2, second)):
            diagonal = jnp.sum(
                jnp.where(row == column, values[:members], 0.0), axis=0, keepdims=True
            )
            projected = values[members : members + 1] + values[members + 1 : members + 2]
            rows = jnp.where(line == place, diagonal, rows)
            rows = jnp.where(line == place + 1, projected, rows)
        high = rows.astype(BF16).astype(F32)
        out_ref[0, pair, members:, :] = jnp.concatenate([high, rows - high], axis=0).astype(BF16)


def partial_grams(sizes, far, core, count, requests, staged):
    patches, per_owner = sizes[0], sizes[5]
    members = staged[0].shape[2]
    rows = members + EXT
    block = (1, patches // 2, rows, members)
    return pl.pallas_call(
        functools.partial(gram_kernel, sizes, far, core),
        out_shape=jax.ShapeDtypeStruct((count, *block[1:]), BF16),
        grid_spec=pltpu.PrefetchScalarGridSpec(
            num_scalar_prefetch=0,
            grid=(count,),
            in_specs=[pl.BlockSpec(memory_space=pltpu.SMEM)] + [pl.BlockSpec(memory_space=pltpu.VMEM)] * 5,
            out_specs=pl.BlockSpec(block, lambda i, *_: (i, 0, 0, 0)),
            scratch_shapes=[pltpu.VMEM((patches, members + 8, members), F32)],
        ),
        compiler_params=pltpu.CompilerParams(vmem_limit_bytes=8 * 2**20),
        cost_estimate=pl.CostEstimate(
            flops=count * per_owner * 100 * members**3, bytes_accessed=0, transcendentals=0
        ),
        name="partial_grams",
    )(requests, *staged)


def added(left, right):
    members = left.shape[-1]
    total = left.astype(F32) + right.astype(F32)
    rows = total[:, members : members + 8] + total[:, members + 8 :]
    high = rows.astype(BF16).astype(F32)
    rows = jnp.concatenate([high, rows - high], axis=1)
    return total[:, :members].astype(BF16), rows.astype(BF16)


def add_kernel(inputs, size, jobs, *refs):
    for left, left_row, right, right_row, at, out, row, place in jobs:
        out_ref = refs[inputs + out]
        members = out_ref.shape[-1]
        span, to = slice(at, at + size), slice(place, place + size)
        body, rows = added(refs[left][left_row, span], refs[right][right_row, span])
        out_ref[row, to, :members, :] = body
        out_ref[row, to, members:, :] = rows


def add_all(arrays, size, jobs, shapes, hides):
    inner = arrays[0].shape[2:]
    whole = pl.BlockSpec(memory_space=pltpu.VMEM)
    work = len(jobs) * size * inner[0] * inner[1]
    return pl.pallas_call(
        functools.partial(add_kernel, len(arrays), size, jobs),
        out_shape=[jax.ShapeDtypeStruct((*shape, *inner), BF16) for shape in shapes],
        in_specs=[whole] * len(arrays),
        out_specs=[whole] * len(shapes),
        compiler_params=pltpu.CompilerParams(vmem_limit_bytes=8 * 2**20),
        cost_estimate=pl.CostEstimate(flops=work * (10000 if hides else 4), bytes_accessed=work * 6, transcendentals=0),
        name="add_partials",
    )(*arrays)


def product(left, right):
    left_high, left_low = left
    right_high, right_low = right
    return jnp.dot(
        jnp.concatenate([left_high, left_low, left_high], axis=1),
        jnp.concatenate([right_high, right_high, right_low], axis=0),
        preferred_element_type=F32,
    )


def solve_group(parts, total_obs, first, count):
    members = parts[0].shape[-1]
    row = lax.broadcasted_iota(jnp.int32, (members, members), 0)
    column = lax.broadcasted_iota(jnp.int32, (members, members), 1)
    identity = (row == column).astype(F32)
    systems, projected = [], []
    for pair in range(count):
        total = parts[0][0, first + pair].astype(F32)
        for part in parts[1:]:
            total = total + part[0, first + pair].astype(F32)
        packed = total[:members]
        values = total[members : members + 8] + total[members + 8 :]
        flipped = packed.T
        innovation = jnp.sum(values[4:5], axis=1, keepdims=True)
        spread = jnp.sum(values[5:6], axis=1, keepdims=True)
        ridge = (members - 1) * (spread + total_obs) / innovation
        for place, full in (
            (0, jnp.where(row < column, packed, flipped)),
            (2, jnp.where(row > column, packed, flipped)),
        ):
            systems.append(jnp.where(row == column, values[place : place + 1] + ridge, full))
            projected.append(values[place + 1 : place + 2])
    scalings, roots = [], []
    for system in systems:
        squares = jnp.sum(system * system, axis=0, keepdims=True)
        scaling = jnp.sqrt(jnp.sum(squares, axis=1, keepdims=True))
        scalings.append(scaling)
        roots.append(system * (1.0 / scaling))
    factors = [1.5 * identity - 0.5 * root for root in roots]
    roots = [product(halves(f), halves(r)) for f, r in zip(factors, roots)]
    inverses = factors
    for iteration in range(1, NS_ITERS):
        split_roots = [halves(r) for r in roots]
        split_inverses = [halves(z) for z in inverses]
        factors = [
            halves(1.5 * identity - 0.5 * product(z, r))
            for z, r in zip(split_inverses, split_roots)
        ]
        if iteration < NS_ITERS - 1:
            both = [
                product(f, [jnp.concatenate([a, b], axis=1) for a, b in zip(r, z)])
                for f, r, z in zip(factors, split_roots, split_inverses)
            ]
            roots = [b[:, :members] for b in both]
            inverses = [b[:, members:] for b in both]
        else:
            inverses = [product(f, z) for f, z in zip(factors, split_inverses)]
    weights = []
    for scaling, inverse, values in zip(scalings, inverses, projected):
        inverse_sqrt = inverse * lax.rsqrt(scaling)
        inner = jnp.sum(inverse_sqrt * values, axis=1, keepdims=True)
        mean = jnp.sum(inverse_sqrt * inner, axis=0, keepdims=True)
        weights.append((jnp.sqrt(F32(members - 1)) * inverse_sqrt + mean).astype(BF16))
    return weights


def analysis_kernel(count, total_obs, group, *refs):
    parts, (pert_ref, mean_ref, out_ref, weights_ref) = refs[:count], refs[count:]
    step = pl.program_id(0)
    size, fields = pert_ref.shape[:2]
    now, before = lax.rem(step, 2), lax.rem(step + 1, 2)
    for patch in range(size):
        held = weights_ref[before, patch]
        for field in range(fields):
            change = jnp.dot(held, pert_ref[patch, field], preferred_element_type=F32)
            out_ref[patch, field] = change + mean_ref[patch, field : field + 1]
    groups = pl.num_programs(0) - 1
    first = jnp.minimum(step, groups - 1) * (group // 2)
    for patch, weights in enumerate(solve_group(parts, total_obs, first, group // 2)):
        weights_ref[now, patch] = weights


def analysis(parts, total_obs, pert, mean):
    patches, fields, members, columns = pert.shape
    group = patches // 2
    whole = pl.BlockSpec(memory_space=pltpu.VMEM)
    return pl.pallas_call(
        functools.partial(analysis_kernel, len(parts), total_obs, group),
        out_shape=jax.ShapeDtypeStruct(pert.shape, F32),
        grid=(patches // group + 1,),
        in_specs=[whole] * len(parts)
        + [
            pl.BlockSpec(
                (group, fields, members, columns), lambda i: (jnp.maximum(i - 1, 0), 0, 0, 0)
            ),
            pl.BlockSpec((group, fields, columns), lambda i: (jnp.maximum(i - 1, 0), 0, 0)),
        ],
        out_specs=pl.BlockSpec(
            (group, fields, members, columns), lambda i: (jnp.maximum(i - 1, 0), 0, 0, 0)
        ),
        scratch_shapes=[pltpu.VMEM((2, group, members, members), BF16)],
        compiler_params=pltpu.CompilerParams(vmem_limit_bytes=40 * 2**20),
        name="analysis",
    )(*parts, pert, mean)


def swap(value, axis, flip):
    size = lax.axis_size(axis)
    return lax.ppermute(value, axis, [(i, i ^ flip) for i in range(size)])


def on_device(
    state_pert, state_mean, obs_anom, innov, obs_rinv, obs_lon, obs_lat, block_list, block_count
):
    lon_devices, lat_devices = lax.axis_size("lon"), lax.axis_size("lat")
    holders = lon_devices * lat_devices
    lon_patches, lat_patches, fields, members, columns = state_pert.shape
    patches = lon_patches * lat_patches
    length = block_list.shape[2]
    held, _, block_obs = obs_anom.shape
    per_owner = patches * length // holders
    table = request_table(block_list, block_count, holders, held)
    requests = lax.all_to_all(table, ("lon", "lat"), split_axis=0, concat_axis=0, tiled=True)

    requests, observed = lax.optimization_barrier(
        (requests, (obs_anom, innov, obs_rinv, obs_lon, obs_lat))
    )
    *staged, requests = stage(*observed, requests)
    sizes = (
        patches,
        lat_patches,
        lon_patches,
        lat_devices,
        held,
        per_owner,
        lon_devices * lon_patches * PSIDE,
    )
    y_count = lon_devices // 2
    pairs = patches // 2
    cut = pairs // 2

    def grams(far, core, after):
        rows, _ = lax.optimization_barrier((staged[-1], after))
        return partial_grams(sizes, far, core, lon_devices, requests, [*staged[:-1], rows])

    along_lon = []
    while 2 ** (len(along_lon) + 1) <= y_count:
        along_lon.append(("lon", y_count >> len(along_lon)))
    routes = [[("lat", 1), *along_lon], [*along_lon[:1], ("lat", 1), *along_lon[1:]]]

    def leaves(target, axis, flip):
        y, near = target
        return near == 1 if axis == "lat" else (2 * y) & flip != 0

    parts, open_chunks, on_their_way = {}, [], [[], [], []]

    def exchange(chunks, merge, behind=(), hides=False):
        arrays, jobs, lengths, where = [], [], {}, {}

        def slot(array):
            for i, known in enumerate(arrays):
                if known is array:
                    return i
            arrays.append(array)
            return len(arrays) - 1

        def take(key):
            row = lengths.get(key, 0)
            lengths[key] = row + 1
            return row

        for far, level, parcels in chunks:
            for half, (targets, at, keep, keep_rows, got, got_rows) in enumerate(parcels):
                for target, keep_row, got_row in zip(targets, keep_rows, got_rows):
                    place = 0
                    if level == len(routes[half]):
                        key, row, place = ("total", far), 0, half * cut
                        lengths[key] = 1
                    elif leaves(target, *routes[half][level]):
                        key = ("send", *routes[half][level], 0 if merge else level)
                        row = take(key)
                    else:
                        key = ("keep", far, half)
                        row = take(key)
                    where[far, half, target] = key, row
                    jobs.append((slot(keep), keep_row, slot(got), got_row, at, key, row, place))
        keys = sorted(lengths, key=lambda k: (k[0], -k[-1] if k[0] == "send" else 0))
        jobs = [(*job[:5], keys.index(job[5]), *job[6:]) for job in jobs]
        shapes = [(lengths[k], pairs if k[0] == "total" else cut) for k in keys]
        due = on_their_way.pop(0)
        on_their_way.append([])
        arrays[0], arrived, _ = lax.optimization_barrier(
            (arrays[0], [parts[far] for far in due], list(behind))
        )
        parts.update(zip(due, arrived))
        outs = dict(zip(keys, add_all(arrays, cut, jobs, shapes, hides)))
        gots = {k: swap(v, k[1], k[2]) for k, v in outs.items() if k[0] == "send"}
        still = []
        for far, level, parcels in chunks:
            if level == len(routes[0]):
                total = outs["total", far]
                parts[far] = swap(total, "lat", 2 * far) if far else total
                if far and merge:
                    on_their_way[2].append(far)
                continue
            following = []
            for half, (targets, *_) in enumerate(parcels):
                staying = [t for t in targets if not leaves(t, *routes[half][level])]
                leaving = [t for t in targets if leaves(t, *routes[half][level])]
                keep_rows = [where[far, half, t][1] for t in staying]
                got_rows = [where[far, half, t][1] for t in leaving]
                got = gots[where[far, half, leaving[0]][0]]
                following.append((staying, 0, outs["keep", far, half], keep_rows, got, got_rows))
            still.append((far, level + 1, following))
        return still, [v for k, v in outs.items() if k[0] != "keep"]

    sent = []
    for far in reversed(range(lat_devices // 2)):
        send = grams(far, 1, sent)
        got = swap(send, "lon", 1)
        keep = grams(far, 0, [send])
        targets = [(y, near) for y in range(y_count) for near in range(2)]
        rows = range(len(targets))
        if not far:
            open_chunks, sent = exchange(open_chunks, False, behind=[keep])
            keep, _ = lax.optimization_barrier((keep, sent))
        newest = (far, 0, [(targets, at, keep, rows, got, rows) for at in (0, cut)])
        if far:
            open_chunks, sent = exchange([*open_chunks, newest], True)
        else:
            open_chunks += exchange([newest], False, hides=False)[0]
    while open_chunks:
        open_chunks = [c for chunk in open_chunks for c in exchange([chunk], False, hides=len(open_chunks) > 1 and chunk is open_chunks[0])[0]]
    updated = analysis(
        list(parts.values()),
        holders * held * block_obs,
        state_pert.reshape(patches, fields, members, columns),
        state_mean.reshape(patches, fields, columns),
    )
    return updated.reshape(lon_patches, lat_patches, fields, members, columns)


def solution(mesh):
    in_specs = (
        P("lon", "lat", None, None, None),
        P("lon", "lat", None, None),
        P(("lon", "lat"), None, None),
        P(("lon", "lat"), None),
        P(("lon", "lat"), None),
        P(("lon", "lat"), None),
        P(("lon", "lat"), None),
        P("lon", "lat", None),
        P("lon", "lat"),
    )
    out_specs = P("lon", "lat", None, None, None)
    return jax.shard_map(
        on_device, mesh=mesh, in_specs=in_specs, out_specs=out_specs, check_vma=False
    )
```

```python
import functools

import jax
import jax.numpy as jnp
from jax import lax
from jax.experimental import pallas as pl
from jax.experimental.pallas import tpu as pltpu
from jax.sharding import PartitionSpec as P

PSIDE = 16
NS_ITERS = 5
LOC_SCALE = 48.0
EXT = 16
F32 = jnp.float32
BF16 = jnp.bfloat16
NT = (((1,), (1,)), ((), ()))


def halves(value):
    high = value.astype(BF16)
    return high, (value - high.astype(F32)).astype(BF16)


def request_table(block_list, block_count, holders, held_blocks):
    length = block_list.shape[2]
    slots = block_list.size
    per_owner = slots // holders
    used = lax.broadcasted_iota(jnp.int32, block_list.shape, 2) < block_count[:, :, None]
    wanted = jnp.where(used, block_list, -1).reshape(slots)
    holder = jnp.where(wanted < 0, holders, lax.div(wanted, held_blocks))
    order = jnp.arange(slots)
    before = (holder[:, None] == holder[None, :]) & (order[None, :] < order[:, None])
    rank = jnp.sum(before.astype(jnp.int32), axis=1)
    code = lax.div(order, length) * held_blocks + lax.rem(wanted, held_blocks)
    place = lax.broadcasted_iota(jnp.int32, (holders, per_owner + 2, 1), 1)
    asked = lax.broadcasted_iota(jnp.int32, (holders, per_owner + 2, 1), 0)
    entry = jnp.where(place == per_owner, 1, jnp.where(rank == place, code, 0))
    table = jnp.sum(jnp.where(holder == asked, entry, 0), axis=2)
    return table + jnp.where(place == per_owner + 1, asked, 0)[:, :, 0]


def stage_kernel(
    chunk,
    anom_hbm,
    innov_hbm,
    rinv_hbm,
    lon_hbm,
    lat_hbm,
    table_hbm,
    left_ref,
    rinv_ref,
    lon_ref,
    lat_ref,
    totals_ref,
    table_ref,
    innov_ref,
    sems,
):
    held, members, block_obs = anom_hbm.shape
    pairs = [(rinv_hbm, rinv_ref), (innov_hbm, innov_ref)]
    for i in range(held // chunk):
        span = pl.ds(i * chunk, chunk)
        pairs.append((anom_hbm.at[span], left_ref.at[span, pl.ds(0, members), :]))
    pairs += [(lon_hbm, lon_ref), (lat_hbm, lat_ref), (table_hbm, table_ref)]
    copies = [pltpu.make_async_copy(a, b, sems.at[i]) for i, (a, b) in enumerate(pairs)]
    for copy in copies:
        copy.start()
    copies[0].wait()
    copies[1].wait()
    line = lax.broadcasted_iota(jnp.int32, (EXT, block_obs), 0)
    sums = jnp.zeros((8, block_obs), F32)
    for i, copy in enumerate(copies[2:-3]):
        copy.wait()

        def block(j, total, first=i * chunk):
            at = first + j
            values = left_ref[at, :members, :].astype(F32)
            squares = jnp.sum((values * values).reshape(members // 8, 8, block_obs), axis=0)
            innov = innov_ref[pl.ds(at, 1), :]
            high = innov.astype(BF16).astype(F32)
            rows = jnp.where(line == 0, high, jnp.where(line == 1, innov - high, 0.0))
            left_ref[at, members:, :] = rows.astype(BF16)
            return total + squares * rinv_ref[pl.ds(at, 1), :]

        sums = lax.fori_loop(0, chunk, block, sums, unroll=4)
    innovation = jnp.sum(rinv_ref[...] * innov_ref[...] * innov_ref[...], axis=0, keepdims=True)
    spread = jnp.sum(sums, axis=0, keepdims=True) / (members - 1)
    line = lax.broadcasted_iota(jnp.int32, (8, block_obs), 0)
    totals_ref[...] = jnp.where(line == 4, innovation, jnp.where(line == 5, spread, 0.0))
    for copy in copies[-3:]:
        copy.wait()


def stage(anom, innov, rinv, lon, lat, table):
    held, members, block_obs = anom.shape
    chunk = 16 if held % 16 == 0 else held
    operands = [pltpu.with_memory_space_constraint(v, pltpu.HBM) for v in (anom, innov, rinv, lon, lat)]
    return pl.pallas_call(
        functools.partial(stage_kernel, chunk),
        out_shape=[
            pltpu.VMEM((held, members + EXT, block_obs), BF16),
            pltpu.VMEM((held, block_obs), F32),
            pltpu.VMEM((held, block_obs), jnp.int32),
            pltpu.VMEM((held, block_obs), jnp.int32),
            pltpu.VMEM((8, block_obs), F32),
            pltpu.SMEM(table.shape, table.dtype),
        ],
        in_specs=[pl.BlockSpec(memory_space=pltpu.HBM)] * 5 + [pl.BlockSpec(memory_space=pl.ANY)],
        out_specs=[pl.BlockSpec(memory_space=pltpu.VMEM)] * 5 + [pl.BlockSpec(memory_space=pltpu.SMEM)],
        scratch_shapes=[
            pltpu.VMEM((held, block_obs), F32),
            pltpu.SemaphoreType.DMA((held // chunk + 5,)),
        ],
        compiler_params=pltpu.CompilerParams(vmem_limit_bytes=4 * 2**20),
        cost_estimate=pl.CostEstimate(flops=0, bytes_accessed=anom.size * 4, transcendentals=0),
        name="stage",
    )(*operands, table)


def gram_kernel(
    sizes,
    far,
    core,
    requests_ref,
    left_ref,
    rinv_ref,
    obs_lon_ref,
    obs_lat_ref,
    totals_ref,
    out_ref,
    acc_ref,
):
    patches, lat_patches, lon_patches, lat_devices, held, per_owner, grid_lon = sizes
    step = pl.program_id(0)
    me = requests_ref[0, per_owner + 1]
    distance = (2 * (step // 2) + core) * lat_devices + (2 * far + step % 2)
    target = me ^ distance
    lon_first = (target // lat_devices) * lon_patches
    lat_first = (target % lat_devices) * lat_patches
    members = left_ref.shape[2]
    acc_ref[...] = jnp.zeros_like(acc_ref)
    number = requests_ref[target, per_owner]

    products = []
    for entry in range(per_owner):
        code = requests_ref[target, entry]
        patch = code // held
        block = code % held
        centre_lon = (lon_first + patch // lat_patches) * (2 * PSIDE) + (PSIDE - 1)
        centre_lat = (lat_first + patch % lat_patches) * (2 * PSIDE) + (PSIDE - 1)
        row = pl.ds(block, 1)
        lon_gap = jnp.abs(2 * obs_lon_ref[row, :] - centre_lon)
        lon_gap = jnp.minimum(lon_gap, 2 * grid_lon - lon_gap)
        lat_gap = 2 * obs_lat_ref[row, :] - centre_lat
        square = (lon_gap * lon_gap + lat_gap * lat_gap).astype(F32)
        rinv = jnp.where(entry < number, rinv_ref[row, :], 0.0)
        weight = rinv * jnp.exp(square * (-1.0 / (8.0 * LOC_SCALE * LOC_SCALE)))
        left = left_ref[block]
        scaled = (left[:members].astype(F32) * weight).astype(BF16)
        product = lax.dot_general(left, scaled, NT, preferred_element_type=F32)
        products.append((patch, product[: members + 8]))
    for patch, product in products:
        acc_ref[patch] += product

    row = lax.broadcasted_iota(jnp.int32, (members, members), 0)
    column = lax.broadcasted_iota(jnp.int32, (members, members), 1)
    line = lax.broadcasted_iota(jnp.int32, (8, members), 0)
    lane = lax.broadcasted_iota(jnp.int32, (8, members), 1)
    for pair in range(patches // 2):
        first = acc_ref[2 * pair]
        second = acc_ref[2 * pair + 1]
        packed = jnp.where(row < column, first[:members], second[:members])
        out_ref[0, pair, :members, :] = packed.astype(BF16)
        rows = totals_ref[...]
        for place, values in ((0, first), (2, second)):
            tile = values[:8]
            for i in range(1, members // 8):
                tile = jnp.where(lane // 8 == i, values[8 * i : 8 * i + 8], tile)
            diagonal = jnp.sum(jnp.where(lane % 8 == line, tile, 0.0), axis=0, keepdims=True)
            projected = values[members : members + 1] + values[members + 1 : members + 2]
            rows = jnp.where(line == place, diagonal, rows)
            rows = jnp.where(line == place + 1, projected, rows)
        high = rows.astype(BF16).astype(F32)
        out_ref[0, pair, members:, :] = jnp.concatenate([high, rows - high], axis=0).astype(BF16)


def partial_grams(sizes, far, core, count, requests, staged):
    patches, per_owner = sizes[0], sizes[5]
    members = staged[0].shape[2]
    rows = members + EXT
    block = (1, patches // 2, rows, members)
    return pl.pallas_call(
        functools.partial(gram_kernel, sizes, far, core),
        out_shape=jax.ShapeDtypeStruct((count, *block[1:]), BF16),
        grid_spec=pltpu.PrefetchScalarGridSpec(
            num_scalar_prefetch=0,
            grid=(count,),
            in_specs=[pl.BlockSpec(memory_space=pltpu.SMEM)] + [pl.BlockSpec(memory_space=pltpu.VMEM)] * 5,
            out_specs=pl.BlockSpec(block, lambda i, *_: (i, 0, 0, 0)),
            scratch_shapes=[pltpu.VMEM((patches, members + 8, members), F32)],
        ),
        compiler_params=pltpu.CompilerParams(vmem_limit_bytes=8 * 2**20),
        cost_estimate=pl.CostEstimate(
            flops=count * per_owner * 100 * members**3, bytes_accessed=0, transcendentals=0
        ),
        name="partial_grams",
    )(requests, *staged)


def added(left, right):
    members = left.shape[-1]
    total = left.astype(F32) + right.astype(F32)
    rows = total[:, members : members + 8] + total[:, members + 8 :]
    high = rows.astype(BF16).astype(F32)
    rows = jnp.concatenate([high, rows - high], axis=1)
    return total[:, :members].astype(BF16), rows.astype(BF16)


def add_kernel(inputs, size, jobs, *refs):
    for left, left_row, right, right_row, at, out, row, place in jobs:
        out_ref = refs[inputs + out]
        members = out_ref.shape[-1]
        span, to = slice(at, at + size), slice(place, place + size)
        body, rows = added(refs[left][left_row, span], refs[right][right_row, span])
        out_ref[row, to, :members, :] = body
        out_ref[row, to, members:, :] = rows


def add_all(arrays, size, jobs, shapes, hides):
    inner = arrays[0].shape[2:]
    whole = pl.BlockSpec(memory_space=pltpu.VMEM)
    work = len(jobs) * size * inner[0] * inner[1]
    return pl.pallas_call(
        functools.partial(add_kernel, len(arrays), size, jobs),
        out_shape=[jax.ShapeDtypeStruct((*shape, *inner), BF16) for shape in shapes],
        in_specs=[whole] * len(arrays),
        out_specs=[whole] * len(shapes),
        compiler_params=pltpu.CompilerParams(vmem_limit_bytes=8 * 2**20),
        cost_estimate=pl.CostEstimate(flops=work * (10000 if hides else 4), bytes_accessed=work * 6, transcendentals=0),
        name="add_partials",
    )(*arrays)


def product(left, right):
    left_high, left_low = left
    right_high, right_low = right
    return jnp.dot(
        jnp.concatenate([left_high, left_low, left_high], axis=1),
        jnp.concatenate([right_high, right_high, right_low], axis=0),
        preferred_element_type=F32,
    )


def solve_group(parts, total_obs, first, count):
    members = parts[0].shape[-1]
    row = lax.broadcasted_iota(jnp.int32, (members, members), 0)
    column = lax.broadcasted_iota(jnp.int32, (members, members), 1)
    identity = (row == column).astype(F32)
    systems, projected = [], []
    for pair in range(count):
        total = parts[0][0, first + pair].astype(F32)
        for part in parts[1:]:
            total = total + part[0, first + pair].astype(F32)
        packed = total[:members]
        values = total[members : members + 8] + total[members + 8 :]
        flipped = packed.T
        innovation = jnp.sum(values[4:5], axis=1, keepdims=True)
        spread = jnp.sum(values[5:6], axis=1, keepdims=True)
        ridge = (members - 1) * (spread + total_obs) / innovation
        for place, full in (
            (0, jnp.where(row < column, packed, flipped)),
            (2, jnp.where(row > column, packed, flipped)),
        ):
            systems.append(jnp.where(row == column, values[place : place + 1] + ridge, full))
            projected.append(values[place + 1 : place + 2])
    scalings, roots = [], []
    for system in systems:
        squares = jnp.sum(system * system, axis=0, keepdims=True)
        scaling = jnp.sqrt(jnp.sum(squares, axis=1, keepdims=True))
        scalings.append(scaling)
        roots.append(system * (1.0 / scaling))
    factors = [1.5 * identity - 0.5 * root for root in roots]
    roots = [product(halves(f), halves(r)) for f, r in zip(factors, roots)]
    inverses = factors
    for iteration in range(1, NS_ITERS):
        split_roots = [halves(r) for r in roots]
        split_inverses = [halves(z) for z in inverses]
        factors = [
            halves(1.5 * identity - 0.5 * product(z, r))
            for z, r in zip(split_inverses, split_roots)
        ]
        if iteration < NS_ITERS - 1:
            both = [
                product(f, [jnp.concatenate([a, b], axis=1) for a, b in zip(r, z)])
                for f, r, z in zip(factors, split_roots, split_inverses)
            ]
            roots = [b[:, :members] for b in both]
            inverses = [b[:, members:] for b in both]
        else:
            inverses = [product(f, z) for f, z in zip(factors, split_inverses)]
    weights = []
    for scaling, inverse, values in zip(scalings, inverses, projected):
        inverse_sqrt = inverse * lax.rsqrt(scaling)
        inner = jnp.sum(inverse_sqrt * values, axis=1, keepdims=True)
        mean = jnp.sum(inverse_sqrt * inner, axis=0, keepdims=True)
        weights.append((jnp.sqrt(F32(members - 1)) * inverse_sqrt + mean).astype(BF16))
    return weights


def analysis_kernel(count, total_obs, group, *refs):
    parts, (pert_ref, mean_ref, out_ref, weights_ref) = refs[:count], refs[count:]
    step = pl.program_id(0)
    size, fields = pert_ref.shape[:2]
    now, before = lax.rem(step, 2), lax.rem(step + 1, 2)
    for patch in range(size):
        held = weights_ref[before, patch]
        for field in range(fields):
            change = jnp.dot(held, pert_ref[patch, field], preferred_element_type=F32)
            out_ref[patch, field] = change + mean_ref[patch, field : field + 1]
    groups = pl.num_programs(0) - 1
    first = jnp.minimum(step, groups - 1) * (group // 2)
    for patch, weights in enumerate(solve_group(parts, total_obs, first, group // 2)):
        weights_ref[now, patch] = weights


def analysis(parts, total_obs, pert, mean):
    patches, fields, members, columns = pert.shape
    group = patches // 2
    whole = pl.BlockSpec(memory_space=pltpu.VMEM)
    return pl.pallas_call(
        functools.partial(analysis_kernel, len(parts), total_obs, group),
        out_shape=jax.ShapeDtypeStruct(pert.shape, F32),
        grid=(patches // group + 1,),
        in_specs=[whole] * len(parts)
        + [
            pl.BlockSpec(
                (group, fields, members, columns), lambda i: (jnp.maximum(i - 1, 0), 0, 0, 0)
            ),
            pl.BlockSpec((group, fields, columns), lambda i: (jnp.maximum(i - 1, 0), 0, 0)),
        ],
        out_specs=pl.BlockSpec(
            (group, fields, members, columns), lambda i: (jnp.maximum(i - 1, 0), 0, 0, 0)
        ),
        scratch_shapes=[pltpu.VMEM((2, group, members, members), BF16)],
        compiler_params=pltpu.CompilerParams(vmem_limit_bytes=40 * 2**20),
        name="analysis",
    )(*parts, pert, mean)


def swap(value, axis, flip):
    size = lax.axis_size(axis)
    return lax.ppermute(value, axis, [(i, i ^ flip) for i in range(size)])


def on_device(
    state_pert, state_mean, obs_anom, innov, obs_rinv, obs_lon, obs_lat, block_list, block_count
):
    lon_devices, lat_devices = lax.axis_size("lon"), lax.axis_size("lat")
    holders = lon_devices * lat_devices
    lon_patches, lat_patches, fields, members, columns = state_pert.shape
    patches = lon_patches * lat_patches
    length = block_list.shape[2]
    held, _, block_obs = obs_anom.shape
    per_owner = patches * length // holders
    table = request_table(block_list, block_count, holders, held)
    requests = lax.all_to_all(table, ("lon", "lat"), split_axis=0, concat_axis=0, tiled=True)

    requests, observed = lax.optimization_barrier(
        (requests, (obs_anom, innov, obs_rinv, obs_lon, obs_lat))
    )
    *staged, requests = stage(*observed, requests)
    sizes = (
        patches,
        lat_patches,
        lon_patches,
        lat_devices,
        held,
        per_owner,
        lon_devices * lon_patches * PSIDE,
    )
    y_count = lon_devices // 2
    pairs = patches // 2
    cut = pairs // 2

    def grams(far, core, after):
        rows, _ = lax.optimization_barrier((staged[-1], after))
        return partial_grams(sizes, far, core, lon_devices, requests, [*staged[:-1], rows])

    along_lon = []
    while 2 ** (len(along_lon) + 1) <= y_count:
        along_lon.append(("lon", y_count >> len(along_lon)))
    routes = [[("lat", 1), *along_lon], [*along_lon[:1], ("lat", 1), *along_lon[1:]]]

    def leaves(target, axis, flip):
        y, near = target
        return near == 1 if axis == "lat" else (2 * y) & flip != 0

    parts, open_chunks, on_their_way = {}, [], [[], [], []]

    def exchange(chunks, merge, behind=(), hides=False):
        arrays, jobs, lengths, where = [], [], {}, {}

        def slot(array):
            for i, known in enumerate(arrays):
                if known is array:
                    return i
            arrays.append(array)
            return len(arrays) - 1

        def take(key):
            row = lengths.get(key, 0)
            lengths[key] = row + 1
            return row

        for far, level, parcels in chunks:
            for half, (targets, at, keep, keep_rows, got, got_rows) in enumerate(parcels):
                for target, keep_row, got_row in zip(targets, keep_rows, got_rows):
                    place = 0
                    if level == len(routes[half]):
                        key, row, place = ("total", far), 0, half * cut
                        lengths[key] = 1
                    elif leaves(target, *routes[half][level]):
                        key = ("send", *routes[half][level], 0 if merge else level)
                        row = take(key)
                    else:
                        key = ("keep", far, half)
                        row = take(key)
                    where[far, half, target] = key, row
                    jobs.append((slot(keep), keep_row, slot(got), got_row, at, key, row, place))
        keys = sorted(lengths, key=lambda k: (k[0], -k[-1] if k[0] == "send" else 0))
        jobs = [(*job[:5], keys.index(job[5]), *job[6:]) for job in jobs]
        shapes = [(lengths[k], pairs if k[0] == "total" else cut) for k in keys]
        due = on_their_way.pop(0)
        on_their_way.append([])
        arrays[0], arrived, _ = lax.optimization_barrier(
            (arrays[0], [parts[far] for far in due], list(behind))
        )
        parts.update(zip(due, arrived))
        outs = dict(zip(keys, add_all(arrays, cut, jobs, shapes, hides)))
        gots = {k: swap(v, k[1], k[2]) for k, v in outs.items() if k[0] == "send"}
        still = []
        for far, level, parcels in chunks:
            if level == len(routes[0]):
                total = outs["total", far]
                parts[far] = swap(total, "lat", 2 * far) if far else total
                if far and merge:
                    on_their_way[2].append(far)
                continue
            following = []
            for half, (targets, *_) in enumerate(parcels):
                staying = [t for t in targets if not leaves(t, *routes[half][level])]
                leaving = [t for t in targets if leaves(t, *routes[half][level])]
                keep_rows = [where[far, half, t][1] for t in staying]
                got_rows = [where[far, half, t][1] for t in leaving]
                got = gots[where[far, half, leaving[0]][0]]
                following.append((staying, 0, outs["keep", far, half], keep_rows, got, got_rows))
            still.append((far, level + 1, following))
        return still, [v for k, v in outs.items() if k[0] != "keep"]

    sent = []
    for far in reversed(range(lat_devices // 2)):
        send = grams(far, 1, sent)
        got = swap(send, "lon", 1)
        keep = grams(far, 0, [send])
        targets = [(y, near) for y in range(y_count) for near in range(2)]
        rows = range(len(targets))
        if not far:
            open_chunks, sent = exchange(open_chunks, False, behind=[keep])
            keep, _ = lax.optimization_barrier((keep, sent))
        newest = (far, 0, [(targets, at, keep, rows, got, rows) for at in (0, cut)])
        if far:
            open_chunks, sent = exchange([*open_chunks, newest], True)
        else:
            open_chunks += exchange([newest], False, hides=False)[0]
    while open_chunks:
        open_chunks = [c for chunk in open_chunks for c in exchange([chunk], False, hides=len(open_chunks) > 1 and chunk is open_chunks[0])[0]]
    updated = analysis(
        list(parts.values()),
        holders * held * block_obs,
        state_pert.reshape(patches, fields, members, columns),
        state_mean.reshape(patches, fields, columns),
    )
    return updated.reshape(lon_patches, lat_patches, fields, members, columns)


def solution(mesh):
    in_specs = (
        P("lon", "lat", None, None, None),
        P("lon", "lat", None, None),
        P(("lon", "lat"), None, None),
        P(("lon", "lat"), None),
        P(("lon", "lat"), None),
        P(("lon", "lat"), None),
        P(("lon", "lat"), None),
        P("lon", "lat", None),
        P("lon", "lat"),
    )
    out_specs = P("lon", "lat", None, None, None)
    return jax.shard_map(
        on_device, mesh=mesh, in_specs=in_specs, out_specs=out_specs, check_vma=False
    )
```
